128 devices in a mesh: tower: 2 (over core), tm: 8 (over z, y_hi), tensor: 8 (over y_lo, x).
Axes of the slice: x: 4, y: 4 (y_hi: 2, y_lo: 2; y = y_hi * 2 + y_lo), z: 4, core: 2. Of those that a mesh axis runs over, the one named last changes fastest.
Arguments:
- video_tokens: bfloat16 [24576, 3072], P(('tower', 'tm'), 'tensor')
- audio_tokens: bfloat16 [512, 3072], P(('tower', 'tm'), 'tensor')
- w_query: bfloat16 [2, 3072, 3072], P(None, None, 'tensor'), may hold values from -0.109375 to 0.109375
- w_key: bfloat16 [2, 3072, 3072], P(None, None, 'tensor'), may hold values from -0.109375 to 0.109375
- w_value: bfloat16 [2, 3072, 3072], P(None, None, 'tensor'), may hold values from -0.109375 to 0.109375
- w_out: bfloat16 [2, 3072, 3072], P(None, 'tensor'), may hold values from -2.5 to 2.5
- video_counts: int32 [16], replicated, may hold values from 1440 to 1536, as said below
- audio_counts: int32 [16], replicated, may hold values from 28 to 32, as said below
- video_windows: int32 [16, 2], replicated, may hold values from 4 to 8
- audio_windows: int32 [16, 2], replicated, may hold values from 192 to 384
Outputs:
- video_update: bfloat16 [24576, 3072], P(('tower', 'tm'), 'tensor')
- audio_update: bfloat16 [512, 3072], P(('tower', 'tm'), 'tensor')
The draws below stay inside these ranges and needn't reach their ends.
Inputs may be any that keep to these rules, and one draw needn't show every extreme that they name: `video_counts`: valid video tokens lie at the start of their time shard. `audio_counts`: valid audio tokens lie at the start of their time shard.
All inputs are finite; a program needn't handle non-finite values.
Results may differ from the reference program's by a relative error of at most 0.019.
Values may be sent and summed in bfloat16 or wider, within the bound.
No kernel may reach another device: no remote copies, remote signals or barrier semaphores. Data moves between devices by JAX's collectives and lax.ppermute only.
A program may use at most 128 MiB of HBM per device.

```python
import math
import jax
import jax.numpy as jnp
from jax import lax

D = 3072
HEADS = 24
HEAD = 128
HEADS_DEV = 3
VID_DEV = 1536
AUD_DEV = 32
VID_REACH = 384
AUD_REACH = 8
SHARDS = 16
VID_TOKENS = 24576
AUD_TOKENS = 512
N_TENSOR = 8


def scaled_rows(key, rows):
    key_base, key_rows, key_cols = jax.random.split(key, 3)
    row_scale = jnp.exp(jax.random.uniform(key_rows, (rows, 1), minval=0.0, maxval=math.log(10.0)))
    col_scale = jnp.exp(jax.random.uniform(key_cols, (1, D), minval=0.0, maxval=math.log(10.0)))
    values = jax.random.normal(key_base, (rows, D)) * col_scale * row_scale
    return values.astype(jnp.float32)


def draw_video_tokens(key, part):
    return scaled_rows(jax.random.fold_in(key, 3), VID_TOKENS).astype(jnp.bfloat16)


def draw_audio_tokens(key, part):
    return scaled_rows(jax.random.fold_in(key, 5), AUD_TOKENS).astype(jnp.bfloat16)


def ragged_counts(key, lowest, highest):
    key_main, key_first, key_second = jax.random.split(key, 3)
    values = jax.random.randint(key_main, (SHARDS,), lowest, highest + 1)
    first_pick = jax.random.randint(key_first, (), 0, SHARDS)
    second_pick = (first_pick + jax.random.randint(key_second, (), 1, SHARDS)) % SHARDS
    values = values.at[first_pick].set(highest).at[second_pick].set(lowest)
    return values.astype(jnp.int32)


def draw_video_counts(key, part):
    return ragged_counts(jax.random.fold_in(key, 11), VID_DEV - VID_DEV // 16, VID_DEV)


def draw_audio_counts(key, part):
    return ragged_counts(jax.random.fold_in(key, 13), AUD_DEV - AUD_DEV // 8, AUD_DEV)


def window_bounds(key, highest):
    key_main, key_shard, key_shard2 = jax.random.split(key, 3)
    values = jax.random.randint(key_main, (SHARDS, 2), highest // 2, highest + 1)
    shard_pick = jax.random.randint(key_shard, (), 1, SHARDS)
    values = values.at[shard_pick, 0].set(highest)
    shard_pick2 = jax.random.randint(key_shard2, (), 0, SHARDS)
    values = values.at[shard_pick2, 1].set(highest // 2)
    return values.astype(jnp.int32)


def draw_video_windows(key, part):
    return window_bounds(jax.random.fold_in(key, 23), AUD_REACH)


def draw_audio_windows(key, part):
    return window_bounds(jax.random.fold_in(key, 29), VID_REACH)


def strengthened(array, stream_key, source, target, blocks, factor):
    def block_of(dim):
        return (jnp.arange(array.shape[dim]) // (array.shape[dim] // blocks)).reshape((-1,) + (1,) * (array.ndim - 1 - dim))

    first = jax.random.permutation(stream_key, blocks)[block_of(target)]
    second = (block_of(target) + blocks // 2) % blocks
    return jnp.where((block_of(source) == first) | (block_of(source) == second), factor * array, array)


def levels(stream_key, extent, pieces, least, top_value):
    loudness, own = 1.0, jax.random.fold_in(stream_key, 6)
    for dim, parts in pieces:
        heights = jnp.exp(jax.random.uniform(jax.random.fold_in(own, dim), (parts,), jnp.float32, least / len(pieces), top_value / len(pieces)))
        loudness = loudness * jnp.repeat(heights, extent[dim] // parts).reshape([-1 if axis == dim else 1 for axis in range(len(extent))])
    return loudness


def normal_values(key, shape, scale, bound, cuts=(), held_as=jnp.bfloat16):
    level = levels(key, shape, cuts, -0.22, 0.18) if cuts else 1.0
    array = jax.random.normal(key, shape, jnp.float32) * scale * level
    return jnp.minimum(jnp.maximum(array, -bound), bound).astype(held_as)


def noise_with(stream_key, extent, deviation, most, pieces, heavy, kind=jnp.bfloat16):
    result = deviation * jax.random.normal(stream_key, extent, jnp.float32)
    if pieces:
        result = result * levels(stream_key, extent, pieces, -0.22, 0.18)
    return jnp.clip(strengthened(result, jax.random.fold_in(stream_key, 3), *heavy), -most, most).astype(kind)


def setup_inputs(seed: int = 0) -> dict:
    splits = jax.random.split(jax.random.key(seed), 11)
    video_tokens = draw_video_tokens(jax.random.fold_in(splits[10], 71), 0)
    audio_tokens = draw_audio_tokens(jax.random.fold_in(splits[10], 71), 0)
    w_query = normal_values(splits[2], (2, D, D), D ** -0.5, 0.109375, ((2, 8),))
    w_key = normal_values(splits[3], (2, D, D), D ** -0.5, 0.109375, ((2, 8),))
    w_value = normal_values(splits[4], (2, D, D), D ** -0.5, 0.109375, ((2, 8),))
    w_out = noise_with(splits[5], (2, D, D), 0.25, 2.5, ((1, 8),), (1, 2, 8, 2.0))
    video_counts = draw_video_counts(jax.random.fold_in(splits[10], 71), 0)
    audio_counts = draw_audio_counts(jax.random.fold_in(splits[10], 71), 0)
    video_windows = draw_video_windows(jax.random.fold_in(splits[10], 71), 0)
    audio_windows = draw_audio_windows(jax.random.fold_in(splits[10], 71), 0)
    return {"video_tokens": video_tokens, "audio_tokens": audio_tokens, "w_query": w_query, "w_key": w_key, "w_value": w_value, "w_out": w_out, "video_counts": video_counts, "audio_counts": audio_counts, "video_windows": video_windows, "audio_windows": audio_windows}


epsilon = 1e-06

def layer_norm(row_block):
    values = row_block.astype(jnp.float32)
    centred = values - lax.optimization_barrier(jnp.mean(values, axis=-1, keepdims=True))
    spread = lax.optimization_barrier(jnp.mean(centred * centred, axis=-1, keepdims=True))
    return (centred * lax.rsqrt(spread + epsilon)).astype(jnp.bfloat16)

def head_norm(product, head_size):
    shaped = product.reshape(product.shape[0], -1, head_size)
    mean_square = lax.optimization_barrier(jnp.mean(shaped * shaped, axis=-1, keepdims=True))
    return (shaped * lax.rsqrt(mean_square + epsilon)).reshape(product.shape).astype(jnp.bfloat16)

def attend_shards(queries, key_slots, value_slots, key_counts, window_table, query_dev, key_dev, key_reach):
    span_rows = key_dev + 2 * key_reach
    slot_index = jnp.arange(SHARDS * key_dev, dtype=jnp.int32)
    valid_keys = slot_index % key_dev < key_counts[slot_index // key_dev]
    key_padded = jnp.pad(key_slots, ((key_reach, key_reach), (0, 0)))
    value_padded = jnp.pad(value_slots, ((key_reach, key_reach), (0, 0)))
    valid_padded = jnp.pad(valid_keys, (key_reach, key_reach))
    score_scale = 1.0 / math.sqrt(HEAD)

    def one_shard(shard_pos):
        first_key = shard_pos * key_dev
        query_rows = lax.dynamic_slice_in_dim(queries, shard_pos * query_dev, query_dev, 0)
        key_rows = lax.dynamic_slice_in_dim(key_padded, first_key, span_rows, 0)
        value_rows = lax.dynamic_slice_in_dim(value_padded, first_key, span_rows, 0)
        valid_rows = lax.dynamic_slice_in_dim(valid_padded, first_key, span_rows, 0)
        position = first_key - key_reach + jnp.arange(span_rows, dtype=jnp.int32)
        lower = first_key - window_table[shard_pos, 0]
        upper = first_key + key_dev + window_table[shard_pos, 1]
        used_keys = valid_rows & (position >= lower) & (position < upper)
        query_float = query_rows.astype(jnp.float32).reshape(query_dev, HEADS, HEAD)
        key_float = key_rows.astype(jnp.float32).reshape(span_rows, HEADS, HEAD)
        value_float = value_rows.astype(jnp.float32).reshape(span_rows, HEADS, HEAD)
        scores = jnp.einsum('qhd,khd->hqk', query_float, key_float) * score_scale
        weights = jnp.where(used_keys[None, None, :], jnp.exp(scores), 0.0)
        denominator = lax.optimization_barrier(jnp.sum(weights, axis=-1, keepdims=True))
        probabilities = (weights / denominator).astype(jnp.bfloat16)
        mixed_heads = jnp.einsum('hqk,khd->qhd', probabilities.astype(jnp.float32), value_float)
        return mixed_heads.astype(jnp.bfloat16).reshape(query_dev, D)
    return lax.map(one_shard, jnp.arange(SHARDS, dtype=jnp.int32)).reshape(SHARDS * query_dev, D)

def project_out(attended, weight, own_counts, query_dev):
    group_width = HEADS_DEV * HEAD
    summed = jnp.zeros((attended.shape[0], D), jnp.float32)
    for group_pos in range(N_TENSOR):
        low_col = group_pos * group_width
        product = jnp.dot(attended[:, low_col:low_col + group_width], weight[low_col:low_col + group_width, :], preferred_element_type=jnp.float32)
        rounded = lax.optimization_barrier(product.astype(jnp.bfloat16))
        summed = summed + rounded.astype(jnp.float32)
    slot_index = jnp.arange(attended.shape[0], dtype=jnp.int32)
    valid_query = slot_index % query_dev < own_counts[slot_index // query_dev]
    return jnp.where(valid_query[:, None], summed, 0.0).astype(jnp.bfloat16)

def reference(video_tokens, audio_tokens, w_query, w_key, w_value, w_out, video_counts, audio_counts, video_windows, audio_windows):
    video_normed = layer_norm(video_tokens)
    audio_normed = layer_norm(audio_tokens)
    video_queries = head_norm(jnp.dot(video_normed, w_query[0], preferred_element_type=jnp.float32), HEAD)
    audio_queries = head_norm(jnp.dot(audio_normed, w_query[1], preferred_element_type=jnp.float32), HEAD)
    audio_keys = head_norm(jnp.dot(audio_normed, w_key[0], preferred_element_type=jnp.float32), HEAD)
    audio_values = jnp.dot(audio_normed, w_value[0], preferred_element_type=jnp.float32).astype(jnp.bfloat16)
    video_keys = head_norm(jnp.dot(video_normed, w_key[1], preferred_element_type=jnp.float32), HEAD)
    video_values = jnp.dot(video_normed, w_value[1], preferred_element_type=jnp.float32).astype(jnp.bfloat16)
    video_attended = attend_shards(video_queries, audio_keys, audio_values, audio_counts, video_windows, VID_DEV, AUD_DEV, AUD_REACH)
    audio_attended = attend_shards(audio_queries, video_keys, video_values, video_counts, audio_windows, AUD_DEV, VID_DEV, VID_REACH)
    video_update = project_out(video_attended, w_out[0], video_counts, VID_DEV)
    audio_update = project_out(audio_attended, w_out[1], audio_counts, AUD_DEV)
    return (video_update, audio_update)
```

```python
import math

import jax
import jax.numpy as jnp
from jax import lax
from jax.experimental import pallas as pl
from jax.experimental.pallas import tpu as pltpu
from jax.sharding import PartitionSpec as P

D = 3072
HEAD = 128
HEADS_DEV = 3
GROUP = HEADS_DEV * HEAD
N_TENSOR = 8
VID = 1536
AUD = 32
REACH = 8
SPAN = AUD + 2 * REACH
KEYS = HEADS_DEV * SPAN
SHARDS = 16
TILE = 256
TILES = VID // TILE
HALF = VID // 2
THIRD = VID // 3
EPS = 1e-6
SCALE = math.log2(math.e) / math.sqrt(HEAD)
F32 = jnp.float32
BF16 = jnp.bfloat16


def params(mib, semantics=1):
    return pltpu.CompilerParams(
        dimension_semantics=("arbitrary",) * semantics, vmem_limit_bytes=mib * 2**20
    )


def dot(a, b):
    return jnp.dot(a, b, preferred_element_type=F32)


def dot_nt(a, b):
    return lax.dot_general(a, b, (((1,), (1,)), ((), ())), preferred_element_type=F32)


def dot_tn(a, b):
    return lax.dot_general(a, b, (((0,), (0,)), ((), ())), preferred_element_type=F32)


def full(shape):
    return pl.BlockSpec(shape, lambda *_: (0,) * len(shape))


def moved(index, dy, dx):
    return (index // 4 + dy) % 2 * 4 + (index % 4 + dx) % 4


def send(array, dy, dx):
    pairs = [(i, moved(i, dy, dx)) for i in range(N_TENSOR)]
    return lax.ppermute(array, "tensor", pairs)


def right(array):
    return send(array, 0, 1)


def left(array):
    return send(array, 0, 3)


def across(array):
    return send(array, 1, 0)


def cat(*arrays):
    return jnp.concatenate(arrays, axis=0)


def audio_in_kernel(a_ref, wq_ref, wk_ref, wv_ref, qkv_ref, prev_ref, next_ref, stat, acc):
    step = pl.program_id(0)

    @pl.when(step == 0)
    def _():
        values = a_ref[...].astype(F32)
        mean = jnp.sum(jnp.sum(values, axis=0), axis=-1, keepdims=True) / D
        centred = values - mean[None]
        var = jnp.sum(jnp.sum(centred * centred, axis=0), axis=-1, keepdims=True) / D
        stat[0] = jnp.broadcast_to(mean, (AUD, HEAD))
        stat[1] = jnp.broadcast_to(lax.rsqrt(var + EPS), (AUD, HEAD))
        acc[...] = jnp.zeros_like(acc)

    block = a_ref[step].astype(F32)
    normed = ((block - stat[0][:, :1]) * stat[1][:, :1]).astype(BF16)
    weights = jnp.concatenate([wq_ref[0], wk_ref[0], wv_ref[0]], axis=1)
    acc[...] += dot(normed, weights)

    @pl.when(step == N_TENSOR - 1)
    def _():
        total = acc[...]
        heads = []
        for h in range(2 * HEADS_DEV):
            part = total[:, h * HEAD : (h + 1) * HEAD]
            mean_square = jnp.mean(part * part, axis=-1, keepdims=True)
            heads.append(part * lax.rsqrt(mean_square + EPS))
        q = jnp.concatenate(heads[:HEADS_DEV], axis=1)
        k = jnp.concatenate(heads[HEADS_DEV:], axis=1)
        v = total[:, 2 * GROUP :]
        qkv_ref[...] = cat(q, k, v).astype(BF16)
        prev_ref[...] = cat(q, k[:REACH], v[:REACH]).astype(BF16)
        next_ref[...] = cat(q, k[AUD - REACH :], v[AUD - REACH :]).astype(BF16)


def audio_in(gathered, w_query, w_key, w_value):
    def weight(tower):
        return pl.BlockSpec((1, GROUP, GROUP), lambda j: (tower, j, 0))

    packed = AUD + 2 * REACH
    return pl.pallas_call(
        audio_in_kernel,
        grid=(N_TENSOR,),
        in_specs=[full((N_TENSOR, AUD, GROUP)), weight(1), weight(0), weight(0)],
        out_specs=[full((3 * AUD, GROUP)), full((packed, GROUP)), full((packed, GROUP))],
        out_shape=[
            jax.ShapeDtypeStruct((3 * AUD, GROUP), BF16),
            jax.ShapeDtypeStruct((packed, GROUP), BF16),
            jax.ShapeDtypeStruct((packed, GROUP), BF16),
        ],
        scratch_shapes=[pltpu.VMEM((2, AUD, HEAD), F32), pltpu.VMEM((AUD, 3 * GROUP), F32)],
        compiler_params=params(32),
        cost_estimate=pl.CostEstimate(
            flops=2 * AUD * D * 3 * GROUP, bytes_accessed=3 * D * GROUP * 2, transcendentals=0
        ),
        name="audio_in",
    )(gathered, w_query, w_key, w_value)


def value_out_kernel(dest_ref, qkv_ref, prev_ref, next_ref, w_ref, out_ref):
    before = prev_ref[...].astype(F32)[AUD + REACH :]
    own = qkv_ref[...].astype(F32)[2 * AUD :]
    after = next_ref[...].astype(F32)[AUD + REACH :]
    values = cat(before, own, after).astype(BF16)
    for h in range(HEADS_DEV):
        cols = slice(h * HEAD, (h + 1) * HEAD)
        out_ref[0, h * SPAN : (h + 1) * SPAN, :] = dot(values[:, cols], w_ref[0, cols, :]).astype(
            BF16
        )


def value_out(dest, qkv, from_prev, from_next, w_out):
    packed = AUD + 2 * REACH
    return pl.pallas_call(
        value_out_kernel,
        grid_spec=pltpu.PrefetchScalarGridSpec(
            num_scalar_prefetch=1,
            grid=(N_TENSOR,),
            in_specs=[
                full((3 * AUD, GROUP)),
                full((packed, GROUP)),
                full((packed, GROUP)),
                pl.BlockSpec((1, GROUP, GROUP), lambda j, dest: (0, 0, dest[j])),
            ],
            out_specs=pl.BlockSpec((1, KEYS, GROUP), lambda j, dest: (j, 0, 0)),
        ),
        out_shape=jax.ShapeDtypeStruct((N_TENSOR, KEYS, GROUP), BF16),
        compiler_params=params(32),
        cost_estimate=pl.CostEstimate(
            flops=2 * KEYS * HEAD * D, bytes_accessed=GROUP * D * 2 + KEYS * D * 2, transcendentals=0
        ),
        name="value_out",
    )(dest, qkv, from_prev, from_next, w_out)


def row_stats(block):
    values = block.astype(F32)
    mean = jnp.mean(values, axis=-1, keepdims=True)
    centred = values - mean
    return mean, jnp.sum(centred * centred, axis=-1, keepdims=True)


def fill_weights(w_refs, wcat, sums):
    for part in range(3):
        for j in range(4):
            wcat[j * GROUP : (j + 1) * GROUP, part * GROUP : (part + 1) * GROUP] = w_refs[
                part * 4 + j
            ][0]
    sums[...] = dot(jnp.ones((8, 4 * GROUP), BF16), wcat[...])


def first_kernel(order_ref, *refs):
    x_refs, w_refs = refs[:4], refs[4:16]
    acc_ref, stat_ref, sums_ref, wcat = refs[16:]

    @pl.when(pl.program_id(0) == 0)
    def _():
        fill_weights(w_refs, wcat, sums_ref)

    block = jnp.concatenate([ref[...] for ref in x_refs], axis=1)
    acc_ref[...] = dot(block, wcat[...])
    mean, square = row_stats(block)
    lane = lax.broadcasted_iota(jnp.int32, (TILE, HEAD), 1)
    stat_ref[...] = jnp.where(lane == 0, mean, square)


def weight_specs(first):
    specs = []
    for tower in (0, 1, 1):
        for j in range(first, first + 4):
            specs.append(
                pl.BlockSpec(
                    (1, GROUP, GROUP), lambda i, order, *_, t=tower, j=j: (t, order[j], 0)
                )
            )
    return specs


def weight_args(w_query, w_key, w_value):
    return [w_query] * 4 + [w_key] * 4 + [w_value] * 4


def first_half(order, blocks, w_query, w_key, w_value):
    rows = pl.BlockSpec((TILE, GROUP), lambda i, order: (i, 0))
    return pl.pallas_call(
        first_kernel,
        grid_spec=pltpu.PrefetchScalarGridSpec(
            num_scalar_prefetch=1,
            grid=(TILES,),
            in_specs=[rows] * 4 + weight_specs(0),
            out_specs=[
                pl.BlockSpec((TILE, 3 * GROUP), lambda i, order: (i, 0)),
                pl.BlockSpec((TILE, HEAD), lambda i, order: (i, 0)),
                full((8, 3 * GROUP)),
            ],
            scratch_shapes=[pltpu.VMEM((4 * GROUP, 3 * GROUP), BF16)],
        ),
        out_shape=[
            jax.ShapeDtypeStruct((VID, 3 * GROUP), F32),
            jax.ShapeDtypeStruct((VID, HEAD), F32),
            jax.ShapeDtypeStruct((8, 3 * GROUP), F32),
        ],
        compiler_params=params(40),
        cost_estimate=pl.CostEstimate(
            flops=2 * VID * 4 * GROUP * 3 * GROUP,
            bytes_accessed=4 * VID * GROUP * 2 + VID * 3 * GROUP * 4 + 12 * GROUP * GROUP * 2,
            transcendentals=0,
        ),
        name="first_half",
    )(order, *blocks, *weight_args(w_query, w_key, w_value))


def second_kernel(
    order_ref, vc_ref, ac_ref, vw_ref, aw_ref, *refs
):
    x_refs, w_refs = refs[:10], refs[10:22]
    acc_ref, stat_ref, sums1_ref, qkv_ref, prev_ref, next_ref = refs[22:28]
    pt_ref, part_p, part_o, part_n, wcat, sums, xcat, keys, queries = refs[28:]
    i = pl.program_id(0)
    shard = order_ref[N_TENSOR]

    @pl.when(i == 0)
    def _():
        fill_weights(w_refs, wcat, sums)
        before = prev_ref[...].astype(F32)
        own = qkv_ref[...].astype(F32)
        after = next_ref[...].astype(F32)
        keys[...] = cat(
            before[AUD : AUD + REACH], own[AUD : 2 * AUD], after[AUD : AUD + REACH]
        ).astype(BF16)
        queries[...] = cat(before[:AUD], own[:AUD], after[:AUD]).astype(BF16)
        for ref in (part_p, part_o, part_n):
            ref[...] = jnp.zeros_like(ref)

    places = (
        (0, 0, 0, 3), (0, 1, 3, 6),
        (1, 2, 0, 2), (1, 3, 2, 4), (1, 4, 4, 6),
        (2, 5, 0, 2), (2, 6, 2, 4), (2, 7, 4, 6),
        (3, 8, 0, 3), (3, 9, 3, 6),
    )
    for col, source, low, high in places:

        @pl.when((i >= low) & (i < high))
        def _(col=col, source=source):
            xcat[:, col * GROUP : (col + 1) * GROUP] = x_refs[source][...]

    block = xcat[...]
    mean2, square2 = row_stats(block)
    mean1, square1 = stat_ref[:, :1], stat_ref[:, 1:2]
    gap = mean1 - mean2
    mean = 0.5 * (mean1 + mean2)
    var = (square1 + square2 + gap * gap * (D / 4)) / D
    total = acc_ref[...] + dot(block, wcat[...])
    total = total - mean * (sums1_ref[:1, :] + sums[:1, :])
    floor = EPS * (var + EPS)

    prev_at, next_at = jnp.maximum(shard - 1, 0), jnp.minimum(shard + 1, SHARDS - 1)
    has_prev, has_next = shard > 0, shard < SHARDS - 1
    slot = lax.broadcasted_iota(jnp.int32, (SPAN, 1), 0)
    end_prev = jnp.where(has_prev, ac_ref[prev_at] - (AUD - REACH), 0)
    end_own = REACH + ac_ref[shard]
    end_next = jnp.where(
        has_next, REACH + AUD + jnp.minimum(ac_ref[next_at], vw_ref[shard, 1]), 0
    )
    used = (slot >= REACH - vw_ref[shard, 0]) & (slot < jnp.minimum(end_prev, REACH))
    used |= (slot >= REACH) & (slot < end_own)
    used |= (slot >= REACH + AUD) & (slot < end_next)

    count = vc_ref[shard]
    row = lax.broadcasted_iota(jnp.int32, (3 * AUD, 1), 0)
    high_prev = jnp.where(has_prev, jnp.minimum(count, aw_ref[prev_at, 1]), 0)
    high_next = jnp.where(has_next, count, 0)
    low = jnp.where(row < 2 * AUD, 0, VID - aw_ref[next_at, 0])
    high = jnp.where(row < AUD, high_prev, jnp.where(row < 2 * AUD, count, high_next))
    place = i * TILE + lax.broadcasted_iota(jnp.int32, (3 * AUD, TILE), 1)
    seen = (place >= low) & (place < high)
    spread = lax.rsqrt(var + EPS)

    for h in range(HEADS_DEV):
        cols = slice(h * HEAD, (h + 1) * HEAD)

        def normed(first):
            part = total[:, first + h * HEAD : first + (h + 1) * HEAD]
            mean_square = jnp.mean(part * part, axis=-1, keepdims=True)
            return (part * lax.rsqrt(mean_square + floor)).astype(BF16)

        scores = dot_nt(keys[:, cols], normed(0))
        weights = jnp.where(used, jnp.exp2(scores * SCALE), 0.0)
        sums_h = jnp.sum(weights, axis=0, keepdims=True)
        pt_ref[0, h * SPAN : (h + 1) * SPAN, :] = (weights * (1.0 / sums_h)).astype(BF16)

        value = (total[:, 2 * GROUP + h * HEAD : 2 * GROUP + (h + 1) * HEAD] * spread).astype(BF16)
        scores = dot_nt(queries[:, cols], normed(GROUP))
        weights = jnp.where(seen, jnp.exp2(scores * SCALE), 0.0)
        bottom = jnp.broadcast_to(jnp.sum(weights, axis=1, keepdims=True), (3 * AUD, HEAD))
        top = dot(weights.astype(BF16), value)
        for g, ref in enumerate((part_p, part_o, part_n)):
            ref[0, :, cols] += top[g * AUD : (g + 1) * AUD]
            ref[1, :, cols] += bottom[g * AUD : (g + 1) * AUD]


def second_half(order, tables, pieces, w_query, w_key, w_value, acc, stat, sums, qkv, prev, after):
    def rows(low, count, base=0):
        return pl.BlockSpec(
            (TILE, GROUP), lambda i, *_: (base + jnp.clip(i - low, 0, count - 1), 0)
        )

    packed = AUD + 2 * REACH
    part = jax.ShapeDtypeStruct((2, AUD, GROUP), F32)
    piece_specs = [
        rows(0, 3), rows(3, 3),
        rows(0, 2), rows(2, 2), rows(4, 2),
        rows(0, 2, 2), rows(2, 2, 2), rows(4, 2),
        rows(0, 3), rows(3, 3),
    ]
    return pl.pallas_call(
        second_kernel,
        grid_spec=pltpu.PrefetchScalarGridSpec(
            num_scalar_prefetch=5,
            grid=(TILES,),
            in_specs=piece_specs
            + weight_specs(4)
            + [
                pl.BlockSpec((TILE, 3 * GROUP), lambda i, *_: (i, 0)),
                pl.BlockSpec((TILE, HEAD), lambda i, *_: (i, 0)),
                full((8, 3 * GROUP)),
                full((3 * AUD, GROUP)),
                full((packed, GROUP)),
                full((packed, GROUP)),
            ],
            out_specs=[
                pl.BlockSpec((1, KEYS, TILE), lambda i, *_: (i // 3, 0, i % 3)),
                full((2, AUD, GROUP)),
                full((2, AUD, GROUP)),
                full((2, AUD, GROUP)),
            ],
            scratch_shapes=[
                pltpu.VMEM((4 * GROUP, 3 * GROUP), BF16),
                pltpu.VMEM((8, 3 * GROUP), F32),
                pltpu.VMEM((TILE, 4 * GROUP), BF16),
                pltpu.VMEM((SPAN, GROUP), BF16),
                pltpu.VMEM((3 * AUD, GROUP), BF16),
            ],
        ),
        out_shape=[jax.ShapeDtypeStruct((2, KEYS, HALF), BF16), part, part, part],
        compiler_params=params(44),
        cost_estimate=pl.CostEstimate(
            flops=2 * VID * 4 * GROUP * 3 * GROUP,
            bytes_accessed=4 * VID * GROUP * 2 + VID * 3 * GROUP * 4 + 12 * GROUP * GROUP * 2,
            transcendentals=VID * HEADS_DEV * (SPAN + 3 * AUD),
        ),
        name="second_half",
    )(
        order, *tables, *pieces, *weight_args(w_query, w_key, w_value),
        acc, stat, sums, qkv, prev, after,
    )


def audio_out_kernel(own_ref, prev_ref, next_ref, w_ref, out_ref, attended):
    @pl.when(pl.program_id(0) == 0)
    def _():
        total = own_ref[...] + prev_ref[...] + next_ref[...]
        attended[...] = (total[0] / total[1]).astype(BF16)

    out_ref[0] = dot(attended[...], w_ref[0]).astype(BF16)


def audio_out(own, from_prev, from_next, w_out):
    return pl.pallas_call(
        audio_out_kernel,
        grid=(N_TENSOR,),
        in_specs=[full((2, AUD, GROUP))] * 3
        + [pl.BlockSpec((1, GROUP, GROUP), lambda j: (1, 0, j))],
        out_specs=pl.BlockSpec((1, AUD, GROUP), lambda j: (j, 0, 0)),
        out_shape=jax.ShapeDtypeStruct((N_TENSOR, AUD, GROUP), BF16),
        scratch_shapes=[pltpu.VMEM((AUD, GROUP), BF16)],
        compiler_params=params(32),
        cost_estimate=pl.CostEstimate(
            flops=2 * AUD * GROUP * D, bytes_accessed=GROUP * D * 2, transcendentals=0
        ),
        name="audio_out",
    )(own, from_prev, from_next, w_out)


def video_out_kernel(meta_ref, vc_ref, *refs):
    p_refs, a_refs, v_refs = refs[:6], refs[6:8], refs[8:16]
    out_ref, projected, probs = refs[16:]
    i = pl.program_id(0)

    @pl.when(i == 0)
    def _():
        for j, ref in enumerate(v_refs):
            projected[j * KEYS : (j + 1) * KEYS, :] = ref[0] if j == 0 else ref[...]

    for j, ref in enumerate(p_refs):
        probs[j * KEYS : (j + 1) * KEYS, :] = ref[0]

    for half in range(2):

        @pl.when(i // 3 == half)
        def _(half=half):
            for j in range(2):
                probs[(6 + j) * KEYS : (7 + j) * KEYS, :] = a_refs[half][j]

    result = dot_tn(probs[...], projected[...])
    row = i * TILE + lax.broadcasted_iota(jnp.int32, (TILE, 1), 0)
    valid = row < vc_ref[meta_ref[N_TENSOR]]
    out_ref[...] = jnp.where(valid, result, 0.0).astype(BF16)


def video_out(meta, video_counts, probs, fars, own_values, values):
    tile = pl.BlockSpec((1, KEYS, TILE), lambda i, *_: (i // 3, 0, i % 3))
    low = pl.BlockSpec((2, KEYS, TILE), lambda i, *_: (0, 0, jnp.minimum(i, 2)))
    high = pl.BlockSpec((2, KEYS, TILE), lambda i, *_: (0, 0, jnp.maximum(i - 3, 0)))
    return pl.pallas_call(
        video_out_kernel,
        grid_spec=pltpu.PrefetchScalarGridSpec(
            num_scalar_prefetch=2,
            grid=(TILES,),
            in_specs=[tile] * 6
            + [low, high]
            + [full((1, KEYS, GROUP))]
            + [full((KEYS, GROUP))] * 7,
            out_specs=pl.BlockSpec((TILE, GROUP), lambda i, *_: (i, 0)),
            scratch_shapes=[
                pltpu.VMEM((N_TENSOR * KEYS, GROUP), BF16),
                pltpu.VMEM((N_TENSOR * KEYS, TILE), BF16),
            ],
        ),
        out_shape=jax.ShapeDtypeStruct((VID, GROUP), BF16),
        compiler_params=params(40),
        cost_estimate=pl.CostEstimate(
            flops=2 * VID * N_TENSOR * KEYS * GROUP,
            bytes_accessed=VID * N_TENSOR * KEYS * 2 + N_TENSOR * KEYS * GROUP * 2,
            transcendentals=0,
        ),
        name="video_out",
    )(meta, video_counts, *probs, *fars, own_values, *values)


def shards(
    video_tokens,
    audio_tokens,
    w_query,
    w_key,
    w_value,
    w_out,
    video_counts,
    audio_counts,
    video_windows,
    audio_windows,
):
    me = lax.axis_index("tensor")
    shard = lax.axis_index(("tower", "tm"))
    up = [(i, i + 1) for i in range(SHARDS - 1)]
    down = [(i + 1, i) for i in range(SHARDS - 1)]

    def to_next(array):
        return lax.ppermute(array, ("tower", "tm"), up)

    def to_prev(array):
        return lax.ppermute(array, ("tower", "tm"), down)

    offsets = ((0, 0), (0, 3), (0, 1), (1, 0), (0, 2), (1, 3), (1, 1), (1, 2))
    order = jnp.stack([moved(me, dy, dx) for dy, dx in offsets] + [shard]).astype(jnp.int32)
    dest = jnp.stack([moved(me, dy, -dx) for dy, dx in offsets]).astype(jnp.int32)

    own = video_tokens
    xl, xr, xy = right(own), left(own), across(own)
    audio_blocks = lax.all_to_all(
        jnp.broadcast_to(audio_tokens[None], (N_TENSOR, AUD, GROUP)), "tensor", 0, 0
    )
    qkv, for_prev, for_next = audio_in(audio_blocks, w_query, w_key, w_value)
    from_next, from_prev = to_prev(for_prev), to_next(for_next)

    q_top, q_bot = right(xl[:HALF]), left(xr[HALF:])
    yl_a, yr_c = right(xy[:THIRD]), left(xy[2 * THIRD :])
    middle = across(cat(xl[THIRD : 2 * THIRD], xr[THIRD : 2 * THIRD]))
    edge = across(cat(xl[2 * THIRD :], xr[:THIRD]))
    yq_top = right(cat(yl_a, middle[: HALF - THIRD]))
    yq_bot = left(cat(middle[THIRD + HALF - THIRD :], yr_c))

    acc, stat, sums = first_half(order, (own, xl, xr, xy), w_query, w_key, w_value)
    projected = value_out(dest, qkv, from_prev, from_next, w_out)
    values = [send(projected[j], dy, -dx) for j, (dy, dx) in enumerate(offsets) if j]

    pieces = (q_top, q_bot, yl_a, middle, edge, edge, middle, yr_c, yq_top, yq_bot)
    probs, part_prev, part_own, part_next = second_half(
        order,
        (video_counts, audio_counts, video_windows, audio_windows),
        pieces,
        w_query,
        w_key,
        w_value,
        acc,
        stat,
        sums,
        qkv,
        from_prev,
        from_next,
    )

    pl_, pr_, py_ = right(probs), left(probs), across(probs)
    pyl, pyr = right(py_), left(py_)
    far_low = right(jnp.stack([pl_[0], pyl[0]]))
    far_high = left(jnp.stack([pr_[1], pyr[1]]))

    audio_from_next, audio_from_prev = to_prev(part_prev), to_next(part_next)
    audio_parts = audio_out(part_own, audio_from_prev, audio_from_next, w_out)
    audio_sums = jnp.sum(
        lax.all_to_all(audio_parts, "tensor", 0, 0).astype(F32), axis=0
    )
    audio_limit = lax.dynamic_index_in_dim(audio_counts, shard, 0, keepdims=False)
    audio_valid = jnp.arange(AUD, dtype=jnp.int32) < audio_limit
    audio_update = jnp.where(audio_valid[:, None], audio_sums, 0.0).astype(BF16)

    arranged = [values[k - 1] for k in (1, 2, 3, 5, 6, 4, 7)]
    video_update = video_out(
        order,
        video_counts,
        (probs, pl_, pr_, py_, pyl, pyr),
        (far_low, far_high),
        projected[:1],
        arranged,
    )
    return (video_update, audio_update)


def solution(mesh):
    in_specs = (
        P(("tower", "tm"), "tensor"),
        P(("tower", "tm"), "tensor"),
        P(None, None, "tensor"),
        P(None, None, "tensor"),
        P(None, None, "tensor"),
        P(None, "tensor", None),
        P(),
        P(),
        P(),
        P(),
    )
    out_specs = (P(("tower", "tm"), "tensor"), P(("tower", "tm"), "tensor"))
    return jax.shard_map(shards, mesh=mesh, in_specs=in_specs, out_specs=out_specs, check_vma=False)
```

```python
import functools
import math

import jax
import jax.numpy as jnp
import numpy as np
from jax import lax
from jax.experimental import pallas as pl
from jax.experimental.pallas import tpu as pltpu
from jax.sharding import PartitionSpec as P

D = 3072
HEAD = 128
HEADS_DEV = 3
GROUP = HEADS_DEV * HEAD
N_TENSOR = 8
VID = 1536
AUD = 32
REACH = 8
SPAN = AUD + 2 * REACH
KEYS = HEADS_DEV * SPAN
PACKED = AUD + 2 * REACH
SHARDS = 16
TILE = 256
TILES = VID // TILE
THIRD = VID // 3
AT_SHARD = 8
AT_VIDEO = 9
AT_AUDIO = 25
AT_VWIN = 41
AT_AWIN = 73
EPS = 1e-6
SCALE = math.log2(math.e) / math.sqrt(HEAD)
F32 = jnp.float32
BF16 = jnp.bfloat16


def cost(microseconds):
    return pl.CostEstimate(
        flops=int(microseconds * 1e9), bytes_accessed=0, transcendentals=0
    )


def dot(a, b):
    return jnp.dot(a, b, preferred_element_type=F32)


def dot_nt(a, b):
    return lax.dot_general(a, b, (((1,), (1,)), ((), ())), preferred_element_type=F32)


def dot_tn(a, b):
    return lax.dot_general(a, b, (((0,), (0,)), ((), ())), preferred_element_type=F32)


ANY = pl.BlockSpec(memory_space=pl.ANY)


def after(kernel, scalars, inputs, extra):
    def run(*refs):
        kernel(*refs[: scalars + inputs], *refs[scalars + inputs + extra :])

    return run


def gate(arrays, *extra):
    count = len(arrays)
    return pl.pallas_call(
        lambda *refs: None,
        in_specs=[ANY] * (count + len(extra)),
        out_specs=[ANY] * count,
        out_shape=[jax.ShapeDtypeStruct(a.shape, a.dtype) for a in arrays],
        input_output_aliases={i: i for i in range(count)},
        compiler_params=pltpu.CompilerParams(vmem_limit_bytes=2**20),
        cost_estimate=cost(0),
        name="gate",
    )(*arrays, *extra)


def moved(index, dy, dx):
    return (index // 4 + dy) % 2 * 4 + (index % 4 + dx) % 4


def send(array, dy, dx):
    pairs = [(i, moved(i, dy, dx)) for i in range(N_TENSOR)]
    return lax.ppermute(array, "tensor", pairs)


def right(array):
    return send(array, 0, 1)


def left(array):
    return send(array, 0, 3)


def across(array):
    return send(array, 1, 0)


def cat(*arrays):
    return jnp.concatenate(arrays, axis=0)


VMEM = pl.BlockSpec(memory_space=pltpu.VMEM)
SMEM = pl.BlockSpec(memory_space=pltpu.SMEM)


def rows_of(t):
    return pl.ds(pl.multiple_of(t * TILE, TILE), TILE)


def call(kernel, name, micros, inputs, extra, outputs, scratch):
    return pl.pallas_call(
        after(kernel, 0, len(inputs), len(extra)),
        in_specs=[spec for spec, _ in inputs] + [ANY] * len(extra),
        out_specs=[spec for spec, _ in outputs],
        out_shape=[shape for _, shape in outputs],
        scratch_shapes=scratch,
        compiler_params=pltpu.CompilerParams(vmem_limit_bytes=60 * 2**20),
        cost_estimate=cost(micros),
        name=name,
    )(*[array for _, array in inputs], *extra)


def sds(shape, dtype):
    return jax.ShapeDtypeStruct(shape, dtype)


def audio_in_kernel(a_ref, wq, wk, wv, qkv_ref, prev_ref, next_ref, wcat, normed, sems):
    def weight(part, j):
        ref, tower = ((wq, 1), (wk, 0), (wv, 0))[part]
        rows = pl.ds(j * GROUP, GROUP)
        cols = pl.ds(part * GROUP, GROUP)
        return pltpu.make_async_copy(
            ref.at[tower, rows, :], wcat.at[rows, cols], sems.at[3 * j + part]
        )

    for j in range(N_TENSOR):
        for part in range(3):
            weight(part, j).start()

    values = a_ref[...].astype(F32)
    mean = jnp.sum(jnp.sum(values, axis=0), axis=-1, keepdims=True) / D
    centred = values - mean[None]
    var = jnp.sum(jnp.sum(centred * centred, axis=0), axis=-1, keepdims=True) / D
    normed[...] = (centred * lax.rsqrt(var + EPS)[None]).astype(BF16)

    total = jnp.zeros((AUD, 3 * GROUP), F32)
    for j in range(N_TENSOR):
        for part in range(3):
            weight(part, j).wait()
        total = total + dot(normed[j], wcat[j * GROUP : (j + 1) * GROUP, :])

    heads = []
    for h in range(2 * HEADS_DEV):
        part = total[:, h * HEAD : (h + 1) * HEAD]
        mean_square = jnp.mean(part * part, axis=-1, keepdims=True)
        heads.append(part * lax.rsqrt(mean_square + EPS))
    q = jnp.concatenate(heads[:HEADS_DEV], axis=1)
    k = jnp.concatenate(heads[HEADS_DEV:], axis=1)
    v = total[:, 2 * GROUP :]
    qkv_ref[...] = cat(q, k, v).astype(BF16)
    prev_ref[...] = cat(q, k[:REACH], v[:REACH]).astype(BF16)
    next_ref[...] = cat(q, k[AUD - REACH :], v[AUD - REACH :]).astype(BF16)


def audio_in(gathered, w_query, w_key, w_value, *extra):
    return call(
        audio_in_kernel,
        "audio_in",
        2,
        [(VMEM, gathered), (ANY, w_query), (ANY, w_key), (ANY, w_value)],
        extra,
        [
            (VMEM, sds((3 * AUD, GROUP), BF16)),
            (VMEM, sds((PACKED, GROUP), BF16)),
            (VMEM, sds((PACKED, GROUP), BF16)),
        ],
        [
            pltpu.VMEM((D, 3 * GROUP), BF16),
            pltpu.VMEM((N_TENSOR, AUD, GROUP), BF16),
            pltpu.SemaphoreType.DMA((3 * N_TENSOR,)),
        ],
    )


def head_rows(w_ref, tower, wbuf, sems):
    return [
        pltpu.make_async_copy(
            w_ref.at[tower, h * HEAD : (h + 1) * HEAD, :],
            wbuf.at[h * HEAD : (h + 1) * HEAD, :],
            sems.at[h],
        )
        for h in range(HEADS_DEV)
    ]


def value_out_kernel(qkv_ref, prev_ref, next_ref, w_ref, out_ref, wbuf, sems):
    copies = head_rows(w_ref, 0, wbuf, sems)
    for copy in copies:
        copy.start()
    before = prev_ref[...].astype(F32)[AUD + REACH :]
    own = qkv_ref[...].astype(F32)[2 * AUD :]
    behind = next_ref[...].astype(F32)[AUD + REACH :]
    values = cat(before, own, behind).astype(BF16)
    for h in range(HEADS_DEV):
        copies[h].wait()
        product = dot(values[:, h * HEAD : (h + 1) * HEAD], wbuf[h * HEAD : (h + 1) * HEAD, :])
        product = product.astype(BF16)
        for j in range(N_TENSOR):
            out_ref[j, h * SPAN : (h + 1) * SPAN, :] = product[:, j * GROUP : (j + 1) * GROUP]


def value_out(qkv, from_prev, from_next, w_out, *extra):
    (out,) = call(
        value_out_kernel,
        "value_out",
        1,
        [(VMEM, qkv), (VMEM, from_prev), (VMEM, from_next), (ANY, w_out)],
        extra,
        [(VMEM, sds((N_TENSOR, KEYS, GROUP), BF16))],
        [pltpu.VMEM((GROUP, D), BF16), pltpu.SemaphoreType.DMA((HEADS_DEV,))],
    )
    return out


def row_stats(block):
    values = block.astype(F32)
    mean = jnp.mean(values, axis=-1, keepdims=True)
    centred = values - mean
    return mean, jnp.sum(centred * centred, axis=-1, keepdims=True)


def merged_stats(stat, count1, block):
    count2 = block.shape[1]
    mean1, square1 = stat[:, :1], stat[:, 1:2]
    mean2, square2 = row_stats(block)
    gap = mean2 - mean1
    total = count1 + count2
    mean = mean1 + gap * (count2 / total)
    return mean, square1 + square2 + gap * gap * (count1 * count2 / total)


def packed_stats(mean, square):
    lane = lax.broadcasted_iota(jnp.int32, (TILE, HEAD), 1)
    return jnp.where(lane == 0, mean, square)


def weight_copies(meta_ref, weights, first, count, wcat, sems):
    copies = []
    for part, (ref, tower) in enumerate(weights):
        for j in range(count):
            row = pl.multiple_of(meta_ref[first + j] * GROUP, GROUP)
            copies.append(
                pltpu.make_async_copy(
                    ref.at[tower, pl.ds(row, GROUP), :],
                    wcat.at[j * GROUP : (j + 1) * GROUP, part * GROUP : (part + 1) * GROUP],
                    sems.at[part * count + j],
                )
            )
    return copies


def column_sums(wcat):
    return dot(jnp.ones((8, wcat.shape[0]), BF16), wcat[...])


def stage_kernel(first, count, start, meta_ref, *refs):
    x_refs, weights, refs = refs[:count], refs[count : count + 3], refs[count + 3 :]
    if not start:
        acc_in, stat_in, sums_in = refs[:3]
        refs = refs[3:]
    acc_ref, stat_ref, sums_ref, wcat, xbuf, acc, stat, wsem, xsem, insem, outsem = refs

    def x_copy(t, j):
        return pltpu.make_async_copy(
            x_refs[j].at[rows_of(t), :],
            xbuf.at[rows_of(t), pl.ds(j * GROUP, GROUP)],
            xsem.at[t * count + j],
        )

    def in_copies(t):
        if start:
            return []
        return [
            pltpu.make_async_copy(acc_in.at[rows_of(t), :], acc.at[rows_of(t), :], insem.at[t]),
            pltpu.make_async_copy(
                stat_in.at[rows_of(t), :], stat.at[rows_of(t), :], insem.at[TILES + t]
            ),
        ]

    def out_copies(t):
        return [
            pltpu.make_async_copy(acc.at[rows_of(t), :], acc_ref.at[rows_of(t), :], outsem.at[t]),
            pltpu.make_async_copy(
                stat.at[rows_of(t), :], stat_ref.at[rows_of(t), :], outsem.at[TILES + t]
            ),
        ]

    wq, wk, wv = weights
    w_copies = weight_copies(meta_ref, ((wq, 0), (wk, 1), (wv, 1)), first, count, wcat, wsem)
    for copy in w_copies:
        copy.start()

    def fetch(t):
        for j in range(count):
            x_copy(t, j).start()
        for copy in in_copies(t):
            copy.start()

    fetch(0)
    for copy in w_copies:
        copy.wait()
    for t in range(1, TILES):
        fetch(t)
    here = column_sums(wcat)
    sums_ref[...] = here if start else sums_in[...] + here

    @pl.loop(0, TILES)
    def _(t):
        for j in range(count):
            x_copy(t, j).wait()
        for copy in in_copies(t):
            copy.wait()
        rows = rows_of(t)
        block = xbuf[rows, :]
        total = dot(block, wcat[...])
        if start:
            acc[rows, :] = total
            stat[rows, :] = packed_stats(*row_stats(block))
        else:
            acc[rows, :] += total
            stat[rows, :] = packed_stats(*merged_stats(stat[rows, :], first * GROUP, block))
        for copy in out_copies(t):
            copy.start()

    for t in range(TILES):
        for copy in out_copies(t):
            copy.wait()


def stage(meta, blocks, w_query, w_key, w_value, first, before=(), extra=()):
    count, start = len(blocks), not before
    state = [(ANY, a) for a in before[:2]] + [(VMEM, a) for a in before[2:]]
    return call(
        functools.partial(stage_kernel, first, count, start),
        f"stage_{first}",
        4,
        [(SMEM, meta)]
        + [(ANY, a) for a in blocks]
        + [(ANY, w_query), (ANY, w_key), (ANY, w_value)]
        + state,
        extra,
        [
            (ANY, sds((VID, 3 * GROUP), F32)),
            (ANY, sds((VID, HEAD), F32)),
            (VMEM, sds((8, 3 * GROUP), F32)),
        ],
        [
            pltpu.VMEM((count * GROUP, 3 * GROUP), BF16),
            pltpu.VMEM((VID, count * GROUP), BF16),
            pltpu.VMEM((VID, 3 * GROUP), F32),
            pltpu.VMEM((VID, HEAD), F32),
            pltpu.SemaphoreType.DMA((3 * count,)),
            pltpu.SemaphoreType.DMA((TILES * count,)),
            pltpu.SemaphoreType.DMA((2 * TILES,)),
            pltpu.SemaphoreType.DMA((2 * TILES,)),
        ],
    )


def head_norm(part, floor):
    mean_square = jnp.mean(part * part, axis=-1, keepdims=True)
    return (part * lax.rsqrt(mean_square + floor)).astype(BF16)


def last_fetch(pieces, acc_ref, cols, stat_ref, xbuf, acc, stat, sems):
    def copies(t, piece=None):
        place = pl.ds((t % 2) * TILE, TILE) if isinstance(t, int) else pl.ds(0, TILE)
        source = pieces[0 if piece is None else piece]
        return [
            pltpu.make_async_copy(source.at[place, :], xbuf.at[rows_of(t), :], sems.at[t]),
            pltpu.make_async_copy(
                acc_ref.at[rows_of(t), cols], acc.at[rows_of(t), :], sems.at[TILES + t]
            ),
            pltpu.make_async_copy(
                stat_ref.at[rows_of(t), :], stat.at[rows_of(t), :], sems.at[2 * TILES + t]
            ),
        ]

    for t in range(TILES):
        for copy in copies(t, t // 2):
            copy.start()

    def wait(t):
        for copy in copies(t):
            copy.wait()

    return wait


def query_kernel(
    meta_ref, xa, xb, xc, wq, acc_ref, stat_ref, sums_ref, qkv_ref, prev_ref, next_ref,
    pt_ref, stat_out, wcat, xbuf, acc, stat, ptbuf, wsem, insem, outsem,
):
    (w_copy,) = weight_copies(meta_ref, ((wq, 0),), 7, 1, wcat, wsem)
    w_copy.start()
    wait = last_fetch((xa, xb, xc), acc_ref, pl.ds(0, GROUP), stat_ref, xbuf, acc, stat, insem)

    shard = meta_ref[AT_SHARD]
    before = prev_ref[...].astype(F32)
    own = qkv_ref[...].astype(F32)
    behind = next_ref[...].astype(F32)
    keys = cat(
        before[AUD : AUD + REACH], own[AUD : 2 * AUD], behind[AUD : AUD + REACH]
    ).astype(BF16)

    prev_at, next_at = jnp.maximum(shard - 1, 0), jnp.minimum(shard + 1, SHARDS - 1)
    slot = lax.broadcasted_iota(jnp.int32, (SPAN, 1), 0)
    end_prev = jnp.where(shard > 0, meta_ref[AT_AUDIO + prev_at] - (AUD - REACH), 0)
    reach = jnp.minimum(meta_ref[AT_AUDIO + next_at], meta_ref[AT_VWIN + 2 * shard + 1])
    end_next = jnp.where(shard < SHARDS - 1, REACH + AUD + reach, 0)
    used = (slot >= REACH - meta_ref[AT_VWIN + 2 * shard]) & (slot < jnp.minimum(end_prev, REACH))
    used |= (slot >= REACH) & (slot < REACH + meta_ref[AT_AUDIO + shard])
    used |= (slot >= REACH + AUD) & (slot < end_next)

    w_copy.wait()
    sums = sums_ref[:1, :GROUP] + column_sums(wcat)[:1]

    def out_copies(t):
        return [
            pltpu.make_async_copy(ptbuf.at[t], pt_ref.at[t], outsem.at[t]),
            pltpu.make_async_copy(
                stat.at[rows_of(t), :], stat_out.at[rows_of(t), :], outsem.at[TILES + t]
            ),
        ]

    @pl.loop(0, TILES)
    def _(t):
        wait(t)
        rows = rows_of(t)
        block = xbuf[rows, :]
        mean, square = merged_stats(stat[rows, :], 7 * GROUP, block)
        var = square / D
        stat[rows, :] = packed_stats(mean, var)
        total = acc[rows, :] + dot(block, wcat[...]) - mean * sums
        floor = EPS * (var + EPS)
        for h in range(HEADS_DEV):
            cols = slice(h * HEAD, (h + 1) * HEAD)
            scores = dot_nt(keys[:, cols], head_norm(total[:, cols], floor))
            weights = jnp.where(used, jnp.exp2(scores * SCALE), 0.0)
            below = jnp.sum(weights, axis=0, keepdims=True)
            ptbuf[t, h * SPAN : (h + 1) * SPAN, :] = (weights * (1.0 / below)).astype(BF16)
        for copy in out_copies(t):
            copy.start()

    for t in range(TILES):
        for copy in out_copies(t):
            copy.wait()


def queries_out(meta, pieces, w_query, acc, stat, sums, qkv, from_prev, from_next, *extra):
    return call(
        query_kernel,
        "queries_out",
        2,
        [(SMEM, meta)]
        + [(ANY, a) for a in pieces]
        + [(ANY, w_query), (ANY, acc), (ANY, stat)]
        + [(VMEM, sums), (VMEM, qkv), (VMEM, from_prev), (VMEM, from_next)],
        extra,
        [(ANY, sds((TILES, KEYS, TILE), BF16)), (ANY, sds((VID, HEAD), F32))],
        [
            pltpu.VMEM((GROUP, GROUP), BF16),
            pltpu.VMEM((VID, GROUP), BF16),
            pltpu.VMEM((VID, GROUP), F32),
            pltpu.VMEM((VID, HEAD), F32),
            pltpu.VMEM((TILES, KEYS, TILE), BF16),
            pltpu.SemaphoreType.DMA((1,)),
            pltpu.SemaphoreType.DMA((3 * TILES,)),
            pltpu.SemaphoreType.DMA((2 * TILES,)),
        ],
    )


def audio_part_kernel(
    meta_ref, xa, xb, xc, wk, wv, acc_ref, stat_ref, sums_ref, qkv_ref, prev_ref, next_ref,
    part_p, part_o, part_n, wcat, xbuf, acc, stat, wsem, insem,
):
    w_copies = weight_copies(meta_ref, ((wk, 1), (wv, 1)), 7, 1, wcat, wsem)
    for copy in w_copies:
        copy.start()
    cols = pl.ds(GROUP, 2 * GROUP)
    wait = last_fetch((xa, xb, xc), acc_ref, cols, stat_ref, xbuf, acc, stat, insem)

    shard = meta_ref[AT_SHARD]
    queries = cat(prev_ref[:AUD], qkv_ref[:AUD], next_ref[:AUD])
    for ref in (part_p, part_o, part_n):
        ref[...] = jnp.zeros_like(ref)

    prev_at, next_at = jnp.maximum(shard - 1, 0), jnp.minimum(shard + 1, SHARDS - 1)
    count = meta_ref[AT_VIDEO + shard]
    row = lax.broadcasted_iota(jnp.int32, (3 * AUD, 1), 0)
    high_prev = jnp.where(shard > 0, jnp.minimum(count, meta_ref[AT_AWIN + 2 * prev_at + 1]), 0)
    high_next = jnp.where(shard < SHARDS - 1, count, 0)
    low = jnp.where(row < 2 * AUD, 0, VID - meta_ref[AT_AWIN + 2 * next_at])
    high = jnp.where(row < AUD, high_prev, jnp.where(row < 2 * AUD, count, high_next))

    for copy in w_copies:
        copy.wait()
    sums = sums_ref[:1, GROUP:] + column_sums(wcat)[:1]

    @pl.loop(0, TILES)
    def _(t):
        wait(t)
        rows = rows_of(t)
        block = xbuf[rows, :]
        mean, var = stat[rows, :1], stat[rows, 1:2]
        total = acc[rows, :] + dot(block, wcat[...]) - mean * sums
        floor = EPS * (var + EPS)
        spread = lax.rsqrt(var + EPS)
        place = t * TILE + lax.broadcasted_iota(jnp.int32, (3 * AUD, TILE), 1)
        seen = (place >= low) & (place < high)
        for h in range(HEADS_DEV):
            cols = slice(h * HEAD, (h + 1) * HEAD)
            value = (total[:, GROUP + h * HEAD : GROUP + (h + 1) * HEAD] * spread).astype(BF16)
            scores = dot_nt(queries[:, cols], head_norm(total[:, cols], floor))
            weights = jnp.where(seen, jnp.exp2(scores * SCALE), 0.0)
            bottom = jnp.broadcast_to(jnp.sum(weights, axis=1, keepdims=True), (3 * AUD, HEAD))
            top = dot(weights.astype(BF16), value)
            for g, ref in enumerate((part_p, part_o, part_n)):
                ref[0, :, cols] += top[g * AUD : (g + 1) * AUD]
                ref[1, :, cols] += bottom[g * AUD : (g + 1) * AUD]


def audio_part(meta, pieces, w_key, w_value, acc, stat, sums, qkv, from_prev, from_next):
    return call(
        audio_part_kernel,
        "audio_part",
        0,
        [(SMEM, meta)]
        + [(ANY, a) for a in pieces]
        + [(ANY, w_key), (ANY, w_value), (ANY, acc), (ANY, stat)]
        + [(VMEM, sums), (VMEM, qkv), (VMEM, from_prev), (VMEM, from_next)],
        (),
        [(VMEM, sds((2, AUD, GROUP), F32))] * 3,
        [
            pltpu.VMEM((GROUP, 2 * GROUP), BF16),
            pltpu.VMEM((VID, GROUP), BF16),
            pltpu.VMEM((VID, 2 * GROUP), F32),
            pltpu.VMEM((VID, HEAD), F32),
            pltpu.SemaphoreType.DMA((2,)),
            pltpu.SemaphoreType.DMA((3 * TILES,)),
        ],
    )


def audio_out_kernel(own_ref, prev_ref, next_ref, w_ref, out_ref, wbuf, sems):
    copies = head_rows(w_ref, 1, wbuf, sems)
    for copy in copies:
        copy.start()
    total = own_ref[...] + prev_ref[...] + next_ref[...]
    attended = (total[0] / total[1]).astype(BF16)
    for copy in copies:
        copy.wait()
    for j in range(N_TENSOR):
        out_ref[j] = dot(attended, wbuf[:, j * GROUP : (j + 1) * GROUP]).astype(BF16)


def audio_out(own, from_prev, from_next, w_out, *extra):
    (out,) = call(
        audio_out_kernel,
        "audio_out",
        0,
        [(VMEM, own), (VMEM, from_prev), (VMEM, from_next), (ANY, w_out)],
        extra,
        [(VMEM, sds((N_TENSOR, AUD, GROUP), BF16))],
        [pltpu.VMEM((GROUP, D), BF16), pltpu.SemaphoreType.DMA((HEADS_DEV,))],
    )
    return out


def value_copy(meta_ref, v_ref, j, at, projected, sem):
    return pltpu.make_async_copy(
        v_ref.at[meta_ref[j]], projected.at[at * KEYS : (at + 1) * KEYS, :], sem
    )


def output_first_kernel(meta_ref, *refs):
    p_refs, v_ref = refs[:7], refs[7]
    out_ref, projected, probs, out, vsem, psem, outsem = refs[8:]

    def p_copy(t, j):
        return pltpu.make_async_copy(
            p_refs[j].at[t], probs.at[t, pl.ds(j * KEYS, KEYS), :], psem.at[t * 7 + j]
        )

    def out_copy(t):
        return pltpu.make_async_copy(out.at[rows_of(t), :], out_ref.at[rows_of(t), :], outsem.at[t])

    v_copies = [value_copy(meta_ref, v_ref, j, j, projected, vsem.at[j]) for j in range(7)]
    for copy in v_copies:
        copy.start()
    for t in range(TILES):
        for j in range(7):
            p_copy(t, j).start()
    for copy in v_copies:
        copy.wait()

    @pl.loop(0, TILES)
    def _(t):
        for j in range(7):
            p_copy(t, j).wait()
        out[rows_of(t), :] = dot_tn(probs[t], projected[...])
        out_copy(t).start()

    for t in range(TILES):
        out_copy(t).wait()


def output_first(meta, probs, values, *extra):
    (out,) = call(
        output_first_kernel,
        "output_first",
        0,
        [(SMEM, meta)] + [(ANY, p) for p in probs] + [(ANY, values)],
        extra,
        [(ANY, sds((VID, GROUP), F32))],
        [
            pltpu.VMEM((7 * KEYS, GROUP), BF16),
            pltpu.VMEM((TILES, 7 * KEYS, TILE), BF16),
            pltpu.VMEM((VID, GROUP), F32),
            pltpu.SemaphoreType.DMA((7,)),
            pltpu.SemaphoreType.DMA((7 * TILES,)),
            pltpu.SemaphoreType.DMA((TILES,)),
        ],
    )
    return out


def output_last_kernel(
    meta_ref, low_ref, high_ref, v_ref, sum_ref, out_ref,
    projected, probs, sums, out, vsem, psem, outsem,
):
    def p_copy(t, source):
        return pltpu.make_async_copy(source, probs.at[t], psem.at[t])

    def s_copy(t):
        return pltpu.make_async_copy(
            sum_ref.at[rows_of(t), :], sums.at[rows_of(t), :], psem.at[TILES + t]
        )

    def out_copy(t):
        return pltpu.make_async_copy(out.at[rows_of(t), :], out_ref.at[rows_of(t), :], outsem.at[t])

    v_copy = value_copy(meta_ref, v_ref, 7, 0, projected, vsem.at[0])
    v_copy.start()
    for t in range(TILES):
        p_copy(t, low_ref.at[t] if t < 3 else high_ref.at[t - 3]).start()
        s_copy(t).start()
    v_copy.wait()
    limit = meta_ref[AT_VIDEO + meta_ref[AT_SHARD]]

    @pl.loop(0, TILES)
    def _(t):
        p_copy(t, low_ref.at[0]).wait()
        s_copy(t).wait()
        result = sums[rows_of(t), :] + dot_tn(probs[t], projected[...])
        row = t * TILE + lax.broadcasted_iota(jnp.int32, (TILE, 1), 0)
        out[rows_of(t), :] = jnp.where(row < limit, result, 0.0).astype(BF16)
        out_copy(t).start()

    for t in range(TILES):
        out_copy(t).wait()


def output_last(meta, low, high, values, sums):
    (out,) = call(
        output_last_kernel,
        "output_last",
        1,
        [(SMEM, meta), (ANY, low), (ANY, high), (ANY, values), (ANY, sums)],
        (),
        [(ANY, sds((VID, GROUP), BF16))],
        [
            pltpu.VMEM((KEYS, GROUP), BF16),
            pltpu.VMEM((TILES, KEYS, TILE), BF16),
            pltpu.VMEM((VID, GROUP), F32),
            pltpu.VMEM((VID, GROUP), BF16),
            pltpu.SemaphoreType.DMA((1,)),
            pltpu.SemaphoreType.DMA((2 * TILES,)),
            pltpu.SemaphoreType.DMA((TILES,)),
        ],
    )
    return out


def shards(
    video_tokens,
    audio_tokens,
    w_query,
    w_key,
    w_value,
    w_out,
    video_counts,
    audio_counts,
    video_windows,
    audio_windows,
):
    me = lax.axis_index("tensor")
    shard = lax.axis_index(("tower", "tm"))
    up = [(i, i + 1) for i in range(SHARDS - 1)]
    down = [(i + 1, i) for i in range(SHARDS - 1)]

    def to_next(array):
        return lax.ppermute(array, ("tower", "tm"), up)

    def to_prev(array):
        return lax.ppermute(array, ("tower", "tm"), down)

    offsets = ((0, 0), (0, 3), (0, 1), (1, 0), (1, 3), (0, 2), (1, 1), (1, 2))
    places = np.array([[moved(i, dy, dx) for dy, dx in offsets] for i in range(N_TENSOR)])
    order = lax.dynamic_index_in_dim(jnp.asarray(places, jnp.int32), me, 0, keepdims=False)
    meta = jnp.concatenate(
        [
            order,
            shard.reshape(1).astype(jnp.int32),
            video_counts,
            audio_counts,
            video_windows.reshape(-1),
            audio_windows.reshape(-1),
        ]
    )

    audio_blocks = lax.all_to_all(
        jnp.broadcast_to(audio_tokens[None], (N_TENSOR, AUD, GROUP)), "tensor", 0, 0
    )
    weights = (w_query, w_key, w_value)
    (own,) = gate((video_tokens,), audio_blocks)
    xl, xr, xy = right(own), left(own), across(own)
    qkv, for_prev, for_next = audio_in(audio_blocks, w_query, w_key, w_value, own)
    from_next, from_prev = to_prev(for_prev), to_next(for_next)
    projected = value_out(qkv, from_prev, from_next, w_out)
    xl, xr, xy = gate((xl, xr, xy), projected)
    yl, xq, yr = right(xy), left(xr), across(xr)
    state = stage(meta, (own, xl, xr, xy), *weights, 0)
    yl, xq, yr = gate((yl, xq, yr), state[0])
    pieces = right(yl[:THIRD]), across(xq[THIRD : 2 * THIRD]), left(yr[2 * THIRD :])
    acc, stat, sums = stage(meta, (yl, xq, yr), *weights, 4, state)
    values = lax.all_to_all(projected, "tensor", 0, 0)

    probs, stat = queries_out(
        meta, pieces, w_query, acc, stat, sums, qkv, from_prev, from_next, values
    )
    pl_, pr_, py_ = right(probs), left(probs), across(probs)
    part_prev, part_own, part_next = audio_part(
        meta, pieces, w_key, w_value, acc, stat, sums, qkv, from_prev, from_next
    )
    pl_, pr_, py_ = gate((pl_, pr_, py_), part_prev)
    pyl, pq, pyr = right(py_), left(pr_), across(pr_)
    audio_from_next, audio_from_prev = to_prev(part_prev), to_next(part_next)
    pyl, pq, pyr = gate((pyl, pq, pyr))
    low, high = right(pyl[: TILES // 2]), left(pyr[TILES // 2 :])
    audio_parts = audio_out(part_own, audio_from_prev, audio_from_next, w_out, pyl)
    video_sums = output_first(meta, (probs, pl_, pr_, py_, pyl, pq, pyr), values, audio_parts)

    audio_sums = jnp.sum(lax.all_to_all(audio_parts, "tensor", 0, 0).astype(F32), axis=0)
    audio_limit = lax.dynamic_index_in_dim(audio_counts, shard, 0, keepdims=False)
    audio_valid = jnp.arange(AUD, dtype=jnp.int32) < audio_limit
    audio_update = jnp.where(audio_valid[:, None], audio_sums, 0.0).astype(BF16)

    video_update = output_last(meta, low, high, values, video_sums)
    return (video_update, audio_update)


def solution(mesh):
    in_specs = (
        P(("tower", "tm"), "tensor"),
        P(("tower", "tm"), "tensor"),
        P(None, None, "tensor"),
        P(None, None, "tensor"),
        P(None, None, "tensor"),
        P(None, "tensor", None),
        P(),
        P(),
        P(),
        P(),
    )
    out_specs = (P(("tower", "tm"), "tensor"), P(("tower", "tm"), "tensor"))
    return jax.shard_map(shards, mesh=mesh, in_specs=in_specs, out_specs=out_specs, check_vma=False)
```

```python
import functools
import math

import jax
import jax.numpy as jnp
import numpy as np
from jax import lax
from jax.experimental import pallas as pl
from jax.experimental.pallas import tpu as pltpu
from jax.sharding import PartitionSpec as P

D = 3072
HEAD = 128
HEADS_DEV = 3
GROUP = HEADS_DEV * HEAD
N_TENSOR = 8
VID = 1536
AUD = 32
REACH = 8
SPAN = AUD + 2 * REACH
KEYS = HEADS_DEV * SPAN
PACKED = AUD + 2 * REACH
SHARDS = 16
TILE = 256
TILES = VID // TILE
THIRD = VID // 3
AT_DEST = 8
AT_SHARD = 16
AT_VIDEO = 17
AT_AUDIO = 33
AT_VWIN = 49
AT_AWIN = 81
EPS = 1e-6
SCALE = math.log2(math.e) / math.sqrt(HEAD)
F32 = jnp.float32
BF16 = jnp.bfloat16


def cost(microseconds):
    return pl.CostEstimate(
        flops=int(microseconds * 1e9), bytes_accessed=0, transcendentals=0
    )


def dot(a, b):
    return jnp.dot(a, b, preferred_element_type=F32)


def dot_nt(a, b):
    return lax.dot_general(a, b, (((1,), (1,)), ((), ())), preferred_element_type=F32)


def dot_tn(a, b):
    return lax.dot_general(a, b, (((0,), (0,)), ((), ())), preferred_element_type=F32)


ANY = pl.BlockSpec(memory_space=pl.ANY)
VMEM = pl.BlockSpec(memory_space=pltpu.VMEM)
SMEM = pl.BlockSpec(memory_space=pltpu.SMEM)
HBM = pl.BlockSpec(memory_space=pltpu.HBM)


def sds(shape, dtype):
    return jax.ShapeDtypeStruct(shape, dtype)


def call(kernel, name, micros, inputs, extra, outputs, scratch=(), aliases=None, mib=16, out_spec=VMEM):
    count = len(inputs)

    def run(*refs):
        kernel(*refs[:count], *refs[count + len(extra) :])

    arrays = [
        pltpu.with_memory_space_constraint(array, spec.memory_space)
        if spec is VMEM or spec is HBM
        else array
        for spec, array in inputs
    ]
    return pl.pallas_call(
        run,
        in_specs=[spec for spec, _ in inputs] + [ANY] * len(extra),
        out_specs=[out_spec] * len(outputs),
        out_shape=list(outputs),
        scratch_shapes=list(scratch),
        input_output_aliases=aliases or {},
        compiler_params=pltpu.CompilerParams(vmem_limit_bytes=mib * 2**20),
        cost_estimate=cost(micros),
        name=name,
    )(*arrays, *extra)


def gate(arrays, *extra, spec=ANY):
    shape = sds if spec is ANY else pltpu.VMEM
    return call(
        lambda *refs: None,
        "gate",
        0,
        [(spec, a) for a in arrays],
        extra,
        [shape(a.shape, a.dtype) for a in arrays],
        aliases={i: i for i in range(len(arrays))},
        mib=4,
        out_spec=spec,
    )


def parts(pieces, *extra):
    def kernel(*refs):
        for (_, first, count), ref, out in zip(pieces, refs, refs[len(pieces) :]):
            out[...] = ref[first : first + count]

    return call(
        kernel,
        "parts",
        0,
        [(VMEM, a) for a, _, _ in pieces],
        extra,
        [pltpu.VMEM((count,) + a.shape[1:], a.dtype) for a, _, count in pieces],
    )


def moved(index, dy, dx):
    return (index // 4 + dy) % 2 * 4 + (index % 4 + dx) % 4


OFFSETS = ((0, 0), (0, 3), (0, 1), (1, 0), (1, 3), (0, 2), (1, 1), (1, 2))


def send(array, dy, dx):
    pairs = [(i, moved(i, dy, dx)) for i in range(N_TENSOR)]
    return lax.ppermute(array, "tensor", pairs)


def right(array):
    return send(array, 0, 1)


def left(array):
    return send(array, 0, 3)


def across(array):
    return send(array, 1, 0)


def cat(*arrays):
    return jnp.concatenate(arrays, axis=0)


def rows_of(t):
    return pl.ds(pl.multiple_of(t * TILE, TILE), TILE)


def prefetch_kernel(
    meta_ref, audio_ref, wq, wk, wv, wo, copies_ref, w_ref, out_w_ref, sums_ref, sems
):
    copies = []
    for part, (ref, tower) in enumerate(((wq, 0), (wk, 1), (wv, 1))):
        for j in range(N_TENSOR):
            row = pl.multiple_of(meta_ref[j] * GROUP, GROUP)
            copies.append(
                pltpu.make_async_copy(
                    ref.at[tower, pl.ds(row, GROUP), :],
                    w_ref.at[pl.ds(j * GROUP, GROUP), pl.ds(part * GROUP, GROUP)],
                    sems.at[part * N_TENSOR + j],
                )
            )
    for tower in range(2):
        copies.append(
            pltpu.make_async_copy(
                wo.at[tower], out_w_ref.at[tower], sems.at[3 * N_TENSOR + tower]
            )
        )
    for copy in copies:
        copy.start()
    copies_ref[...] = jnp.broadcast_to(audio_ref[...][None], (N_TENSOR, AUD, GROUP))
    for copy in copies:
        copy.wait()
    sums_ref[...] = dot(jnp.ones((8, D), BF16), w_ref[...])


def prefetch(meta, audio_tokens, w_query, w_key, w_value, w_out):
    return call(
        prefetch_kernel,
        "prefetch",
        0,
        [(SMEM, meta), (VMEM, audio_tokens)]
        + [(HBM, w) for w in (w_query, w_key, w_value, w_out)],
        (),
        [
            pltpu.VMEM((N_TENSOR, AUD, GROUP), BF16),
            pltpu.VMEM((D, 3 * GROUP), BF16),
            pltpu.VMEM((2, GROUP, D), BF16),
            pltpu.VMEM((8, 3 * GROUP), F32),
        ],
        [pltpu.SemaphoreType.DMA((3 * N_TENSOR + 2,))],
    )


def audio_in_kernel(a_ref, wq, wk, wv, qkv_ref, prev_ref, next_ref, wcat, normed, sems):
    def weight(part, j):
        ref, tower = ((wq, 1), (wk, 0), (wv, 0))[part]
        rows = pl.ds(j * GROUP, GROUP)
        cols = pl.ds(part * GROUP, GROUP)
        return pltpu.make_async_copy(
            ref.at[tower, rows, :], wcat.at[rows, cols], sems.at[3 * j + part]
        )

    for j in range(N_TENSOR):
        for part in range(3):
            weight(part, j).start()

    values = a_ref[...].astype(F32)
    mean = jnp.sum(jnp.sum(values, axis=0), axis=-1, keepdims=True) / D
    centred = values - mean[None]
    var = jnp.sum(jnp.sum(centred * centred, axis=0), axis=-1, keepdims=True) / D
    normed[...] = (centred * lax.rsqrt(var + EPS)[None]).astype(BF16)

    total = jnp.zeros((AUD, 3 * GROUP), F32)
    for j in range(N_TENSOR):
        for part in range(3):
            weight(part, j).wait()
        total = total + dot(normed[j], wcat[j * GROUP : (j + 1) * GROUP, :])

    heads = []
    for h in range(2 * HEADS_DEV):
        part = total[:, h * HEAD : (h + 1) * HEAD]
        mean_square = jnp.mean(part * part, axis=-1, keepdims=True)
        heads.append(part * lax.rsqrt(mean_square + EPS))
    q = jnp.concatenate(heads[:HEADS_DEV], axis=1)
    k = jnp.concatenate(heads[HEADS_DEV:], axis=1)
    v = total[:, 2 * GROUP :]
    qkv_ref[...] = cat(q, k, v).astype(BF16)
    prev_ref[...] = cat(q, k[:REACH], v[:REACH]).astype(BF16)
    next_ref[...] = cat(q, k[AUD - REACH :], v[AUD - REACH :]).astype(BF16)


def audio_in(gathered, w_query, w_key, w_value, *extra):
    return call(
        audio_in_kernel,
        "audio_in",
        2,
        [(VMEM, gathered), (HBM, w_query), (HBM, w_key), (HBM, w_value)],
        extra,
        [
            pltpu.VMEM((3 * AUD, GROUP), BF16),
            pltpu.VMEM((PACKED, GROUP), BF16),
            pltpu.VMEM((PACKED, GROUP), BF16),
        ],
        [
            pltpu.VMEM((D, 3 * GROUP), BF16),
            pltpu.VMEM((N_TENSOR, AUD, GROUP), BF16),
            pltpu.SemaphoreType.DMA((3 * N_TENSOR,)),
        ],
    )


def dest_cols(meta_ref, j):
    return pl.ds(pl.multiple_of(meta_ref[AT_DEST + j] * GROUP, GROUP), GROUP)


def dest_cols(meta_ref, j):
    return pl.ds(pl.multiple_of(meta_ref[AT_DEST + j] * GROUP, GROUP), GROUP)


def value_out_kernel(meta_ref, qkv_ref, prev_ref, next_ref, w_ref, keep_ref, give_ref):
    before = prev_ref[...].astype(F32)[AUD + REACH :]
    own = qkv_ref[...].astype(F32)[2 * AUD :]
    behind = next_ref[...].astype(F32)[AUD + REACH :]
    values = cat(before, own, behind).astype(BF16)
    for h in range(HEADS_DEV):
        cols = slice(h * HEAD, (h + 1) * HEAD)
        for j, (dy, dx) in enumerate(OFFSETS):
            product = dot(values[:, cols], w_ref[0, cols, dest_cols(meta_ref, j)])
            out_ref = give_ref if dy else keep_ref
            out_ref[dx, h * SPAN : (h + 1) * SPAN, :] = product.astype(BF16)


def value_out(meta, qkv, from_prev, from_next, w_out, *extra):
    return call(
        value_out_kernel,
        "value_out",
        0,
        [(SMEM, meta), (VMEM, qkv), (VMEM, from_prev), (VMEM, from_next), (VMEM, w_out)],
        extra,
        [pltpu.VMEM((4, KEYS, GROUP), BF16)] * 2,
    )


def value_pairs_kernel(keep_ref, got_ref, *out_refs):
    for dx in range(1, 4):
        out_refs[dx - 1][0] = keep_ref[dx]
        out_refs[dx - 1][1] = got_ref[dx]


def value_pairs(keep, got, *extra):
    return call(
        value_pairs_kernel,
        "value_pairs",
        0,
        [(VMEM, keep), (VMEM, got)],
        extra,
        [pltpu.VMEM((2, KEYS, GROUP), BF16)] * 3,
    )


def row_stats(block):
    values = block.astype(F32)
    mean = jnp.mean(values, axis=-1, keepdims=True)
    centred = values - mean
    return mean, jnp.sum(centred * centred, axis=-1, keepdims=True)


def merged_stats(stat, count1, block):
    count2 = block.shape[1]
    mean1, square1 = stat[:, :1], stat[:, 1:2]
    mean2, square2 = row_stats(block)
    gap = mean2 - mean1
    total = count1 + count2
    mean = mean1 + gap * (count2 / total)
    return mean, square1 + square2 + gap * gap * (count1 * count2 / total)


def packed_stats(mean, square):
    lane = lax.broadcasted_iota(jnp.int32, (TILE, HEAD), 1)
    return jnp.where(lane == 0, mean, square)


def stage_kernel(first, count, start, *refs):
    x_refs, w_ref, refs = refs[:count], refs[count], refs[count + 1 :]
    acc_in, stat_in = (None, None) if start else refs[:2]
    acc, stat = refs[-2:]
    weights = pl.ds(first * GROUP, count * GROUP)

    @pl.loop(0, TILES)
    def _(t):
        rows = rows_of(t)
        block = jnp.concatenate([ref[rows, :] for ref in x_refs], axis=1)
        total = dot(block, w_ref[weights, :])
        if start:
            acc[rows, :] = total
            stat[rows, :] = packed_stats(*row_stats(block))
        else:
            acc[rows, :] = acc_in[rows, :] + total
            stat[rows, :] = packed_stats(*merged_stats(stat_in[rows, :], first * GROUP, block))


def stage(blocks, weights, first, before=(), extra=()):
    count, start = len(blocks), not before
    inputs = [(VMEM, a) for a in (*blocks, weights, *before)]
    return call(
        functools.partial(stage_kernel, first, count, start),
        f"stage_{first}",
        4,
        inputs,
        extra,
        [pltpu.VMEM((VID, 3 * GROUP), F32), pltpu.VMEM((VID, HEAD), F32)],
        aliases={} if start else {count + 1: 0, count + 2: 1},
    )


def head_norm(part, floor):
    mean_square = jnp.mean(part * part, axis=-1, keepdims=True)
    return (part * lax.rsqrt(mean_square + floor)).astype(BF16)


def by_thirds(body, pieces):
    for k, piece in enumerate(pieces):

        @pl.loop(0, TILES // 3)
        def _(u, k=k, piece=piece):
            body(k * (TILES // 3) + u, piece[rows_of(u), :])


LAST = pl.ds(7 * GROUP, GROUP)


def query_kernel(
    meta_ref, xa, xb, xc, w_ref, acc, stat_in, sums_ref, qkv_ref, prev_ref, next_ref,
    pt_ref, stat,
):
    shard = meta_ref[AT_SHARD]
    before = prev_ref[...].astype(F32)
    own = qkv_ref[...].astype(F32)
    behind = next_ref[...].astype(F32)
    keys = cat(
        before[AUD : AUD + REACH], own[AUD : 2 * AUD], behind[AUD : AUD + REACH]
    ).astype(BF16)

    prev_at, next_at = jnp.maximum(shard - 1, 0), jnp.minimum(shard + 1, SHARDS - 1)
    slot = lax.broadcasted_iota(jnp.int32, (SPAN, 1), 0)
    end_prev = jnp.where(shard > 0, meta_ref[AT_AUDIO + prev_at] - (AUD - REACH), 0)
    reach = jnp.minimum(meta_ref[AT_AUDIO + next_at], meta_ref[AT_VWIN + SHARDS + shard])
    end_next = jnp.where(shard < SHARDS - 1, REACH + AUD + reach, 0)
    used = (slot >= REACH - meta_ref[AT_VWIN + shard]) & (slot < jnp.minimum(end_prev, REACH))
    used |= (slot >= REACH) & (slot < REACH + meta_ref[AT_AUDIO + shard])
    used |= (slot >= REACH + AUD) & (slot < end_next)
    sums = sums_ref[:1, :GROUP]

    def body(t, block):
        rows = rows_of(t)
        mean, square = merged_stats(stat_in[rows, :], 7 * GROUP, block)
        var = square / D
        stat[rows, :] = packed_stats(mean, var)
        total = acc[rows, :GROUP] + dot(block, w_ref[LAST, :GROUP]) - mean * sums
        floor = EPS * (var + EPS)
        for h in range(HEADS_DEV):
            cols = slice(h * HEAD, (h + 1) * HEAD)
            scores = dot_nt(keys[:, cols], head_norm(total[:, cols], floor))
            weights = jnp.where(used, jnp.exp2(scores * SCALE), 0.0)
            below = jnp.sum(weights, axis=0, keepdims=True)
            pt_ref[t, h * SPAN : (h + 1) * SPAN, :] = (weights * (1.0 / below)).astype(BF16)

    by_thirds(body, (xa, xb, xc))


def queries_out(meta, pieces, weights, acc, stat, sums, qkv, from_prev, from_next, *extra):
    return call(
        query_kernel,
        "queries_out",
        2,
        [(SMEM, meta)]
        + [(VMEM, a) for a in (*pieces, weights, acc, stat, sums, qkv, from_prev, from_next)],
        extra,
        [pltpu.VMEM((TILES, KEYS, TILE), BF16), pltpu.VMEM((VID, HEAD), F32)],
        aliases={6: 1},
    )


def audio_part_kernel(
    meta_ref, xa, xb, xc, w_ref, acc, stat, sums_ref, qkv_ref, prev_ref, next_ref,
    part_p, part_o, part_n,
):
    shard = meta_ref[AT_SHARD]
    queries = cat(prev_ref[:AUD], qkv_ref[:AUD], next_ref[:AUD])
    for ref in (part_p, part_o, part_n):
        ref[...] = jnp.zeros_like(ref)

    prev_at, next_at = jnp.maximum(shard - 1, 0), jnp.minimum(shard + 1, SHARDS - 1)
    count = meta_ref[AT_VIDEO + shard]
    row = lax.broadcasted_iota(jnp.int32, (3 * AUD, 1), 0)
    high_prev = jnp.where(shard > 0, jnp.minimum(count, meta_ref[AT_AWIN + SHARDS + prev_at]), 0)
    high_next = jnp.where(shard < SHARDS - 1, count, 0)
    low = jnp.where(row < 2 * AUD, 0, VID - meta_ref[AT_AWIN + next_at])
    high = jnp.where(row < AUD, high_prev, jnp.where(row < 2 * AUD, count, high_next))
    sums = sums_ref[:1, GROUP:]

    def body(t, block):
        rows = rows_of(t)
        mean, var = stat[rows, :1], stat[rows, 1:2]
        total = acc[rows, GROUP:] + dot(block, w_ref[LAST, GROUP:]) - mean * sums
        floor = EPS * (var + EPS)
        spread = lax.rsqrt(var + EPS)
        place = t * TILE + lax.broadcasted_iota(jnp.int32, (3 * AUD, TILE), 1)
        seen = (place >= low) & (place < high)
        for h in range(HEADS_DEV):
            cols = slice(h * HEAD, (h + 1) * HEAD)
            value = (total[:, GROUP + h * HEAD : GROUP + (h + 1) * HEAD] * spread).astype(BF16)
            scores = dot_nt(queries[:, cols], head_norm(total[:, cols], floor))
            weights = jnp.where(seen, jnp.exp2(scores * SCALE), 0.0)
            bottom = jnp.broadcast_to(jnp.sum(weights, axis=1, keepdims=True), (3 * AUD, HEAD))
            top = dot(weights.astype(BF16), value)
            for g, ref in enumerate((part_p, part_o, part_n)):
                ref[0, :, cols] += top[g * AUD : (g + 1) * AUD]
                ref[1, :, cols] += bottom[g * AUD : (g + 1) * AUD]

    by_thirds(body, (xa, xb, xc))


def audio_part(meta, pieces, weights, acc, stat, sums, qkv, from_prev, from_next, *extra):
    return call(
        audio_part_kernel,
        "audio_part",
        0,
        [(SMEM, meta)]
        + [(VMEM, a) for a in (*pieces, weights, acc, stat, sums, qkv, from_prev, from_next)],
        extra,
        [pltpu.VMEM((2, AUD, GROUP), F32)] * 3,
    )


def audio_out_kernel(meta_ref, own_ref, prev_ref, next_ref, w_ref, keep_ref, give_ref):
    total = own_ref[...] + prev_ref[...] + next_ref[...]
    attended = (total[0] / total[1]).astype(BF16)
    for j, (dy, dx) in enumerate(OFFSETS):
        product = dot(attended, w_ref[1, :, dest_cols(meta_ref, j)]).astype(BF16)
        (give_ref if dy else keep_ref)[dx] = product


def audio_out(meta, own, from_prev, from_next, w_out, *extra):
    return call(
        audio_out_kernel,
        "audio_out",
        0,
        [(SMEM, meta), (VMEM, own), (VMEM, from_prev), (VMEM, from_next), (VMEM, w_out)],
        extra,
        [pltpu.VMEM((4, AUD, GROUP), BF16)] * 2,
    )


def audio_pair_kernel(keep_ref, got_ref, *out_refs):
    for dx in range(4):
        total = keep_ref[dx].astype(F32) + got_ref[dx].astype(F32)
        out_refs[dx][...] = total.astype(BF16)


def audio_pair(keep, got):
    return call(
        audio_pair_kernel,
        "audio_pair",
        0,
        [(VMEM, keep), (VMEM, got)],
        (),
        [pltpu.VMEM((AUD, GROUP), BF16)] * 4,
    )


def audio_sum_kernel(meta_ref, *refs):
    total = sum(ref[...].astype(F32) for ref in refs[:4])
    row = lax.broadcasted_iota(jnp.int32, (AUD, 1), 0)
    valid = row < meta_ref[AT_AUDIO + meta_ref[AT_SHARD]]
    refs[4][...] = jnp.where(valid, total, 0.0).astype(BF16)


def audio_sum(meta, received):
    (out,) = call(
        audio_sum_kernel,
        "audio_sum",
        0,
        [(SMEM, meta)] + [(VMEM, a) for a in received],
        (),
        [sds((AUD, GROUP), BF16)],
    )
    return out


def output_first_kernel(*refs):
    p_refs, (keep, got, v1, v2, v3), (out_ref, projected) = refs[:7], refs[7:12], refs[12:]
    blocks = (keep[0], v3[0], v1[0], got[0], v3[1], v2[0], v1[1])
    for j, block in enumerate(blocks):
        projected[j * KEYS : (j + 1) * KEYS, :] = block

    @pl.loop(0, TILES)
    def _(t):
        probs = jnp.concatenate([ref[t] for ref in p_refs], axis=0)
        out_ref[rows_of(t), :] = dot_tn(probs, projected[...])


def output_first(probs, values, *extra):
    (out,) = call(
        output_first_kernel,
        "output_first",
        0,
        [(VMEM, a) for a in (*probs, *values)],
        extra,
        [pltpu.VMEM((VID, GROUP), F32)],
        [pltpu.VMEM((7 * KEYS, GROUP), BF16)],
    )
    return out


def output_last_kernel(meta_ref, low_ref, high_ref, v_ref, sum_ref, out_ref, out, sems):
    limit = meta_ref[AT_VIDEO + meta_ref[AT_SHARD]]
    value = v_ref[1]

    def copy(t):
        return pltpu.make_async_copy(out.at[rows_of(t), :], out_ref.at[rows_of(t), :], sems.at[t])

    for k, ref in enumerate((low_ref, high_ref)):

        @pl.loop(0, TILES // 2)
        def _(u, k=k, ref=ref):
            t = k * (TILES // 2) + u
            result = sum_ref[rows_of(t), :] + dot_tn(ref[u], value)
            row = t * TILE + lax.broadcasted_iota(jnp.int32, (TILE, 1), 0)
            out[rows_of(t), :] = jnp.where(row < limit, result, 0.0).astype(BF16)
            copy(t).start()

    for t in range(TILES):
        copy(t).wait()


def output_last(meta, low, high, values, sums):
    (out,) = call(
        output_last_kernel,
        "output_last",
        1,
        [(SMEM, meta), (VMEM, low), (VMEM, high), (VMEM, values), (VMEM, sums)],
        (),
        [sds((VID, GROUP), BF16)],
        [pltpu.VMEM((VID, GROUP), BF16), pltpu.SemaphoreType.DMA((TILES,))],
        out_spec=ANY,
    )
    return out


def shards(
    video_tokens,
    audio_tokens,
    w_query,
    w_key,
    w_value,
    w_out,
    video_counts,
    audio_counts,
    video_windows,
    audio_windows,
):
    me = lax.axis_index("tensor")
    shard = lax.axis_index(("tower", "tm"))
    up = [(i, i + 1) for i in range(SHARDS - 1)]
    down = [(i + 1, i) for i in range(SHARDS - 1)]

    def to_next(array):
        return lax.ppermute(array, ("tower", "tm"), up)

    def to_prev(array):
        return lax.ppermute(array, ("tower", "tm"), down)

    places = np.array(
        [
            [moved(i, dy, dx) for dy, dx in OFFSETS] + [moved(i, dy, -dx) for dy, dx in OFFSETS]
            for i in range(N_TENSOR)
        ]
    )
    order = lax.dynamic_index_in_dim(jnp.asarray(places, jnp.int32), me, 0, keepdims=False)
    meta = jnp.concatenate(
        [
            order,
            shard.reshape(1).astype(jnp.int32),
            video_counts,
            audio_counts,
            video_windows.T.reshape(-1),
            audio_windows.T.reshape(-1),
        ]
    )

    xl, xr, xy = right(video_tokens), left(video_tokens), across(video_tokens)
    audio_copies, weights, w_back, sums = prefetch(
        meta, audio_tokens, w_query, w_key, w_value, w_out
    )
    audio_blocks = lax.all_to_all(audio_copies, "tensor", 0, 0)

    xl, xr, xy = gate((xl, xr, xy), audio_blocks)
    yl, xq, yr = right(xy), left(xr), across(xr)
    qkv, for_prev, for_next = audio_in(audio_blocks, w_query, w_key, w_value, xl)
    from_next, from_prev = to_prev(for_prev), to_next(for_next)
    acc, stat = stage((video_tokens, xl, xr, xy), weights, 0, (), (for_prev, for_next))

    thirds = parts(((yl, 0, THIRD), (xq, THIRD, THIRD), (yr, 2 * THIRD, THIRD)), stat)
    pieces = right(thirds[0]), across(thirds[1]), left(thirds[2])
    keep_v, give_v = value_out(meta, qkv, from_prev, from_next, w_back, thirds[0])
    got_v = across(give_v)
    acc, stat = stage((yl, xq, yr), weights, 4, (acc, stat), (keep_v,))

    heard = (qkv, from_prev, from_next)
    probs, stat = queries_out(meta, pieces, weights, acc, stat, sums, *heard)
    pl_, pr_, py_ = right(probs), left(probs), across(probs)
    to_send = value_pairs(keep_v, got_v, probs)
    v1, v2, v3 = [send(pair, 0, -dx) for dx, pair in enumerate(to_send, 1)]
    part_prev, part_own, part_next = audio_part(
        meta, pieces, weights, acc, stat, sums, *heard, to_send[0]
    )
    pl_, pr_, py_ = gate((pl_, pr_, py_), part_prev)
    pyl, pq, pyr = right(py_), left(pr_), across(pr_)
    audio_from_next, audio_from_prev = to_prev(part_prev), to_next(part_next)
    half = TILES // 2
    low, high = parts(((pyl, 0, half), (pyr, half, half)), pq)
    far_low, far_high = right(low), left(high)
    keep, give = audio_out(meta, part_own, audio_from_prev, audio_from_next, w_back, low)
    pairs = audio_pair(keep, across(give))
    received = [pairs[0]] + [send(pairs[dx], 0, -dx) for dx in range(1, 4)]
    video_sums = output_first(
        (probs, pl_, pr_, py_, pyl, pq, pyr), (keep_v, got_v, v1, v2, v3), give
    )
    audio_update = audio_sum(meta, received)
    video_update = output_last(meta, far_low, far_high, v2, video_sums)
    return (video_update, audio_update)


def solution(mesh):
    in_specs = (
        P(("tower", "tm"), "tensor"),
        P(("tower", "tm"), "tensor"),
        P(None, None, "tensor"),
        P(None, None, "tensor"),
        P(None, None, "tensor"),
        P(None, "tensor", None),
        P(),
        P(),
        P(),
        P(),
    )
    out_specs = (P(("tower", "tm"), "tensor"), P(("tower", "tm"), "tensor"))
    return jax.shard_map(shards, mesh=mesh, in_specs=in_specs, out_specs=out_specs, check_vma=False)
```

```python
import functools
import math

import jax
import jax.numpy as jnp
import numpy as np
from jax import lax
from jax.experimental import pallas as pl
from jax.experimental.pallas import tpu as pltpu
from jax.sharding import PartitionSpec as P

D = 3072
HEAD = 128
HEADS_DEV = 3
GROUP = HEADS_DEV * HEAD
N_TENSOR = 8
VID = 1536
AUD = 32
REACH = 8
SPAN = AUD + 2 * REACH
KEYS = HEADS_DEV * SPAN
PACKED = AUD + 2 * REACH
SHARDS = 16
TILE = 256
TILES = VID // TILE
THIRD = VID // 3
AT_DEST = 8
AT_SHARD = 16
AT_VIDEO = 17
AT_AUDIO = 33
AT_VWIN = 49
AT_AWIN = 81
EPS = 1e-6
SCALE = math.log2(math.e) / math.sqrt(HEAD)
F32 = jnp.float32
BF16 = jnp.bfloat16


def cost(microseconds):
    return pl.CostEstimate(
        flops=int(microseconds * 1e9), bytes_accessed=0, transcendentals=0
    )


def dot(a, b):
    return jnp.dot(a, b, preferred_element_type=F32)


def dot_nt(a, b):
    return lax.dot_general(a, b, (((1,), (1,)), ((), ())), preferred_element_type=F32)


def dot_tn(a, b):
    return lax.dot_general(a, b, (((0,), (0,)), ((), ())), preferred_element_type=F32)


ANY = pl.BlockSpec(memory_space=pl.ANY)
VMEM = pl.BlockSpec(memory_space=pltpu.VMEM)
SMEM = pl.BlockSpec(memory_space=pltpu.SMEM)
HBM = pl.BlockSpec(memory_space=pltpu.HBM)


def sds(shape, dtype):
    return jax.ShapeDtypeStruct(shape, dtype)


def call(kernel, name, micros, inputs, extra, outputs, scratch=(), aliases=None, mib=16, out_spec=VMEM):
    count = len(inputs)

    def run(*refs):
        kernel(*refs[:count], *refs[count + len(extra) :])

    arrays = [
        pltpu.with_memory_space_constraint(array, spec.memory_space)
        if spec is VMEM or spec is HBM
        else array
        for spec, array in inputs
    ]
    return pl.pallas_call(
        run,
        in_specs=[spec for spec, _ in inputs] + [ANY] * len(extra),
        out_specs=[out_spec] * len(outputs),
        out_shape=list(outputs),
        scratch_shapes=list(scratch),
        input_output_aliases=aliases or {},
        compiler_params=pltpu.CompilerParams(vmem_limit_bytes=mib * 2**20),
        cost_estimate=cost(micros),
        name=name,
    )(*arrays, *extra)


def gate(arrays, *extra, spec=ANY):
    shape = sds if spec is ANY else pltpu.VMEM
    return call(
        lambda *refs: None,
        "gate",
        0,
        [(spec, a) for a in arrays],
        extra,
        [shape(a.shape, a.dtype) for a in arrays],
        aliases={i: i for i in range(len(arrays))},
        mib=4,
        out_spec=spec,
    )


def parts(pieces, *extra):
    def kernel(*refs):
        for (_, first, count), ref, out in zip(pieces, refs, refs[len(pieces) :]):
            out[...] = ref[first : first + count]

    return call(
        kernel,
        "parts",
        0,
        [(VMEM, a) for a, _, _ in pieces],
        extra,
        [pltpu.VMEM((count,) + a.shape[1:], a.dtype) for a, _, count in pieces],
    )


def moved(index, dy, dx):
    return (index // 4 + dy) % 2 * 4 + (index % 4 + dx) % 4


OFFSETS = ((0, 0), (0, 3), (0, 1), (1, 0), (1, 3), (0, 2), (1, 1), (1, 2))


def send(array, dy, dx):
    pairs = [(i, moved(i, dy, dx)) for i in range(N_TENSOR)]
    return lax.ppermute(array, "tensor", pairs)


def right(array):
    return send(array, 0, 1)


def left(array):
    return send(array, 0, 3)


def across(array):
    return send(array, 1, 0)


def cat(*arrays):
    return jnp.concatenate(arrays, axis=0)


def rows_of(t):
    return pl.ds(pl.multiple_of(t * TILE, TILE), TILE)


def prefetch_kernel(
    meta_ref, audio_ref, wq, wk, wv, wo, copies_ref, w_ref, out_w_ref, sums_ref, sems
):
    copies = []
    for part, (ref, tower) in enumerate(((wq, 0), (wk, 1), (wv, 1))):
        for j in range(N_TENSOR):
            row = pl.multiple_of(meta_ref[j] * GROUP, GROUP)
            copies.append(
                pltpu.make_async_copy(
                    ref.at[tower, pl.ds(row, GROUP), :],
                    w_ref.at[pl.ds(j * GROUP, GROUP), pl.ds(part * GROUP, GROUP)],
                    sems.at[part * N_TENSOR + j],
                )
            )
    for tower in range(2):
        copies.append(
            pltpu.make_async_copy(
                wo.at[tower], out_w_ref.at[tower], sems.at[3 * N_TENSOR + tower]
            )
        )
    for copy in copies:
        copy.start()
    copies_ref[...] = jnp.broadcast_to(audio_ref[...][None], (N_TENSOR, AUD, GROUP))
    for copy in copies:
        copy.wait()
    sums_ref[...] = dot(jnp.ones((8, D), BF16), w_ref[...])


def prefetch(meta, audio_tokens, w_query, w_key, w_value, w_out):
    return call(
        prefetch_kernel,
        "prefetch",
        0,
        [(SMEM, meta), (VMEM, audio_tokens)]
        + [(HBM, w) for w in (w_query, w_key, w_value, w_out)],
        (),
        [
            pltpu.VMEM((N_TENSOR, AUD, GROUP), BF16),
            pltpu.VMEM((D, 3 * GROUP), BF16),
            pltpu.VMEM((2, GROUP, D), BF16),
            pltpu.VMEM((8, 3 * GROUP), F32),
        ],
        [pltpu.SemaphoreType.DMA((3 * N_TENSOR + 2,))],
    )


def audio_in_kernel(a_ref, wq, wk, wv, qkv_ref, prev_ref, next_ref, wcat, normed, sems):
    def weight(part, j):
        ref, tower = ((wq, 1), (wk, 0), (wv, 0))[part]
        rows = pl.ds(j * GROUP, GROUP)
        cols = pl.ds(part * GROUP, GROUP)
        return pltpu.make_async_copy(
            ref.at[tower, rows, :], wcat.at[rows, cols], sems.at[3 * j + part]
        )

    for j in range(N_TENSOR):
        for part in range(3):
            weight(part, j).start()

    values = a_ref[...].astype(F32)
    mean = jnp.sum(jnp.sum(values, axis=0), axis=-1, keepdims=True) / D
    centred = values - mean[None]
    var = jnp.sum(jnp.sum(centred * centred, axis=0), axis=-1, keepdims=True) / D
    normed[...] = (centred * lax.rsqrt(var + EPS)[None]).astype(BF16)

    total = jnp.zeros((AUD, 3 * GROUP), F32)
    for j in range(N_TENSOR):
        for part in range(3):
            weight(part, j).wait()
        total = total + dot(normed[j], wcat[j * GROUP : (j + 1) * GROUP, :])

    heads = []
    for h in range(2 * HEADS_DEV):
        part = total[:, h * HEAD : (h + 1) * HEAD]
        mean_square = jnp.mean(part * part, axis=-1, keepdims=True)
        heads.append(part * lax.rsqrt(mean_square + EPS))
    q = jnp.concatenate(heads[:HEADS_DEV], axis=1)
    k = jnp.concatenate(heads[HEADS_DEV:], axis=1)
    v = total[:, 2 * GROUP :]
    qkv_ref[...] = cat(q, k, v).astype(BF16)
    prev_ref[...] = cat(q, k[:REACH], v[:REACH]).astype(BF16)
    next_ref[...] = cat(q, k[AUD - REACH :], v[AUD - REACH :]).astype(BF16)


def audio_in(gathered, w_query, w_key, w_value, *extra):
    return call(
        audio_in_kernel,
        "audio_in",
        2,
        [(VMEM, gathered), (HBM, w_query), (HBM, w_key), (HBM, w_value)],
        extra,
        [
            pltpu.VMEM((3 * AUD, GROUP), BF16),
            pltpu.VMEM((PACKED, GROUP), BF16),
            pltpu.VMEM((PACKED, GROUP), BF16),
        ],
        [
            pltpu.VMEM((D, 3 * GROUP), BF16),
            pltpu.VMEM((N_TENSOR, AUD, GROUP), BF16),
            pltpu.SemaphoreType.DMA((3 * N_TENSOR,)),
        ],
    )


def dest_cols(meta_ref, j):
    return pl.ds(pl.multiple_of(meta_ref[AT_DEST + j] * GROUP, GROUP), GROUP)


def dest_cols(meta_ref, j):
    return pl.ds(pl.multiple_of(meta_ref[AT_DEST + j] * GROUP, GROUP), GROUP)


def value_out_kernel(meta_ref, qkv_ref, prev_ref, next_ref, w_ref, keep_ref, give_ref):
    before = prev_ref[...].astype(F32)[AUD + REACH :]
    own = qkv_ref[...].astype(F32)[2 * AUD :]
    behind = next_ref[...].astype(F32)[AUD + REACH :]
    values = cat(before, own, behind).astype(BF16)
    for h in range(HEADS_DEV):
        cols = slice(h * HEAD, (h + 1) * HEAD)
        for j, (dy, dx) in enumerate(OFFSETS):
            product = dot(values[:, cols], w_ref[0, cols, dest_cols(meta_ref, j)])
            out_ref = give_ref if dy else keep_ref
            out_ref[dx, h * SPAN : (h + 1) * SPAN, :] = product.astype(BF16)


def value_out(meta, qkv, from_prev, from_next, w_out, *extra):
    return call(
        value_out_kernel,
        "value_out",
        0,
        [(SMEM, meta), (VMEM, qkv), (VMEM, from_prev), (VMEM, from_next), (VMEM, w_out)],
        extra,
        [pltpu.VMEM((4, KEYS, GROUP), BF16)] * 2,
    )


FAR = TILES
NEAR = FAR + 2
MID = NEAR + 3
LATE = TILES // 2 + 2


def mid_parts_kernel(across_ref, right_ref, keep_ref, got_ref, for_right, for_left, for_across):
    for ref, far, dx, out in (
        (across_ref, keep_ref, 3, for_right),
        (right_ref, got_ref, 1, for_left),
    ):
        out[:TILES] = ref[...]
        out[FAR] = far[2, :, :TILE]
        out[FAR + 1, :, :HEAD] = far[2, :, TILE:]
        out[FAR + 1, :, HEAD:] = jnp.zeros((KEYS, HEAD), BF16)
        out[NEAR] = keep_ref[dx, :, :TILE]
        out[NEAR + 1] = got_ref[dx, :, :TILE]
        out[NEAR + 2, :, :HEAD] = keep_ref[dx, :, TILE:]
        out[NEAR + 2, :, HEAD:] = got_ref[dx, :, TILE:]
    for_across[...] = right_ref[...]


def mid_parts(from_across, from_right, keep, got, *extra):
    return call(
        mid_parts_kernel,
        "mid_parts",
        0,
        [(VMEM, a) for a in (from_across, from_right, keep, got)],
        extra,
        [pltpu.VMEM((MID, KEYS, TILE), BF16)] * 2 + [pltpu.VMEM((TILES, KEYS, TILE), BF16)],
    )


def last_parts_kernel(left_ref, far_ref, right_ref, for_right, for_left):
    half = TILES // 2
    for_right[:half] = left_ref[:half]
    for_right[half:] = left_ref[FAR:NEAR]
    for_left[:half] = right_ref[half:TILES]
    for_left[half:] = far_ref[FAR:NEAR]


def last_parts(from_left, far, from_right, *extra):
    return call(
        last_parts_kernel,
        "last_parts",
        0,
        [(VMEM, a) for a in (from_left, far, from_right)],
        extra,
        [pltpu.VMEM((LATE, KEYS, TILE), BF16)] * 2,
    )


def row_stats(block):
    values = block.astype(F32)
    mean = jnp.mean(values, axis=-1, keepdims=True)
    centred = values - mean
    return mean, jnp.sum(centred * centred, axis=-1, keepdims=True)


def merged_stats(stat, count1, block):
    count2 = block.shape[1]
    mean1, square1 = stat[:, :1], stat[:, 1:2]
    mean2, square2 = row_stats(block)
    gap = mean2 - mean1
    total = count1 + count2
    mean = mean1 + gap * (count2 / total)
    return mean, square1 + square2 + gap * gap * (count1 * count2 / total)


def packed_stats(mean, square):
    lane = lax.broadcasted_iota(jnp.int32, (TILE, HEAD), 1)
    return jnp.where(lane == 0, mean, square)


def first_kernel(*refs):
    x_refs, (w_ref, acc_q, acc_kv, stat) = refs[:4], refs[4:]

    @pl.loop(0, TILES)
    def _(t):
        rows = rows_of(t)
        block = jnp.concatenate([ref[rows, :] for ref in x_refs], axis=1)
        total = dot(block, w_ref[: 4 * GROUP, :])
        acc_q[rows, :] = total[:, :GROUP]
        acc_kv[rows, :] = total[:, GROUP:]
        stat[rows, :] = packed_stats(*row_stats(block))


def first_half(blocks, weights, *extra):
    return call(
        first_kernel,
        "first_half",
        4,
        [(VMEM, a) for a in (*blocks, weights)],
        extra,
        [
            pltpu.VMEM((VID, GROUP), F32),
            pltpu.VMEM((VID, 2 * GROUP), F32),
            pltpu.VMEM((VID, HEAD), F32),
        ],
    )


def middle_kernel(xa, xb, xc, w_ref, acc_in, stat_in, acc, stat):
    @pl.loop(0, TILES, unroll=2)
    def _(t):
        rows = rows_of(t)
        block = jnp.concatenate([xa[rows, :], xb[rows, :], xc[rows, :]], axis=1)
        acc[rows, :] = acc_in[rows, :] + dot(block, w_ref[4 * GROUP : 7 * GROUP, :GROUP])
        stat[rows, :] = packed_stats(*merged_stats(stat_in[rows, :], 4 * GROUP, block))


def middle(blocks, weights, acc, stat, *extra):
    return call(
        middle_kernel,
        "middle",
        4,
        [(VMEM, a) for a in (*blocks, weights, acc, stat)],
        extra,
        [pltpu.VMEM((VID, GROUP), F32), pltpu.VMEM((VID, HEAD), F32)],
        aliases={4: 0, 5: 1},
    )


def head_norm(part, floor):
    mean_square = jnp.mean(part * part, axis=-1, keepdims=True)
    return (part * lax.rsqrt(mean_square + floor)).astype(BF16)


def by_thirds(body, pieces):
    for k, piece in enumerate(pieces):

        @pl.loop(0, TILES // 3, unroll=True)
        def _(u, k=k, piece=piece):
            body(k * (TILES // 3) + u, piece[rows_of(u), :])


LAST = pl.ds(7 * GROUP, GROUP)


def query_kernel(
    meta_ref, xa, xb, xc, w_ref, acc, stat_in, sums_ref, qkv_ref, prev_ref, next_ref,
    pt_ref, stat,
):
    shard = meta_ref[AT_SHARD]
    before = prev_ref[...].astype(F32)
    own = qkv_ref[...].astype(F32)
    behind = next_ref[...].astype(F32)
    keys = cat(
        before[AUD : AUD + REACH], own[AUD : 2 * AUD], behind[AUD : AUD + REACH]
    ).astype(BF16)

    prev_at, next_at = jnp.maximum(shard - 1, 0), jnp.minimum(shard + 1, SHARDS - 1)
    slot = lax.broadcasted_iota(jnp.int32, (SPAN, 1), 0)
    end_prev = jnp.where(shard > 0, meta_ref[AT_AUDIO + prev_at] - (AUD - REACH), 0)
    reach = jnp.minimum(meta_ref[AT_AUDIO + next_at], meta_ref[AT_VWIN + SHARDS + shard])
    end_next = jnp.where(shard < SHARDS - 1, REACH + AUD + reach, 0)
    used = (slot >= REACH - meta_ref[AT_VWIN + shard]) & (slot < jnp.minimum(end_prev, REACH))
    used |= (slot >= REACH) & (slot < REACH + meta_ref[AT_AUDIO + shard])
    used |= (slot >= REACH + AUD) & (slot < end_next)
    sums = sums_ref[:1, :GROUP]

    def body(t, block):
        rows = rows_of(t)
        mean, square = merged_stats(stat_in[rows, :], 7 * GROUP, block)
        var = square / D
        stat[rows, :] = packed_stats(mean, var)
        total = acc[rows, :] + dot(block, w_ref[LAST, :GROUP]) - mean * sums
        floor = EPS * (var + EPS)
        for h in range(HEADS_DEV):
            cols = slice(h * HEAD, (h + 1) * HEAD)
            scores = dot_nt(keys[:, cols], head_norm(total[:, cols], floor))
            weights = jnp.where(used, jnp.exp2(scores * SCALE), 0.0)
            below = jnp.sum(weights, axis=0, keepdims=True)
            pt_ref[t, h * SPAN : (h + 1) * SPAN, :] = (weights * (1.0 / below)).astype(BF16)

    by_thirds(body, (xa, xb, xc))


def queries_out(meta, pieces, weights, acc, stat, sums, qkv, from_prev, from_next, *extra):
    return call(
        query_kernel,
        "queries_out",
        2,
        [(SMEM, meta)]
        + [(VMEM, a) for a in (*pieces, weights, acc, stat, sums, qkv, from_prev, from_next)],
        extra,
        [pltpu.VMEM((TILES, KEYS, TILE), BF16), pltpu.VMEM((VID, HEAD), F32)],
        aliases={6: 1},
    )


def audio_part_kernel(
    meta_ref, ya, yb, yc, xa, xb, xc, w_ref, acc, stat, sums_ref, qkv_ref, prev_ref, next_ref,
    part_p, part_o, part_n,
):
    shard = meta_ref[AT_SHARD]
    queries = cat(prev_ref[:AUD], qkv_ref[:AUD], next_ref[:AUD])
    for ref in (part_p, part_o, part_n):
        ref[...] = jnp.zeros_like(ref)

    prev_at, next_at = jnp.maximum(shard - 1, 0), jnp.minimum(shard + 1, SHARDS - 1)
    count = meta_ref[AT_VIDEO + shard]
    row = lax.broadcasted_iota(jnp.int32, (3 * AUD, 1), 0)
    high_prev = jnp.where(shard > 0, jnp.minimum(count, meta_ref[AT_AWIN + SHARDS + prev_at]), 0)
    high_next = jnp.where(shard < SHARDS - 1, count, 0)
    low = jnp.where(row < 2 * AUD, 0, VID - meta_ref[AT_AWIN + next_at])
    high = jnp.where(row < AUD, high_prev, jnp.where(row < 2 * AUD, count, high_next))
    sums = sums_ref[:1, GROUP:]

    def body(t, block):
        rows = rows_of(t)
        mean, var = stat[rows, :1], stat[rows, 1:2]
        block = jnp.concatenate([ya[rows, :], yb[rows, :], yc[rows, :], block], axis=1)
        total = acc[rows, :] + dot(block, w_ref[4 * GROUP :, GROUP:]) - mean * sums
        floor = EPS * (var + EPS)
        spread = lax.rsqrt(var + EPS)
        place = t * TILE + lax.broadcasted_iota(jnp.int32, (3 * AUD, TILE), 1)
        seen = (place >= low) & (place < high)
        for h in range(HEADS_DEV):
            cols = slice(h * HEAD, (h + 1) * HEAD)
            value = (total[:, GROUP + h * HEAD : GROUP + (h + 1) * HEAD] * spread).astype(BF16)
            scores = dot_nt(queries[:, cols], head_norm(total[:, cols], floor))
            weights = jnp.where(seen, jnp.exp2(scores * SCALE), 0.0)
            bottom = jnp.broadcast_to(jnp.sum(weights, axis=1, keepdims=True), (3 * AUD, HEAD))
            top = dot(weights.astype(BF16), value)
            for g, ref in enumerate((part_p, part_o, part_n)):
                ref[0, :, cols] += top[g * AUD : (g + 1) * AUD]
                ref[1, :, cols] += bottom[g * AUD : (g + 1) * AUD]

    by_thirds(body, (xa, xb, xc))


def audio_part(meta, pieces, weights, acc, stat, sums, qkv, from_prev, from_next, *extra):
    return call(
        audio_part_kernel,
        "audio_part",
        0,
        [(SMEM, meta)]
        + [(VMEM, a) for a in (*pieces, weights, acc, stat, sums, qkv, from_prev, from_next)],
        extra,
        [pltpu.VMEM((2, AUD, GROUP), F32)] * 3,
    )


def audio_out_kernel(meta_ref, own_ref, prev_ref, next_ref, w_ref, keep_ref, give_ref):
    total = own_ref[...] + prev_ref[...] + next_ref[...]
    attended = (total[0] / total[1]).astype(BF16)
    for j, (dy, dx) in enumerate(OFFSETS):
        product = dot(attended, w_ref[1, :, dest_cols(meta_ref, j)]).astype(BF16)
        (give_ref if dy else keep_ref)[dx] = product


def audio_out(meta, own, from_prev, from_next, w_out, *extra):
    return call(
        audio_out_kernel,
        "audio_out",
        0,
        [(SMEM, meta), (VMEM, own), (VMEM, from_prev), (VMEM, from_next), (VMEM, w_out)],
        extra,
        [pltpu.VMEM((4, AUD, GROUP), BF16)] * 2,
    )


def audio_pair_kernel(keep_ref, got_ref, *out_refs):
    for dx in range(4):
        total = keep_ref[dx].astype(F32) + got_ref[dx].astype(F32)
        out_refs[dx][...] = total.astype(BF16)


def audio_pair(keep, got):
    return call(
        audio_pair_kernel,
        "audio_pair",
        0,
        [(VMEM, keep), (VMEM, got)],
        (),
        [pltpu.VMEM((AUD, GROUP), BF16)] * 4,
    )


def audio_sum_kernel(meta_ref, done_ref, *refs):
    total = sum(ref[...].astype(F32) for ref in refs[:4])
    row = lax.broadcasted_iota(jnp.int32, (AUD, 1), 0)
    valid = row < meta_ref[AT_AUDIO + meta_ref[AT_SHARD]]
    refs[4][...] = jnp.where(valid, total, 0.0).astype(BF16)


def audio_sum(meta, received, done):
    (out,) = call(
        audio_sum_kernel,
        "audio_sum",
        0,
        [(SMEM, meta), (HBM, done)] + [(VMEM, a) for a in received],
        (),
        [sds((AUD, GROUP), BF16)],
    )
    return out


def output_kernel(meta_ref, *refs):
    p_refs, (low_ref, high_ref, keep, got, out_ref, projected, out, sems) = refs[:7], refs[7:]
    half = TILES // 2

    left_ref, right_ref = p_refs[4], p_refs[5]

    def near(ref, k):
        tail = slice(k * HEAD, (k + 1) * HEAD)
        return jnp.concatenate([ref[NEAR + k], ref[NEAR + 2, :, tail]], axis=1)

    def far(ref):
        return jnp.concatenate([ref[half], ref[half + 1, :, :HEAD]], axis=1)

    blocks = (
        keep[0], near(left_ref, 0), near(right_ref, 0), got[0],
        near(left_ref, 1), far(low_ref), near(right_ref, 1), far(high_ref),
    )
    for j, block in enumerate(blocks):
        projected[j * KEYS : (j + 1) * KEYS, :] = block
    limit = meta_ref[AT_VIDEO + meta_ref[AT_SHARD]]

    def copy(t):
        return pltpu.make_async_copy(out.at[rows_of(t), :], out_ref.at[rows_of(t), :], sems.at[t])

    for k, ref in enumerate((low_ref, high_ref)):

        @pl.loop(0, half)
        def _(u, k=k, ref=ref):
            t = k * half + u
            probs = jnp.concatenate([p[t] for p in p_refs] + [ref[u]], axis=0)
            result = dot_tn(probs, projected[...])
            row = t * TILE + lax.broadcasted_iota(jnp.int32, (TILE, 1), 0)
            out[rows_of(t), :] = jnp.where(row < limit, result, 0.0).astype(BF16)
            copy(t).start()

    for t in range(TILES):
        copy(t).wait()


def output(meta, probs, low, high, keep, got, *extra):
    (out,) = call(
        output_kernel,
        "output",
        1,
        [(SMEM, meta)] + [(VMEM, a) for a in (*probs, low, high, keep, got)],
        (),
        [sds((VID, GROUP), BF16)],
        [
            pltpu.VMEM((N_TENSOR * KEYS, GROUP), BF16),
            pltpu.VMEM((VID, GROUP), BF16),
            pltpu.SemaphoreType.DMA((TILES,)),
        ],
        out_spec=ANY,
    )
    return out


def shards(
    video_tokens,
    audio_tokens,
    w_query,
    w_key,
    w_value,
    w_out,
    video_counts,
    audio_counts,
    video_windows,
    audio_windows,
):
    me = lax.axis_index("tensor")
    shard = lax.axis_index(("tower", "tm"))
    up = [(i, i + 1) for i in range(SHARDS - 1)]
    down = [(i + 1, i) for i in range(SHARDS - 1)]

    def to_next(array):
        return lax.ppermute(array, ("tower", "tm"), up)

    def to_prev(array):
        return lax.ppermute(array, ("tower", "tm"), down)

    places = np.array(
        [
            [moved(i, dy, dx) for dy, dx in OFFSETS] + [moved(i, dy, -dx) for dy, dx in OFFSETS]
            for i in range(N_TENSOR)
        ]
    )
    order = lax.dynamic_index_in_dim(jnp.asarray(places, jnp.int32), me, 0, keepdims=False)
    meta = jnp.concatenate(
        [
            order,
            shard.reshape(1).astype(jnp.int32),
            video_counts,
            audio_counts,
            video_windows.T.reshape(-1),
            audio_windows.T.reshape(-1),
        ]
    )

    xl, xr, xy = right(video_tokens), left(video_tokens), across(video_tokens)
    audio_copies, weights, w_back, sums = prefetch(
        meta, audio_tokens, w_query, w_key, w_value, w_out
    )
    audio_blocks = lax.all_to_all(audio_copies, "tensor", 0, 0)

    xl, xr, xy = gate((xl, xr, xy), audio_blocks)
    yl, xq, yr = right(xy), left(xr), across(xr)
    qkv, for_prev, for_next = audio_in(audio_blocks, w_query, w_key, w_value, xl)
    from_next, from_prev = to_prev(for_prev), to_next(for_next)
    acc_q, acc_kv, stat = first_half(
        (video_tokens, xl, xr, xy), weights, for_prev, for_next
    )

    thirds = parts(((yl, 0, THIRD), (xq, THIRD, THIRD), (yr, 2 * THIRD, THIRD)), stat)
    pieces = right(thirds[0]), across(thirds[1]), left(thirds[2])
    keep_v, give_v = value_out(meta, qkv, from_prev, from_next, w_back, thirds[0])
    got_v = across(give_v)
    blocks = (yl, xq, yr)
    acc_q, stat = middle(blocks, weights, acc_q, stat, keep_v)

    heard = (qkv, from_prev, from_next)
    probs, stat = queries_out(meta, pieces, weights, acc_q, stat, sums, *heard)
    pl_, pr_, py_ = right(probs), left(probs), across(probs)
    part_prev, part_own, part_next = audio_part(
        meta, (*blocks, *pieces), weights, acc_kv, stat, sums, *heard
    )
    for_right, for_left, for_across = mid_parts(py_, pr_, keep_v, got_v, part_prev, pl_)
    pyl, pq, pyr = right(for_right), left(for_left), across(for_across)
    audio_from_next, audio_from_prev = to_prev(part_prev), to_next(part_next)
    keep, give = audio_out(meta, part_own, audio_from_prev, audio_from_next, w_back, for_right)
    for_right, for_left = last_parts(pyl, pq, pyr, give)
    low, high = right(for_right), left(for_left)
    pairs = audio_pair(keep, across(give))
    received = [pairs[0]] + [send(pairs[dx], 0, -dx) for dx in range(1, 4)]
    video_update = output(
        meta, (probs, pl_, pr_, py_, pyl, pq, pyr), low, high, keep_v, got_v, pairs[0]
    )
    audio_update = audio_sum(meta, received, video_update)
    return (video_update, audio_update)


def solution(mesh):
    in_specs = (
        P(("tower", "tm"), "tensor"),
        P(("tower", "tm"), "tensor"),
        P(None, None, "tensor"),
        P(None, None, "tensor"),
        P(None, None, "tensor"),
        P(None, "tensor", None),
        P(),
        P(),
        P(),
        P(),
    )
    out_specs = (P(("tower", "tm"), "tensor"), P(("tower", "tm"), "tensor"))
    return jax.shard_map(shards, mesh=mesh, in_specs=in_specs, out_specs=out_specs, check_vma=False)
```

```python
import functools
import math

import jax
import jax.numpy as jnp
import numpy as np
from jax import lax
from jax.experimental import pallas as pl
from jax.experimental.pallas import tpu as pltpu
from jax.sharding import PartitionSpec as P

D = 3072
HEAD = 128
HEADS_DEV = 3
GROUP = HEADS_DEV * HEAD
N_TENSOR = 8
VID = 1536
AUD = 32
REACH = 8
SPAN = AUD + 2 * REACH
KEYS = HEADS_DEV * SPAN
PACKED = AUD + 2 * REACH
SHARDS = 16
TILE = 256
TILES = VID // TILE
THIRD = VID // 3
AT_DEST = 8
AT_SHARD = 16
AT_VIDEO = 17
AT_AUDIO = 33
AT_VWIN = 49
AT_AWIN = 81
EPS = 1e-6
SCALE = math.log2(math.e) / math.sqrt(HEAD)
F32 = jnp.float32
BF16 = jnp.bfloat16


def cost(microseconds):
    return pl.CostEstimate(
        flops=int(microseconds * 1e9), bytes_accessed=0, transcendentals=0
    )


def dot(a, b):
    return jnp.dot(a, b, preferred_element_type=F32)


def dot_nt(a, b):
    return lax.dot_general(a, b, (((1,), (1,)), ((), ())), preferred_element_type=F32)


def dot_tn(a, b):
    return lax.dot_general(a, b, (((0,), (0,)), ((), ())), preferred_element_type=F32)


ANY = pl.BlockSpec(memory_space=pl.ANY)
VMEM = pl.BlockSpec(memory_space=pltpu.VMEM)
SMEM = pl.BlockSpec(memory_space=pltpu.SMEM)
HBM = pl.BlockSpec(memory_space=pltpu.HBM)


def sds(shape, dtype):
    return jax.ShapeDtypeStruct(shape, dtype)


def call(kernel, name, micros, inputs, extra, outputs, scratch=(), aliases=None, mib=16, out_spec=VMEM):
    count = len(inputs)

    def run(*refs):
        kernel(*refs[:count], *refs[count + len(extra) :])

    arrays = [
        pltpu.with_memory_space_constraint(array, spec.memory_space)
        if spec is VMEM or spec is HBM
        else array
        for spec, array in inputs
    ]
    return pl.pallas_call(
        run,
        in_specs=[spec for spec, _ in inputs] + [ANY] * len(extra),
        out_specs=[out_spec] * len(outputs),
        out_shape=list(outputs),
        scratch_shapes=list(scratch),
        input_output_aliases=aliases or {},
        compiler_params=pltpu.CompilerParams(vmem_limit_bytes=mib * 2**20),
        cost_estimate=cost(micros),
        name=name,
    )(*arrays, *extra)


def gate(arrays, *extra, spec=ANY):
    shape = sds if spec is ANY else pltpu.VMEM
    return call(
        lambda *refs: None,
        "gate",
        0,
        [(spec, a) for a in arrays],
        extra,
        [shape(a.shape, a.dtype) for a in arrays],
        aliases={i: i for i in range(len(arrays))},
        mib=4,
        out_spec=spec,
    )


def parts(pieces, *extra):
    def kernel(*refs):
        for (_, first, count), ref, out in zip(pieces, refs, refs[len(pieces) :]):
            out[...] = ref[first : first + count]

    return call(
        kernel,
        "parts",
        0,
        [(VMEM, a) for a, _, _ in pieces],
        extra,
        [pltpu.VMEM((count,) + a.shape[1:], a.dtype) for a, _, count in pieces],
    )


def moved(index, dy, dx):
    return (index // 4 + dy) % 2 * 4 + (index % 4 + dx) % 4


OFFSETS = ((0, 0), (0, 3), (0, 1), (1, 0), (1, 3), (0, 2), (1, 1), (1, 2))


def send(array, dy, dx):
    pairs = [(i, moved(i, dy, dx)) for i in range(N_TENSOR)]
    return lax.ppermute(array, "tensor", pairs)


def right(array):
    return send(array, 0, 1)


def left(array):
    return send(array, 0, 3)


def across(array):
    return send(array, 1, 0)


def cat(*arrays):
    return jnp.concatenate(arrays, axis=0)


def rows_of(t):
    return pl.ds(pl.multiple_of(t * TILE, TILE), TILE)


def prefetch_kernel(
    meta_ref, audio_ref, wq, wk, wv, wo, copies_ref, w_ref, out_w_ref, sums_ref, sems
):
    copies = []
    for part, (ref, tower) in enumerate(((wq, 0), (wk, 1), (wv, 1))):
        for j in range(N_TENSOR):
            row = pl.multiple_of(meta_ref[j] * GROUP, GROUP)
            copies.append(
                pltpu.make_async_copy(
                    ref.at[tower, pl.ds(row, GROUP), :],
                    w_ref.at[pl.ds(j * GROUP, GROUP), pl.ds(part * GROUP, GROUP)],
                    sems.at[part * N_TENSOR + j],
                )
            )
    for tower in range(2):
        copies.append(
            pltpu.make_async_copy(
                wo.at[tower], out_w_ref.at[tower], sems.at[3 * N_TENSOR + tower]
            )
        )
    for copy in copies:
        copy.start()
    copies_ref[...] = jnp.broadcast_to(audio_ref[...][None], (N_TENSOR, AUD, GROUP))
    for copy in copies:
        copy.wait()
    sums_ref[...] = dot(jnp.ones((8, D), BF16), w_ref[...])


def prefetch(meta, audio_tokens, w_query, w_key, w_value, w_out):
    return call(
        prefetch_kernel,
        "prefetch",
        0,
        [(SMEM, meta), (VMEM, audio_tokens)]
        + [(HBM, w) for w in (w_query, w_key, w_value, w_out)],
        (),
        [
            pltpu.VMEM((N_TENSOR, AUD, GROUP), BF16),
            pltpu.VMEM((D, 3 * GROUP), BF16),
            pltpu.VMEM((2, GROUP, D), BF16),
            pltpu.VMEM((8, 3 * GROUP), F32),
        ],
        [pltpu.SemaphoreType.DMA((3 * N_TENSOR + 2,))],
    )


def audio_in_kernel(a_ref, wq, wk, wv, qkv_ref, prev_ref, next_ref, wcat, normed, sems):
    def weight(part, j):
        ref, tower = ((wq, 1), (wk, 0), (wv, 0))[part]
        rows = pl.ds(j * GROUP, GROUP)
        cols = pl.ds(part * GROUP, GROUP)
        return pltpu.make_async_copy(
            ref.at[tower, rows, :], wcat.at[rows, cols], sems.at[3 * j + part]
        )

    for j in range(N_TENSOR):
        for part in range(3):
            weight(part, j).start()

    values = a_ref[...].astype(F32)
    mean = jnp.sum(jnp.sum(values, axis=0), axis=-1, keepdims=True) / D
    centred = values - mean[None]
    var = jnp.sum(jnp.sum(centred * centred, axis=0), axis=-1, keepdims=True) / D
    normed[...] = (centred * lax.rsqrt(var + EPS)[None]).astype(BF16)

    total = jnp.zeros((AUD, 3 * GROUP), F32)
    for j in range(N_TENSOR):
        for part in range(3):
            weight(part, j).wait()
        total = total + dot(normed[j], wcat[j * GROUP : (j + 1) * GROUP, :])

    heads = []
    for h in range(2 * HEADS_DEV):
        part = total[:, h * HEAD : (h + 1) * HEAD]
        mean_square = jnp.mean(part * part, axis=-1, keepdims=True)
        heads.append(part * lax.rsqrt(mean_square + EPS))
    q = jnp.concatenate(heads[:HEADS_DEV], axis=1)
    k = jnp.concatenate(heads[HEADS_DEV:], axis=1)
    v = total[:, 2 * GROUP :]
    qkv_ref[...] = cat(q, k, v).astype(BF16)
    prev_ref[...] = cat(q, k[:REACH], v[:REACH]).astype(BF16)
    next_ref[...] = cat(q, k[AUD - REACH :], v[AUD - REACH :]).astype(BF16)


def audio_in(gathered, w_query, w_key, w_value, *extra):
    return call(
        audio_in_kernel,
        "audio_in",
        2,
        [(VMEM, gathered), (HBM, w_query), (HBM, w_key), (HBM, w_value)],
        extra,
        [
            pltpu.VMEM((3 * AUD, GROUP), BF16),
            pltpu.VMEM((PACKED, GROUP), BF16),
            pltpu.VMEM((PACKED, GROUP), BF16),
        ],
        [
            pltpu.VMEM((D, 3 * GROUP), BF16),
            pltpu.VMEM((N_TENSOR, AUD, GROUP), BF16),
            pltpu.SemaphoreType.DMA((3 * N_TENSOR,)),
        ],
    )


def dest_cols(meta_ref, j):
    return pl.ds(pl.multiple_of(meta_ref[AT_DEST + j] * GROUP, GROUP), GROUP)


def dest_cols(meta_ref, j):
    return pl.ds(pl.multiple_of(meta_ref[AT_DEST + j] * GROUP, GROUP), GROUP)


def value_out_kernel(meta_ref, qkv_ref, prev_ref, next_ref, w_ref, keep_ref, give_ref):
    before = prev_ref[...].astype(F32)[AUD + REACH :]
    own = qkv_ref[...].astype(F32)[2 * AUD :]
    behind = next_ref[...].astype(F32)[AUD + REACH :]
    values = cat(before, own, behind).astype(BF16)
    for h in range(HEADS_DEV):
        cols = slice(h * HEAD, (h + 1) * HEAD)
        for j, (dy, dx) in enumerate(OFFSETS):
            product = dot(values[:, cols], w_ref[0, cols, dest_cols(meta_ref, j)])
            out_ref = give_ref if dy else keep_ref
            out_ref[dx, h * SPAN : (h + 1) * SPAN, :] = product.astype(BF16)


def value_out(meta, qkv, from_prev, from_next, w_out, *extra):
    return call(
        value_out_kernel,
        "value_out",
        0,
        [(SMEM, meta), (VMEM, qkv), (VMEM, from_prev), (VMEM, from_next), (VMEM, w_out)],
        extra,
        [pltpu.VMEM((4, KEYS, GROUP), BF16)] * 2,
    )


FAR = TILES
NEAR = FAR + 2
MID = NEAR + 3
LATE = TILES // 2 + 2


def mid_parts_kernel(across_ref, right_ref, keep_ref, got_ref, for_right, for_left, for_across):
    for ref, far, dx, out in (
        (across_ref, keep_ref, 3, for_right),
        (right_ref, got_ref, 1, for_left),
    ):
        out[:TILES] = ref[...]
        out[FAR] = far[2, :, :TILE]
        out[FAR + 1, :, :HEAD] = far[2, :, TILE:]
        out[FAR + 1, :, HEAD:] = jnp.zeros((KEYS, HEAD), BF16)
        out[NEAR] = keep_ref[dx, :, :TILE]
        out[NEAR + 1] = got_ref[dx, :, :TILE]
        out[NEAR + 2, :, :HEAD] = keep_ref[dx, :, TILE:]
        out[NEAR + 2, :, HEAD:] = got_ref[dx, :, TILE:]
    for_across[...] = right_ref[...]


def mid_parts(from_across, from_right, keep, got, *extra):
    return call(
        mid_parts_kernel,
        "mid_parts",
        0,
        [(VMEM, a) for a in (from_across, from_right, keep, got)],
        extra,
        [pltpu.VMEM((MID, KEYS, TILE), BF16)] * 2 + [pltpu.VMEM((TILES, KEYS, TILE), BF16)],
    )


def last_parts_kernel(left_ref, far_ref, right_ref, for_right, for_left):
    half = TILES // 2
    for_right[:half] = left_ref[:half]
    for_right[half:] = left_ref[FAR:NEAR]
    for_left[:half] = right_ref[half:TILES]
    for_left[half:] = far_ref[FAR:NEAR]


def last_parts(from_left, far, from_right, *extra):
    return call(
        last_parts_kernel,
        "last_parts",
        0,
        [(VMEM, a) for a in (from_left, far, from_right)],
        extra,
        [pltpu.VMEM((LATE, KEYS, TILE), BF16)] * 2,
    )


def row_stats(block):
    values = block.astype(F32)
    mean = jnp.mean(values, axis=-1, keepdims=True)
    centred = values - mean
    return mean, jnp.sum(centred * centred, axis=-1, keepdims=True)


def merged_stats(stat, count1, block):
    count = count1 + block.shape[1]
    mean1, square1 = stat[:, :1], stat[:, 1:2]
    offset = block.astype(F32) - mean1
    first = jnp.sum(offset, axis=-1, keepdims=True)
    second = jnp.sum(offset * offset, axis=-1, keepdims=True)
    shift = first / count
    return mean1 + shift, square1 + (second - first * shift)


def packed_stats(mean, square):
    lane = lax.broadcasted_iota(jnp.int32, (TILE, HEAD), 1)
    return jnp.where(lane == 0, mean, square)


def first_kernel(*refs):
    x_refs, (w_ref, acc_q, acc_kv, stat) = refs[:4], refs[4:]

    @pl.loop(0, TILES)
    def _(t):
        rows = rows_of(t)
        block = jnp.concatenate([ref[rows, :] for ref in x_refs], axis=1)
        total = dot(block, w_ref[: 4 * GROUP, :])
        acc_q[rows, :] = total[:, :GROUP]
        acc_kv[rows, :] = total[:, GROUP:]
        stat[rows, :] = packed_stats(*row_stats(block))


def first_half(blocks, weights, *extra):
    return call(
        first_kernel,
        "first_half",
        4,
        [(VMEM, a) for a in (*blocks, weights)],
        extra,
        [
            pltpu.VMEM((VID, GROUP), F32),
            pltpu.VMEM((VID, 2 * GROUP), F32),
            pltpu.VMEM((VID, HEAD), F32),
        ],
    )


def middle_kernel(xa, xb, xc, w_ref, acc_in, stat_in, acc, stat):
    @pl.loop(0, TILES, unroll=2)
    def _(t):
        rows = rows_of(t)
        block = jnp.concatenate([xa[rows, :], xb[rows, :], xc[rows, :]], axis=1)
        acc[rows, :] = acc_in[rows, :] + dot(block, w_ref[4 * GROUP : 7 * GROUP, :GROUP])
        stat[rows, :] = packed_stats(*merged_stats(stat_in[rows, :], 4 * GROUP, block))


def middle(blocks, weights, acc, stat, *extra):
    return call(
        middle_kernel,
        "middle",
        4,
        [(VMEM, a) for a in (*blocks, weights, acc, stat)],
        extra,
        [pltpu.VMEM((VID, GROUP), F32), pltpu.VMEM((VID, HEAD), F32)],
        aliases={4: 0, 5: 1},
    )


def head_norm(part, floor):
    mean_square = jnp.mean(part * part, axis=-1, keepdims=True)
    return (part * lax.rsqrt(mean_square + floor)).astype(BF16)


def by_thirds(body, pieces):
    for k, piece in enumerate(pieces):

        @pl.loop(0, TILES // 3, unroll=True)
        def _(u, k=k, piece=piece):
            body(k * (TILES // 3) + u, piece[rows_of(u), :])


LAST = pl.ds(7 * GROUP, GROUP)


def query_kernel(
    meta_ref, xa, xb, xc, w_ref, acc, stat_in, sums_ref, qkv_ref, prev_ref, next_ref,
    pt_ref, stat,
):
    shard = meta_ref[AT_SHARD]
    before = prev_ref[...].astype(F32)
    own = qkv_ref[...].astype(F32)
    behind = next_ref[...].astype(F32)
    keys = cat(
        before[AUD : AUD + REACH], own[AUD : 2 * AUD], behind[AUD : AUD + REACH]
    ).astype(BF16)

    prev_at, next_at = jnp.maximum(shard - 1, 0), jnp.minimum(shard + 1, SHARDS - 1)
    slot = lax.broadcasted_iota(jnp.int32, (SPAN, 1), 0)
    end_prev = jnp.where(shard > 0, meta_ref[AT_AUDIO + prev_at] - (AUD - REACH), 0)
    reach = jnp.minimum(meta_ref[AT_AUDIO + next_at], meta_ref[AT_VWIN + SHARDS + shard])
    end_next = jnp.where(shard < SHARDS - 1, REACH + AUD + reach, 0)
    used = (slot >= REACH - meta_ref[AT_VWIN + shard]) & (slot < jnp.minimum(end_prev, REACH))
    used |= (slot >= REACH) & (slot < REACH + meta_ref[AT_AUDIO + shard])
    used |= (slot >= REACH + AUD) & (slot < end_next)
    sums = sums_ref[:1, :GROUP]

    def body(t, block):
        rows = rows_of(t)
        mean, square = merged_stats(stat_in[rows, :], 7 * GROUP, block)
        var = square / D
        stat[rows, :] = packed_stats(mean, var)
        total = acc[rows, :] + dot(block, w_ref[LAST, :GROUP]) - mean * sums
        floor = EPS * (var + EPS)
        for h in range(HEADS_DEV):
            cols = slice(h * HEAD, (h + 1) * HEAD)
            scores = dot_nt(keys[:, cols], head_norm(total[:, cols], floor))
            weights = jnp.where(used, jnp.exp2(scores * SCALE), 0.0)
            below = jnp.sum(weights, axis=0, keepdims=True)
            pt_ref[t, h * SPAN : (h + 1) * SPAN, :] = (weights * (1.0 / below)).astype(BF16)

    by_thirds(body, (xa, xb, xc))


def queries_out(meta, pieces, weights, acc, stat, sums, qkv, from_prev, from_next, *extra):
    return call(
        query_kernel,
        "queries_out",
        2,
        [(SMEM, meta)]
        + [(VMEM, a) for a in (*pieces, weights, acc, stat, sums, qkv, from_prev, from_next)],
        extra,
        [pltpu.VMEM((TILES, KEYS, TILE), BF16), pltpu.VMEM((VID, HEAD), F32)],
        aliases={6: 1},
    )


def audio_part_kernel(
    meta_ref, ya, yb, yc, xa, xb, xc, w_ref, acc, stat, sums_ref, qkv_ref, prev_ref, next_ref,
    part_p, part_o, part_n,
):
    shard = meta_ref[AT_SHARD]
    queries = cat(prev_ref[:AUD], qkv_ref[:AUD], next_ref[:AUD])
    for ref in (part_p, part_o, part_n):
        ref[...] = jnp.zeros_like(ref)

    prev_at, next_at = jnp.maximum(shard - 1, 0), jnp.minimum(shard + 1, SHARDS - 1)
    count = meta_ref[AT_VIDEO + shard]
    row = lax.broadcasted_iota(jnp.int32, (3 * AUD, 1), 0)
    high_prev = jnp.where(shard > 0, jnp.minimum(count, meta_ref[AT_AWIN + SHARDS + prev_at]), 0)
    high_next = jnp.where(shard < SHARDS - 1, count, 0)
    low = jnp.where(row < 2 * AUD, 0, VID - meta_ref[AT_AWIN + next_at])
    high = jnp.where(row < AUD, high_prev, jnp.where(row < 2 * AUD, count, high_next))
    sums = sums_ref[:1, GROUP:]

    def body(t, block):
        rows = rows_of(t)
        mean, var = stat[rows, :1], stat[rows, 1:2]
        block = jnp.concatenate([ya[rows, :], yb[rows, :], yc[rows, :], block], axis=1)
        total = acc[rows, :] + dot(block, w_ref[4 * GROUP :, GROUP:]) - mean * sums
        floor = EPS * (var + EPS)
        spread = lax.rsqrt(var + EPS)
        place = t * TILE + lax.broadcasted_iota(jnp.int32, (3 * AUD, TILE), 1)
        seen = (place >= low) & (place < high)
        for h in range(HEADS_DEV):
            cols = slice(h * HEAD, (h + 1) * HEAD)
            value = (total[:, GROUP + h * HEAD : GROUP + (h + 1) * HEAD] * spread).astype(BF16)
            scores = dot_nt(queries[:, cols], head_norm(total[:, cols], floor))
            weights = jnp.where(seen, jnp.exp2(scores * SCALE), 0.0)
            bottom = jnp.broadcast_to(jnp.sum(weights, axis=1, keepdims=True), (3 * AUD, HEAD))
            top = dot(weights.astype(BF16), value)
            for g, ref in enumerate((part_p, part_o, part_n)):
                ref[0, :, cols] += top[g * AUD : (g + 1) * AUD]
                ref[1, :, cols] += bottom[g * AUD : (g + 1) * AUD]

    by_thirds(body, (xa, xb, xc))


def audio_part(meta, pieces, weights, acc, stat, sums, qkv, from_prev, from_next, *extra):
    return call(
        audio_part_kernel,
        "audio_part",
        0,
        [(SMEM, meta)]
        + [(VMEM, a) for a in (*pieces, weights, acc, stat, sums, qkv, from_prev, from_next)],
        extra,
        [pltpu.VMEM((2, AUD, GROUP), F32)] * 3,
    )


def audio_out_kernel(meta_ref, own_ref, prev_ref, next_ref, w_ref, keep_ref, give_ref):
    total = own_ref[...] + prev_ref[...] + next_ref[...]
    attended = (total[0] / total[1]).astype(BF16)
    for j, (dy, dx) in enumerate(OFFSETS):
        product = dot(attended, w_ref[1, :, dest_cols(meta_ref, j)]).astype(BF16)
        (give_ref if dy else keep_ref)[dx] = product


def audio_out(meta, own, from_prev, from_next, w_out, *extra):
    return call(
        audio_out_kernel,
        "audio_out",
        0,
        [(SMEM, meta), (VMEM, own), (VMEM, from_prev), (VMEM, from_next), (VMEM, w_out)],
        extra,
        [pltpu.VMEM((4, AUD, GROUP), BF16)] * 2,
    )


def audio_pair_kernel(keep_ref, got_ref, *out_refs):
    for dx in range(4):
        total = keep_ref[dx].astype(F32) + got_ref[dx].astype(F32)
        out_refs[dx][...] = total.astype(BF16)


def audio_pair(keep, got):
    return call(
        audio_pair_kernel,
        "audio_pair",
        0,
        [(VMEM, keep), (VMEM, got)],
        (),
        [pltpu.VMEM((AUD, GROUP), BF16)] * 4,
    )


def audio_sum_kernel(meta_ref, done_ref, *refs):
    total = sum(ref[...].astype(F32) for ref in refs[:4])
    row = lax.broadcasted_iota(jnp.int32, (AUD, 1), 0)
    valid = row < meta_ref[AT_AUDIO + meta_ref[AT_SHARD]]
    refs[4][...] = jnp.where(valid, total, 0.0).astype(BF16)


def audio_sum(meta, received, done):
    (out,) = call(
        audio_sum_kernel,
        "audio_sum",
        0,
        [(SMEM, meta), (HBM, done)] + [(VMEM, a) for a in received],
        (),
        [sds((AUD, GROUP), BF16)],
    )
    return out


def output_kernel(meta_ref, *refs):
    p_refs, (low_ref, high_ref, keep, got, out_ref, projected, out, sems) = refs[:7], refs[7:]
    half = TILES // 2

    left_ref, right_ref = p_refs[4], p_refs[5]

    def near(ref, k):
        tail = slice(k * HEAD, (k + 1) * HEAD)
        return jnp.concatenate([ref[NEAR + k], ref[NEAR + 2, :, tail]], axis=1)

    def far(ref):
        return jnp.concatenate([ref[half], ref[half + 1, :, :HEAD]], axis=1)

    blocks = (
        keep[0], near(left_ref, 0), near(right_ref, 0), got[0],
        near(left_ref, 1), far(low_ref), near(right_ref, 1), far(high_ref),
    )
    for j, block in enumerate(blocks):
        projected[j * KEYS : (j + 1) * KEYS, :] = block
    limit = meta_ref[AT_VIDEO + meta_ref[AT_SHARD]]

    def copy(t):
        return pltpu.make_async_copy(out.at[rows_of(t), :], out_ref.at[rows_of(t), :], sems.at[t])

    for k, ref in enumerate((low_ref, high_ref)):

        @pl.loop(0, half, unroll=True)
        def _(u, k=k, ref=ref):
            t = k * half + u
            probs = jnp.concatenate([p[t] for p in p_refs] + [ref[u]], axis=0)
            result = dot_tn(probs, projected[...])
            row = t * TILE + lax.broadcasted_iota(jnp.int32, (TILE, 1), 0)
            out[rows_of(t), :] = jnp.where(row < limit, result, 0.0).astype(BF16)
            copy(t).start()

    for t in range(TILES):
        copy(t).wait()


def output(meta, probs, low, high, keep, got, *extra):
    (out,) = call(
        output_kernel,
        "output",
        1,
        [(SMEM, meta)] + [(VMEM, a) for a in (*probs, low, high, keep, got)],
        (),
        [sds((VID, GROUP), BF16)],
        [
            pltpu.VMEM((N_TENSOR * KEYS, GROUP), BF16),
            pltpu.VMEM((VID, GROUP), BF16),
            pltpu.SemaphoreType.DMA((TILES,)),
        ],
        out_spec=ANY,
    )
    return out


def shards(
    video_tokens,
    audio_tokens,
    w_query,
    w_key,
    w_value,
    w_out,
    video_counts,
    audio_counts,
    video_windows,
    audio_windows,
):
    me = lax.axis_index("tensor")
    shard = lax.axis_index(("tower", "tm"))
    up = [(i, i + 1) for i in range(SHARDS - 1)]
    down = [(i + 1, i) for i in range(SHARDS - 1)]

    def to_next(array):
        return lax.ppermute(array, ("tower", "tm"), up)

    def to_prev(array):
        return lax.ppermute(array, ("tower", "tm"), down)

    places = np.array(
        [
            [moved(i, dy, dx) for dy, dx in OFFSETS] + [moved(i, dy, -dx) for dy, dx in OFFSETS]
            for i in range(N_TENSOR)
        ]
    )
    order = lax.dynamic_index_in_dim(jnp.asarray(places, jnp.int32), me, 0, keepdims=False)
    meta = jnp.concatenate(
        [
            order,
            shard.reshape(1).astype(jnp.int32),
            video_counts,
            audio_counts,
            video_windows.T.reshape(-1),
            audio_windows.T.reshape(-1),
        ]
    )

    xl, xr, xy = right(video_tokens), left(video_tokens), across(video_tokens)
    audio_copies, weights, w_back, sums = prefetch(
        meta, audio_tokens, w_query, w_key, w_value, w_out
    )
    audio_blocks = lax.all_to_all(audio_copies, "tensor", 0, 0)

    xl, xr, xy = gate((xl, xr, xy), audio_blocks)
    yl, xq, yr = right(xy), left(xr), across(xr)
    qkv, for_prev, for_next = audio_in(audio_blocks, w_query, w_key, w_value, xl)
    from_next, from_prev = to_prev(for_prev), to_next(for_next)
    acc_q, acc_kv, stat = first_half(
        (video_tokens, xl, xr, xy), weights, for_prev, for_next
    )

    thirds = parts(((yl, 0, THIRD), (xq, THIRD, THIRD), (yr, 2 * THIRD, THIRD)), stat)
    pieces = right(thirds[0]), across(thirds[1]), left(thirds[2])
    keep_v, give_v = value_out(meta, qkv, from_prev, from_next, w_back, thirds[0])
    got_v = across(give_v)
    blocks = (yl, xq, yr)
    acc_q, stat = middle(blocks, weights, acc_q, stat, keep_v)

    heard = (qkv, from_prev, from_next)
    probs, stat = queries_out(meta, pieces, weights, acc_q, stat, sums, *heard)
    pl_, pr_, py_ = right(probs), left(probs), across(probs)
    part_prev, part_own, part_next = audio_part(
        meta, (*blocks, *pieces), weights, acc_kv, stat, sums, *heard
    )
    for_right, for_left, for_across = mid_parts(py_, pr_, keep_v, got_v, part_prev, pl_)
    pyl, pq, pyr = right(for_right), left(for_left), across(for_across)
    audio_from_next, audio_from_prev = to_prev(part_prev), to_next(part_next)
    keep, give = audio_out(meta, part_own, audio_from_prev, audio_from_next, w_back, for_right)
    for_right, for_left = last_parts(pyl, pq, pyr, give)
    low, high = right(for_right), left(for_left)
    pairs = audio_pair(keep, across(give))
    received = [pairs[0]] + [send(pairs[dx], 0, -dx) for dx in range(1, 4)]
    video_update = output(
        meta, (probs, pl_, pr_, py_, pyl, pq, pyr), low, high, keep_v, got_v, pairs[0]
    )
    audio_update = audio_sum(meta, received, video_update)
    return (video_update, audio_update)


def solution(mesh):
    in_specs = (
        P(("tower", "tm"), "tensor"),
        P(("tower", "tm"), "tensor"),
        P(None, None, "tensor"),
        P(None, None, "tensor"),
        P(None, None, "tensor"),
        P(None, "tensor", None),
        P(),
        P(),
        P(),
        P(),
    )
    out_specs = (P(("tower", "tm"), "tensor"), P(("tower", "tm"), "tensor"))
    return jax.shard_map(shards, mesh=mesh, in_specs=in_specs, out_specs=out_specs, check_vma=False)
```

```python
import functools
import math

import jax
import jax.numpy as jnp
import numpy as np
from jax import lax
from jax.experimental import pallas as pl
from jax.experimental.pallas import tpu as pltpu
from jax.sharding import PartitionSpec as P

D = 3072
HEAD = 128
HEADS_DEV = 3
GROUP = HEADS_DEV * HEAD
N_TENSOR = 8
VID = 1536
AUD = 32
REACH = 8
SPAN = AUD + 2 * REACH
KEYS = HEADS_DEV * SPAN
PACKED = AUD + 2 * REACH
SHARDS = 16
TILE = 256
TILES = VID // TILE
THIRD = VID // 3
AT_DEST = 8
AT_SHARD = 16
AT_VIDEO = 17
AT_AUDIO = 33
AT_VWIN = 49
AT_AWIN = 81
EPS = 1e-6
SCALE = math.log2(math.e) / math.sqrt(HEAD)
F32 = jnp.float32
BF16 = jnp.bfloat16


def cost(microseconds):
    return pl.CostEstimate(
        flops=int(microseconds * 1e9), bytes_accessed=0, transcendentals=0
    )


def dot(a, b):
    return jnp.dot(a, b, preferred_element_type=F32)


def dot_nt(a, b):
    return lax.dot_general(a, b, (((1,), (1,)), ((), ())), preferred_element_type=F32)


def dot_tn(a, b):
    return lax.dot_general(a, b, (((0,), (0,)), ((), ())), preferred_element_type=F32)


ANY = pl.BlockSpec(memory_space=pl.ANY)
VMEM = pl.BlockSpec(memory_space=pltpu.VMEM)
SMEM = pl.BlockSpec(memory_space=pltpu.SMEM)
HBM = pl.BlockSpec(memory_space=pltpu.HBM)


def sds(shape, dtype):
    return jax.ShapeDtypeStruct(shape, dtype)


def call(kernel, name, micros, inputs, extra, outputs, scratch=(), aliases=None, mib=16, out_spec=VMEM):
    count = len(inputs)

    def run(*refs):
        kernel(*refs[:count], *refs[count + len(extra) :])

    arrays = [
        pltpu.with_memory_space_constraint(array, spec.memory_space)
        if spec is VMEM or spec is HBM
        else array
        for spec, array in inputs
    ]
    return pl.pallas_call(
        run,
        in_specs=[spec for spec, _ in inputs] + [ANY] * len(extra),
        out_specs=[out_spec] * len(outputs),
        out_shape=list(outputs),
        scratch_shapes=list(scratch),
        input_output_aliases=aliases or {},
        compiler_params=pltpu.CompilerParams(vmem_limit_bytes=mib * 2**20),
        cost_estimate=cost(micros),
        name=name,
    )(*arrays, *extra)


def gate(arrays, *extra, spec=ANY):
    shape = sds if spec is ANY else pltpu.VMEM
    return call(
        lambda *refs: None,
        "gate",
        0,
        [(spec, a) for a in arrays],
        extra,
        [shape(a.shape, a.dtype) for a in arrays],
        aliases={i: i for i in range(len(arrays))},
        mib=4,
        out_spec=spec,
    )


def parts(pieces, *extra):
    def kernel(*refs):
        for (_, first, count), ref, out in zip(pieces, refs, refs[len(pieces) :]):
            out[...] = ref[first : first + count]

    return call(
        kernel,
        "parts",
        0,
        [(VMEM, a) for a, _, _ in pieces],
        extra,
        [pltpu.VMEM((count,) + a.shape[1:], a.dtype) for a, _, count in pieces],
    )


def moved(index, dy, dx):
    return (index // 4 + dy) % 2 * 4 + (index % 4 + dx) % 4


OFFSETS = ((0, 0), (0, 3), (0, 1), (1, 0), (1, 3), (0, 2), (1, 1), (1, 2))


def send(array, dy, dx):
    pairs = [(i, moved(i, dy, dx)) for i in range(N_TENSOR)]
    return lax.ppermute(array, "tensor", pairs)


def right(array):
    return send(array, 0, 1)


def left(array):
    return send(array, 0, 3)


def across(array):
    return send(array, 1, 0)


def cat(*arrays):
    return jnp.concatenate(arrays, axis=0)


def rows_of(t):
    return pl.ds(pl.multiple_of(t * TILE, TILE), TILE)


def prefetch_kernel(
    meta_ref, audio_ref, wq, wk, wv, wo, copies_ref, w_ref, out_w_ref, sums_ref, sems
):
    copies = []
    for part, (ref, tower) in enumerate(((wq, 0), (wk, 1), (wv, 1))):
        for j in range(N_TENSOR):
            row = pl.multiple_of(meta_ref[j] * GROUP, GROUP)
            copies.append(
                pltpu.make_async_copy(
                    ref.at[tower, pl.ds(row, GROUP), :],
                    w_ref.at[pl.ds(j * GROUP, GROUP), pl.ds(part * GROUP, GROUP)],
                    sems.at[part * N_TENSOR + j],
                )
            )
    for tower in range(2):
        copies.append(
            pltpu.make_async_copy(
                wo.at[tower], out_w_ref.at[tower], sems.at[3 * N_TENSOR + tower]
            )
        )
    for copy in copies:
        copy.start()
    copies_ref[...] = jnp.broadcast_to(audio_ref[...][None], (N_TENSOR, AUD, GROUP))
    for copy in copies:
        copy.wait()
    sums_ref[...] = dot(jnp.ones((8, D), BF16), w_ref[...])


def prefetch(meta, audio_tokens, w_query, w_key, w_value, w_out):
    return call(
        prefetch_kernel,
        "prefetch",
        0,
        [(SMEM, meta), (VMEM, audio_tokens)]
        + [(HBM, w) for w in (w_query, w_key, w_value, w_out)],
        (),
        [
            pltpu.VMEM((N_TENSOR, AUD, GROUP), BF16),
            pltpu.VMEM((D, 3 * GROUP), BF16),
            pltpu.VMEM((2, GROUP, D), BF16),
            pltpu.VMEM((8, 3 * GROUP), F32),
        ],
        [pltpu.SemaphoreType.DMA((3 * N_TENSOR + 2,))],
    )


def audio_in_kernel(a_ref, wq, wk, wv, qkv_ref, prev_ref, next_ref, wcat, normed, sems):
    def weight(part, j):
        ref, tower = ((wq, 1), (wk, 0), (wv, 0))[part]
        rows = pl.ds(j * GROUP, GROUP)
        cols = pl.ds(part * GROUP, GROUP)
        return pltpu.make_async_copy(
            ref.at[tower, rows, :], wcat.at[rows, cols], sems.at[3 * j + part]
        )

    for j in range(N_TENSOR):
        for part in range(3):
            weight(part, j).start()

    values = a_ref[...].astype(F32)
    mean = jnp.sum(jnp.sum(values, axis=0), axis=-1, keepdims=True) / D
    centred = values - mean[None]
    var = jnp.sum(jnp.sum(centred * centred, axis=0), axis=-1, keepdims=True) / D
    normed[...] = (centred * lax.rsqrt(var + EPS)[None]).astype(BF16)

    total = jnp.zeros((AUD, 3 * GROUP), F32)
    for j in range(N_TENSOR):
        for part in range(3):
            weight(part, j).wait()
        total = total + dot(normed[j], wcat[j * GROUP : (j + 1) * GROUP, :])

    heads = []
    for h in range(2 * HEADS_DEV):
        part = total[:, h * HEAD : (h + 1) * HEAD]
        mean_square = jnp.mean(part * part, axis=-1, keepdims=True)
        heads.append(part * lax.rsqrt(mean_square + EPS))
    q = jnp.concatenate(heads[:HEADS_DEV], axis=1)
    k = jnp.concatenate(heads[HEADS_DEV:], axis=1)
    v = total[:, 2 * GROUP :]
    qkv_ref[...] = cat(q, k, v).astype(BF16)
    prev_ref[...] = cat(q, k[:REACH], v[:REACH]).astype(BF16)
    next_ref[...] = cat(q, k[AUD - REACH :], v[AUD - REACH :]).astype(BF16)


def audio_in(gathered, w_query, w_key, w_value, *extra):
    return call(
        audio_in_kernel,
        "audio_in",
        2,
        [(VMEM, gathered), (HBM, w_query), (HBM, w_key), (HBM, w_value)],
        extra,
        [
            pltpu.VMEM((3 * AUD, GROUP), BF16),
            pltpu.VMEM((PACKED, GROUP), BF16),
            pltpu.VMEM((PACKED, GROUP), BF16),
        ],
        [
            pltpu.VMEM((D, 3 * GROUP), BF16),
            pltpu.VMEM((N_TENSOR, AUD, GROUP), BF16),
            pltpu.SemaphoreType.DMA((3 * N_TENSOR,)),
        ],
    )


def dest_cols(meta_ref, j):
    return pl.ds(pl.multiple_of(meta_ref[AT_DEST + j] * GROUP, GROUP), GROUP)


def dest_cols(meta_ref, j):
    return pl.ds(pl.multiple_of(meta_ref[AT_DEST + j] * GROUP, GROUP), GROUP)


def value_out_kernel(meta_ref, qkv_ref, prev_ref, next_ref, w_ref, keep_ref, give_ref):
    before = prev_ref[...].astype(F32)[AUD + REACH :]
    own = qkv_ref[...].astype(F32)[2 * AUD :]
    behind = next_ref[...].astype(F32)[AUD + REACH :]
    values = cat(before, own, behind).astype(BF16)
    for h in range(HEADS_DEV):
        cols = slice(h * HEAD, (h + 1) * HEAD)
        for j, (dy, dx) in enumerate(OFFSETS):
            product = dot(values[:, cols], w_ref[0, cols, dest_cols(meta_ref, j)])
            out_ref = give_ref if dy else keep_ref
            out_ref[dx, h * SPAN : (h + 1) * SPAN, :] = product.astype(BF16)


def value_out(meta, qkv, from_prev, from_next, w_out, *extra):
    return call(
        value_out_kernel,
        "value_out",
        0,
        [(SMEM, meta), (VMEM, qkv), (VMEM, from_prev), (VMEM, from_next), (VMEM, w_out)],
        extra,
        [pltpu.VMEM((4, KEYS, GROUP), BF16)] * 2,
    )


FAR = TILES
NEAR = FAR + 2
MID = NEAR + 3
LATE = TILES // 2 + 2


def mid_parts_kernel(across_ref, right_ref, keep_ref, got_ref, for_right, for_left, for_across):
    for ref, far, dx, out in (
        (across_ref, keep_ref, 3, for_right),
        (right_ref, got_ref, 1, for_left),
    ):
        out[:TILES] = ref[...]
        out[FAR] = far[2, :, :TILE]
        out[FAR + 1, :, :HEAD] = far[2, :, TILE:]
        out[FAR + 1, :, HEAD:] = jnp.zeros((KEYS, HEAD), BF16)
        out[NEAR] = keep_ref[dx, :, :TILE]
        out[NEAR + 1] = got_ref[dx, :, :TILE]
        out[NEAR + 2, :, :HEAD] = keep_ref[dx, :, TILE:]
        out[NEAR + 2, :, HEAD:] = got_ref[dx, :, TILE:]
    for_across[...] = right_ref[...]


def mid_parts(from_across, from_right, keep, got, *extra):
    return call(
        mid_parts_kernel,
        "mid_parts",
        0,
        [(VMEM, a) for a in (from_across, from_right, keep, got)],
        extra,
        [pltpu.VMEM((MID, KEYS, TILE), BF16)] * 2 + [pltpu.VMEM((TILES, KEYS, TILE), BF16)],
    )


def last_parts_kernel(left_ref, far_ref, right_ref, for_right, for_left):
    half = TILES // 2
    for_right[:half] = left_ref[:half]
    for_right[half:] = left_ref[FAR:NEAR]
    for_left[:half] = right_ref[half:TILES]
    for_left[half:] = far_ref[FAR:NEAR]


def last_parts(from_left, far, from_right, *extra):
    return call(
        last_parts_kernel,
        "last_parts",
        0,
        [(VMEM, a) for a in (from_left, far, from_right)],
        extra,
        [pltpu.VMEM((LATE, KEYS, TILE), BF16)] * 2,
    )


def row_stats(block):
    values = block.astype(F32)
    mean = jnp.mean(values, axis=-1, keepdims=True)
    centred = values - mean
    return mean, jnp.sum(centred * centred, axis=-1, keepdims=True)


def merged_stats(stat, count1, block):
    count = count1 + block.shape[1]
    mean1, square1 = stat[:, :1], stat[:, 1:2]
    offset = block.astype(F32) - mean1
    first = jnp.sum(offset, axis=-1, keepdims=True)
    second = jnp.sum(offset * offset, axis=-1, keepdims=True)
    shift = first / count
    return mean1 + shift, square1 + (second - first * shift)


def packed_stats(mean, square):
    lane = lax.broadcasted_iota(jnp.int32, (TILE, HEAD), 1)
    return jnp.where(lane == 0, mean, square)


def first_kernel(*refs):
    x_refs, (w_ref, acc_q, acc_kv, stat) = refs[:4], refs[4:]

    @pl.loop(0, TILES)
    def _(t):
        rows = rows_of(t)
        block = jnp.concatenate([ref[rows, :] for ref in x_refs], axis=1)
        total = dot(block, w_ref[: 4 * GROUP, :])
        acc_q[rows, :] = total[:, :GROUP]
        acc_kv[rows, :] = total[:, GROUP:]
        stat[rows, :] = packed_stats(*row_stats(block))


def first_half(blocks, weights, *extra):
    return call(
        first_kernel,
        "first_half",
        4,
        [(VMEM, a) for a in (*blocks, weights)],
        extra,
        [
            pltpu.VMEM((VID, GROUP), F32),
            pltpu.VMEM((VID, 2 * GROUP), F32),
            pltpu.VMEM((VID, HEAD), F32),
        ],
    )


def middle_kernel(xa, xb, xc, w_ref, acc_in, stat_in, acc, stat):
    @pl.loop(0, TILES, unroll=2)
    def _(t):
        rows = rows_of(t)
        block = jnp.concatenate([xa[rows, :], xb[rows, :], xc[rows, :]], axis=1)
        acc[rows, :] = acc_in[rows, :] + dot(block, w_ref[4 * GROUP : 7 * GROUP, :GROUP])
        stat[rows, :] = packed_stats(*merged_stats(stat_in[rows, :], 4 * GROUP, block))


def middle(blocks, weights, acc, stat, *extra):
    return call(
        middle_kernel,
        "middle",
        4,
        [(VMEM, a) for a in (*blocks, weights, acc, stat)],
        extra,
        [pltpu.VMEM((VID, GROUP), F32), pltpu.VMEM((VID, HEAD), F32)],
        aliases={4: 0, 5: 1},
    )


def head_norm(part, floor):
    mean_square = jnp.mean(part * part, axis=-1, keepdims=True)
    return (part * lax.rsqrt(mean_square + floor)).astype(BF16)


def by_thirds(body, pieces):
    for k, piece in enumerate(pieces):

        @pl.loop(0, TILES // 3, unroll=True)
        def _(u, k=k, piece=piece):
            body(k * (TILES // 3) + u, piece[rows_of(u), :])


LAST = pl.ds(7 * GROUP, GROUP)


def query_kernel(
    meta_ref, xa, xb, xc, w_ref, acc, stat_in, sums_ref, qkv_ref, prev_ref, next_ref,
    pt_ref, stat,
):
    shard = meta_ref[AT_SHARD]
    before = prev_ref[...].astype(F32)
    own = qkv_ref[...].astype(F32)
    behind = next_ref[...].astype(F32)
    keys = cat(
        before[AUD : AUD + REACH], own[AUD : 2 * AUD], behind[AUD : AUD + REACH]
    ).astype(BF16)

    prev_at, next_at = jnp.maximum(shard - 1, 0), jnp.minimum(shard + 1, SHARDS - 1)
    slot = lax.broadcasted_iota(jnp.int32, (SPAN, 1), 0)
    end_prev = jnp.where(shard > 0, meta_ref[AT_AUDIO + prev_at] - (AUD - REACH), 0)
    reach = jnp.minimum(meta_ref[AT_AUDIO + next_at], meta_ref[AT_VWIN + SHARDS + shard])
    end_next = jnp.where(shard < SHARDS - 1, REACH + AUD + reach, 0)
    used = (slot >= REACH - meta_ref[AT_VWIN + shard]) & (slot < jnp.minimum(end_prev, REACH))
    used |= (slot >= REACH) & (slot < REACH + meta_ref[AT_AUDIO + shard])
    used |= (slot >= REACH + AUD) & (slot < end_next)
    sums = sums_ref[:1, :GROUP]

    def body(t, block):
        rows = rows_of(t)
        mean, square = merged_stats(stat_in[rows, :], 7 * GROUP, block)
        var = square / D
        stat[rows, :] = packed_stats(mean, var)
        total = acc[rows, :] + dot(block, w_ref[LAST, :GROUP]) - mean * sums
        floor = EPS * (var + EPS)
        place = t * TILE + lax.broadcasted_iota(jnp.int32, (1, TILE), 1)
        valid = place < meta_ref[AT_VIDEO + shard]
        for h in range(HEADS_DEV):
            cols = slice(h * HEAD, (h + 1) * HEAD)
            scores = dot_nt(keys[:, cols], head_norm(total[:, cols], floor))
            weights = jnp.where(used, jnp.exp2(scores * SCALE), 0.0)
            share = jnp.where(valid, 1.0 / jnp.sum(weights, axis=0, keepdims=True), 0.0)
            pt_ref[t, h * SPAN : (h + 1) * SPAN, :] = (weights * share).astype(BF16)

    by_thirds(body, (xa, xb, xc))


def queries_out(meta, pieces, weights, acc, stat, sums, qkv, from_prev, from_next, *extra):
    return call(
        query_kernel,
        "queries_out",
        2,
        [(SMEM, meta)]
        + [(VMEM, a) for a in (*pieces, weights, acc, stat, sums, qkv, from_prev, from_next)],
        extra,
        [pltpu.VMEM((TILES, KEYS, TILE), BF16), pltpu.VMEM((VID, HEAD), F32)],
        aliases={6: 1},
    )


def audio_part_kernel(
    meta_ref, ya, yb, yc, xa, xb, xc, w_ref, acc, stat, sums_ref, qkv_ref, prev_ref, next_ref,
    part_p, part_o, part_n,
):
    shard = meta_ref[AT_SHARD]
    queries = cat(prev_ref[:AUD], qkv_ref[:AUD], next_ref[:AUD])
    for ref in (part_p, part_o, part_n):
        ref[...] = jnp.zeros_like(ref)

    prev_at, next_at = jnp.maximum(shard - 1, 0), jnp.minimum(shard + 1, SHARDS - 1)
    count = meta_ref[AT_VIDEO + shard]
    row = lax.broadcasted_iota(jnp.int32, (3 * AUD, 1), 0)
    high_prev = jnp.where(shard > 0, jnp.minimum(count, meta_ref[AT_AWIN + SHARDS + prev_at]), 0)
    high_next = jnp.where(shard < SHARDS - 1, count, 0)
    low = jnp.where(row < 2 * AUD, 0, VID - meta_ref[AT_AWIN + next_at])
    high = jnp.where(row < AUD, high_prev, jnp.where(row < 2 * AUD, count, high_next))
    sums = sums_ref[:1, GROUP:]

    def body(t, block):
        rows = rows_of(t)
        mean, var = stat[rows, :1], stat[rows, 1:2]
        block = jnp.concatenate([ya[rows, :], yb[rows, :], yc[rows, :], block], axis=1)
        total = acc[rows, :] + dot(block, w_ref[4 * GROUP :, GROUP:]) - mean * sums
        floor = EPS * (var + EPS)
        spread = lax.rsqrt(var + EPS)
        place = t * TILE + lax.broadcasted_iota(jnp.int32, (3 * AUD, TILE), 1)
        seen = (place >= low) & (place < high)
        for h in range(HEADS_DEV):
            cols = slice(h * HEAD, (h + 1) * HEAD)
            value = (total[:, GROUP + h * HEAD : GROUP + (h + 1) * HEAD] * spread).astype(BF16)
            scores = dot_nt(queries[:, cols], head_norm(total[:, cols], floor))
            weights = jnp.where(seen, jnp.exp2(scores * SCALE), 0.0)
            bottom = jnp.broadcast_to(jnp.sum(weights, axis=1, keepdims=True), (3 * AUD, HEAD))
            top = dot(weights.astype(BF16), value)
            for g, ref in enumerate((part_p, part_o, part_n)):
                ref[0, :, cols] += top[g * AUD : (g + 1) * AUD]
                ref[1, :, cols] += bottom[g * AUD : (g + 1) * AUD]

    by_thirds(body, (xa, xb, xc))


def audio_part(meta, pieces, weights, acc, stat, sums, qkv, from_prev, from_next, *extra):
    return call(
        audio_part_kernel,
        "audio_part",
        0,
        [(SMEM, meta)]
        + [(VMEM, a) for a in (*pieces, weights, acc, stat, sums, qkv, from_prev, from_next)],
        extra,
        [pltpu.VMEM((2, AUD, GROUP), F32)] * 3,
    )


def audio_out_kernel(meta_ref, own_ref, prev_ref, next_ref, w_ref, keep_ref, give_ref):
    total = own_ref[...] + prev_ref[...] + next_ref[...]
    row = lax.broadcasted_iota(jnp.int32, (AUD, 1), 0)
    valid = row < meta_ref[AT_AUDIO + meta_ref[AT_SHARD]]
    attended = jnp.where(valid, total[0] / total[1], 0.0).astype(BF16)
    for j, (dy, dx) in enumerate(OFFSETS):
        product = dot(attended, w_ref[1, :, dest_cols(meta_ref, j)]).astype(BF16)
        (give_ref if dy else keep_ref)[dx] = product


def audio_out(meta, own, from_prev, from_next, w_out, *extra):
    return call(
        audio_out_kernel,
        "audio_out",
        0,
        [(SMEM, meta), (VMEM, own), (VMEM, from_prev), (VMEM, from_next), (VMEM, w_out)],
        extra,
        [pltpu.VMEM((4, AUD, GROUP), BF16)] * 2,
    )


def audio_pair_kernel(keep_ref, got_ref, *out_refs):
    for dx in range(4):
        total = keep_ref[dx].astype(F32) + got_ref[dx].astype(F32)
        out_refs[dx][...] = total.astype(BF16)


def audio_pair(keep, got):
    return call(
        audio_pair_kernel,
        "audio_pair",
        0,
        [(VMEM, keep), (VMEM, got)],
        (),
        [pltpu.VMEM((AUD, GROUP), BF16)] * 4,
    )


def audio_sum_kernel(done_ref, *refs):
    refs[4][...] = sum(ref[...].astype(F32) for ref in refs[:4]).astype(BF16)


def audio_sum(received, done):
    (out,) = call(
        audio_sum_kernel,
        "audio_sum",
        0,
        [(HBM, done)] + [(VMEM, a) for a in received],
        (),
        [sds((AUD, GROUP), BF16)],
    )
    return out


def output_kernel(*refs):
    p_refs, (low_ref, high_ref, keep, got, out_ref, projected, out, sems) = refs[:7], refs[7:]
    half = TILES // 2

    left_ref, right_ref = p_refs[4], p_refs[5]

    def near(ref, k):
        tail = slice(k * HEAD, (k + 1) * HEAD)
        return jnp.concatenate([ref[NEAR + k], ref[NEAR + 2, :, tail]], axis=1)

    def far(ref):
        return jnp.concatenate([ref[half], ref[half + 1, :, :HEAD]], axis=1)

    blocks = (
        keep[0], near(left_ref, 0), near(right_ref, 0), got[0],
        near(left_ref, 1), far(low_ref), near(right_ref, 1), far(high_ref),
    )
    for j, block in enumerate(blocks):
        projected[j * KEYS : (j + 1) * KEYS, :] = block

    def copy(t):
        return pltpu.make_async_copy(out.at[rows_of(t), :], out_ref.at[rows_of(t), :], sems.at[t])

    for k, ref in enumerate((low_ref, high_ref)):

        @pl.loop(0, half, unroll=True)
        def _(u, k=k, ref=ref):
            t = k * half + u
            probs = jnp.concatenate([p[t] for p in p_refs] + [ref[u]], axis=0)
            result = dot_tn(probs, projected[...])
            out[rows_of(t), :] = result.astype(BF16)
            copy(t).start()

    for t in range(TILES):
        copy(t).wait()


def output(probs, low, high, keep, got, *extra):
    (out,) = call(
        output_kernel,
        "output",
        1,
        [(VMEM, a) for a in (*probs, low, high, keep, got)],
        (),
        [sds((VID, GROUP), BF16)],
        [
            pltpu.VMEM((N_TENSOR * KEYS, GROUP), BF16),
            pltpu.VMEM((VID, GROUP), BF16),
            pltpu.SemaphoreType.DMA((TILES,)),
        ],
        out_spec=ANY,
    )
    return out


def shards(
    video_tokens,
    audio_tokens,
    w_query,
    w_key,
    w_value,
    w_out,
    video_counts,
    audio_counts,
    video_windows,
    audio_windows,
):
    me = lax.axis_index("tensor")
    shard = lax.axis_index(("tower", "tm"))
    up = [(i, i + 1) for i in range(SHARDS - 1)]
    down = [(i + 1, i) for i in range(SHARDS - 1)]

    def to_next(array):
        return lax.ppermute(array, ("tower", "tm"), up)

    def to_prev(array):
        return lax.ppermute(array, ("tower", "tm"), down)

    places = np.array(
        [
            [moved(i, dy, dx) for dy, dx in OFFSETS] + [moved(i, dy, -dx) for dy, dx in OFFSETS]
            for i in range(N_TENSOR)
        ]
    )
    order = lax.dynamic_index_in_dim(jnp.asarray(places, jnp.int32), me, 0, keepdims=False)
    meta = jnp.concatenate(
        [
            order,
            shard.reshape(1).astype(jnp.int32),
            video_counts,
            audio_counts,
            video_windows.T.reshape(-1),
            audio_windows.T.reshape(-1),
        ]
    )

    xl, xr, xy = right(video_tokens), left(video_tokens), across(video_tokens)
    audio_copies, weights, w_back, sums = prefetch(
        meta, audio_tokens, w_query, w_key, w_value, w_out
    )
    audio_blocks = lax.all_to_all(audio_copies, "tensor", 0, 0)

    xl, xr, xy = gate((xl, xr, xy), audio_blocks)
    yl, xq, yr = right(xy), left(xr), across(xr)
    qkv, for_prev, for_next = audio_in(audio_blocks, w_query, w_key, w_value, xl)
    from_next, from_prev = to_prev(for_prev), to_next(for_next)
    acc_q, acc_kv, stat = first_half(
        (video_tokens, xl, xr, xy), weights, for_prev, for_next
    )

    thirds = parts(((yl, 0, THIRD), (xq, THIRD, THIRD), (yr, 2 * THIRD, THIRD)), stat)
    pieces = right(thirds[0]), across(thirds[1]), left(thirds[2])
    keep_v, give_v = value_out(meta, qkv, from_prev, from_next, w_back, thirds[0])
    got_v = across(give_v)
    blocks = (yl, xq, yr)
    acc_q, stat = middle(blocks, weights, acc_q, stat, keep_v)

    heard = (qkv, from_prev, from_next)
    probs, stat = queries_out(meta, pieces, weights, acc_q, stat, sums, *heard)
    pl_, pr_, py_ = right(probs), left(probs), across(probs)
    part_prev, part_own, part_next = audio_part(
        meta, (*blocks, *pieces), weights, acc_kv, stat, sums, *heard
    )
    for_right, for_left, for_across = mid_parts(py_, pr_, keep_v, got_v, part_prev, pl_)
    pyl, pq, pyr = right(for_right), left(for_left), across(for_across)
    audio_from_next, audio_from_prev = to_prev(part_prev), to_next(part_next)
    keep, give = audio_out(meta, part_own, audio_from_prev, audio_from_next, w_back, for_right)
    for_right, for_left = last_parts(pyl, pq, pyr, give)
    low, high = right(for_right), left(for_left)
    pairs = audio_pair(keep, across(give))
    received = [pairs[0]] + [send(pairs[dx], 0, -dx) for dx in range(1, 4)]
    video_update = output(
        (probs, pl_, pr_, py_, pyl, pq, pyr), low, high, keep_v, got_v, pairs[0]
    )
    audio_update = audio_sum(received, video_update)
    return (video_update, audio_update)


def solution(mesh):
    in_specs = (
        P(("tower", "tm"), "tensor"),
        P(("tower", "tm"), "tensor"),
        P(None, None, "tensor"),
        P(None, None, "tensor"),
        P(None, None, "tensor"),
        P(None, "tensor", None),
        P(),
        P(),
        P(),
        P(),
    )
    out_specs = (P(("tower", "tm"), "tensor"), P(("tower", "tm"), "tensor"))
    return jax.shard_map(shards, mesh=mesh, in_specs=in_specs, out_specs=out_specs, check_vma=False)
```

```python
import functools
import math

import jax
import jax.numpy as jnp
import numpy as np
from jax import lax
from jax.experimental import pallas as pl
from jax.experimental.pallas import tpu as pltpu
from jax.sharding import PartitionSpec as P

D = 3072
HEAD = 128
HEADS_DEV = 3
GROUP = HEADS_DEV * HEAD
N_TENSOR = 8
VID = 1536
AUD = 32
REACH = 8
SPAN = AUD + 2 * REACH
KEYS = HEADS_DEV * SPAN
PACKED = AUD + 2 * REACH
SHARDS = 16
TILE = 256
TILES = VID // TILE
THIRD = VID // 3
AT_DEST = 8
AT_SHARD = 16
AT_VIDEO = 17
AT_AUDIO = 33
AT_VWIN = 49
AT_AWIN = 81
EPS = 1e-6
SCALE = math.log2(math.e) / math.sqrt(HEAD)
F32 = jnp.float32
BF16 = jnp.bfloat16


def cost(microseconds):
    return pl.CostEstimate(
        flops=int(microseconds * 1e9), bytes_accessed=0, transcendentals=0
    )


def dot(a, b):
    return jnp.dot(a, b, preferred_element_type=F32)


def dot_nt(a, b):
    return lax.dot_general(a, b, (((1,), (1,)), ((), ())), preferred_element_type=F32)


def dot_tn(a, b):
    return lax.dot_general(a, b, (((0,), (0,)), ((), ())), preferred_element_type=F32)


ANY = pl.BlockSpec(memory_space=pl.ANY)
VMEM = pl.BlockSpec(memory_space=pltpu.VMEM)
SMEM = pl.BlockSpec(memory_space=pltpu.SMEM)
HBM = pl.BlockSpec(memory_space=pltpu.HBM)


def sds(shape, dtype):
    return jax.ShapeDtypeStruct(shape, dtype)


def call(kernel, name, micros, inputs, extra, outputs, scratch=(), aliases=None, mib=16, out_spec=VMEM):
    count = len(inputs)

    def run(*refs):
        kernel(*refs[:count], *refs[count + len(extra) :])

    arrays = [
        pltpu.with_memory_space_constraint(array, spec.memory_space)
        if spec is VMEM or spec is HBM
        else array
        for spec, array in inputs
    ]
    return pl.pallas_call(
        run,
        in_specs=[spec for spec, _ in inputs] + [ANY] * len(extra),
        out_specs=[out_spec] * len(outputs),
        out_shape=list(outputs),
        scratch_shapes=list(scratch),
        input_output_aliases=aliases or {},
        compiler_params=pltpu.CompilerParams(vmem_limit_bytes=mib * 2**20),
        cost_estimate=cost(micros),
        name=name,
    )(*arrays, *extra)


def gate(arrays, *extra, spec=ANY):
    shape = sds if spec is ANY else pltpu.VMEM
    return call(
        lambda *refs: None,
        "gate",
        0,
        [(spec, a) for a in arrays],
        extra,
        [shape(a.shape, a.dtype) for a in arrays],
        aliases={i: i for i in range(len(arrays))},
        mib=4,
        out_spec=spec,
    )


def parts(pieces, *extra):
    def kernel(*refs):
        for (_, first, count), ref, out in zip(pieces, refs, refs[len(pieces) :]):
            out[...] = ref[first : first + count]

    return call(
        kernel,
        "parts",
        0,
        [(VMEM, a) for a, _, _ in pieces],
        extra,
        [pltpu.VMEM((count,) + a.shape[1:], a.dtype) for a, _, count in pieces],
    )


def moved(index, dy, dx):
    return (index // 4 + dy) % 2 * 4 + (index % 4 + dx) % 4


OFFSETS = ((0, 0), (0, 3), (0, 1), (1, 0), (1, 3), (0, 2), (1, 1), (1, 2))


def send(array, dy, dx):
    pairs = [(i, moved(i, dy, dx)) for i in range(N_TENSOR)]
    return lax.ppermute(array, "tensor", pairs)


def right(array):
    return send(array, 0, 1)


def left(array):
    return send(array, 0, 3)


def across(array):
    return send(array, 1, 0)


def cat(*arrays):
    return jnp.concatenate(arrays, axis=0)


def rows_of(t):
    return pl.ds(pl.multiple_of(t * TILE, TILE), TILE)


def prefetch_kernel(
    meta_ref, audio_ref, wq, wk, wv, wo, copies_ref, w_ref, out_w_ref, sums_ref, sems
):
    copies = []
    for part, (ref, tower) in enumerate(((wq, 0), (wk, 1), (wv, 1))):
        for j in range(N_TENSOR):
            row = pl.multiple_of(meta_ref[j] * GROUP, GROUP)
            copies.append(
                pltpu.make_async_copy(
                    ref.at[tower, pl.ds(row, GROUP), :],
                    w_ref.at[pl.ds(j * GROUP, GROUP), pl.ds(part * GROUP, GROUP)],
                    sems.at[part * N_TENSOR + j],
                )
            )
    for tower in range(2):
        copies.append(
            pltpu.make_async_copy(
                wo.at[tower], out_w_ref.at[tower], sems.at[3 * N_TENSOR + tower]
            )
        )
    for copy in copies:
        copy.start()
    copies_ref[...] = jnp.broadcast_to(audio_ref[...][None], (N_TENSOR, AUD, GROUP))
    for copy in copies:
        copy.wait()
    sums_ref[...] = dot(jnp.ones((8, D), BF16), w_ref[...])


def prefetch(meta, audio_tokens, w_query, w_key, w_value, w_out):
    return call(
        prefetch_kernel,
        "prefetch",
        0,
        [(SMEM, meta), (VMEM, audio_tokens)]
        + [(HBM, w) for w in (w_query, w_key, w_value, w_out)],
        (),
        [
            pltpu.VMEM((N_TENSOR, AUD, GROUP), BF16),
            pltpu.VMEM((D, 3 * GROUP), BF16),
            pltpu.VMEM((2, GROUP, D), BF16),
            pltpu.VMEM((8, 3 * GROUP), F32),
        ],
        [pltpu.SemaphoreType.DMA((3 * N_TENSOR + 2,))],
    )


def audio_in_kernel(a_ref, wq, wk, wv, qkv_ref, prev_ref, next_ref, wcat, normed, sems):
    def weight(part, j):
        ref, tower = ((wq, 1), (wk, 0), (wv, 0))[part]
        rows = pl.ds(j * GROUP, GROUP)
        cols = pl.ds(part * GROUP, GROUP)
        return pltpu.make_async_copy(
            ref.at[tower, rows, :], wcat.at[rows, cols], sems.at[3 * j + part]
        )

    for j in range(N_TENSOR):
        for part in range(3):
            weight(part, j).start()

    values = a_ref[...].astype(F32)
    mean = jnp.sum(jnp.sum(values, axis=0), axis=-1, keepdims=True) / D
    centred = values - mean[None]
    var = jnp.sum(jnp.sum(centred * centred, axis=0), axis=-1, keepdims=True) / D
    normed[...] = (centred * lax.rsqrt(var + EPS)[None]).astype(BF16)

    total = jnp.zeros((AUD, 3 * GROUP), F32)
    for j in range(N_TENSOR):
        for part in range(3):
            weight(part, j).wait()
        total = total + dot(normed[j], wcat[j * GROUP : (j + 1) * GROUP, :])

    heads = []
    for h in range(2 * HEADS_DEV):
        part = total[:, h * HEAD : (h + 1) * HEAD]
        mean_square = jnp.mean(part * part, axis=-1, keepdims=True)
        heads.append(part * lax.rsqrt(mean_square + EPS))
    q = jnp.concatenate(heads[:HEADS_DEV], axis=1)
    k = jnp.concatenate(heads[HEADS_DEV:], axis=1)
    v = total[:, 2 * GROUP :]
    qkv_ref[...] = cat(q, k, v).astype(BF16)
    prev_ref[...] = cat(q, k[:REACH], v[:REACH]).astype(BF16)
    next_ref[...] = cat(q, k[AUD - REACH :], v[AUD - REACH :]).astype(BF16)


def audio_in(gathered, w_query, w_key, w_value, *extra):
    return call(
        audio_in_kernel,
        "audio_in",
        2,
        [(VMEM, gathered), (HBM, w_query), (HBM, w_key), (HBM, w_value)],
        extra,
        [
            pltpu.VMEM((3 * AUD, GROUP), BF16),
            pltpu.VMEM((PACKED, GROUP), BF16),
            pltpu.VMEM((PACKED, GROUP), BF16),
        ],
        [
            pltpu.VMEM((D, 3 * GROUP), BF16),
            pltpu.VMEM((N_TENSOR, AUD, GROUP), BF16),
            pltpu.SemaphoreType.DMA((3 * N_TENSOR,)),
        ],
    )


def dest_cols(meta_ref, j):
    return pl.ds(pl.multiple_of(meta_ref[AT_DEST + j] * GROUP, GROUP), GROUP)


def dest_cols(meta_ref, j):
    return pl.ds(pl.multiple_of(meta_ref[AT_DEST + j] * GROUP, GROUP), GROUP)


def value_out_kernel(meta_ref, qkv_ref, prev_ref, next_ref, w_ref, keep_ref, give_ref):
    before = prev_ref[...].astype(F32)[AUD + REACH :]
    own = qkv_ref[...].astype(F32)[2 * AUD :]
    behind = next_ref[...].astype(F32)[AUD + REACH :]
    values = cat(before, own, behind).astype(BF16)
    for h in range(HEADS_DEV):
        cols = slice(h * HEAD, (h + 1) * HEAD)
        for j, (dy, dx) in enumerate(OFFSETS):
            product = dot(values[:, cols], w_ref[0, cols, dest_cols(meta_ref, j)])
            out_ref = give_ref if dy else keep_ref
            out_ref[dx, h * SPAN : (h + 1) * SPAN, :] = product.astype(BF16)


def value_out(meta, qkv, from_prev, from_next, w_out, *extra):
    return call(
        value_out_kernel,
        "value_out",
        0,
        [(SMEM, meta), (VMEM, qkv), (VMEM, from_prev), (VMEM, from_next), (VMEM, w_out)],
        extra,
        [pltpu.VMEM((4, KEYS, GROUP), BF16)] * 2,
    )


FAR = TILES
NEAR = FAR + 2
MID = NEAR + 3
LATE = TILES // 2 + 2


def mid_parts_kernel(across_ref, right_ref, keep_ref, got_ref, for_right, for_left, for_across):
    for ref, far, dx, out in (
        (across_ref, keep_ref, 3, for_right),
        (right_ref, got_ref, 1, for_left),
    ):
        out[:TILES] = ref[...]
        out[FAR] = far[2, :, :TILE]
        out[FAR + 1, :, :HEAD] = far[2, :, TILE:]
        out[FAR + 1, :, HEAD:] = jnp.zeros((KEYS, HEAD), BF16)
        out[NEAR] = keep_ref[dx, :, :TILE]
        out[NEAR + 1] = got_ref[dx, :, :TILE]
        out[NEAR + 2, :, :HEAD] = keep_ref[dx, :, TILE:]
        out[NEAR + 2, :, HEAD:] = got_ref[dx, :, TILE:]
    for_across[...] = right_ref[...]


def mid_parts(from_across, from_right, keep, got, *extra):
    return call(
        mid_parts_kernel,
        "mid_parts",
        0,
        [(VMEM, a) for a in (from_across, from_right, keep, got)],
        extra,
        [pltpu.VMEM((MID, KEYS, TILE), BF16)] * 2 + [pltpu.VMEM((TILES, KEYS, TILE), BF16)],
    )


def last_parts_kernel(left_ref, far_ref, right_ref, for_right, for_left):
    half = TILES // 2
    for_right[:half] = left_ref[:half]
    for_right[half:] = left_ref[FAR:NEAR]
    for_left[:half] = right_ref[half:TILES]
    for_left[half:] = far_ref[FAR:NEAR]


def last_parts(from_left, far, from_right, *extra):
    return call(
        last_parts_kernel,
        "last_parts",
        0,
        [(VMEM, a) for a in (from_left, far, from_right)],
        extra,
        [pltpu.VMEM((LATE, KEYS, TILE), BF16)] * 2,
    )


def row_stats(block):
    values = block.astype(F32)
    mean = jnp.mean(values, axis=-1, keepdims=True)
    centred = values - mean
    return mean, jnp.sum(centred * centred, axis=-1, keepdims=True)


def merged_stats(stat, count1, block):
    count = count1 + block.shape[1]
    mean1, square1 = stat[:, :1], stat[:, 1:2]
    offset = block.astype(F32) - mean1
    first = jnp.sum(offset, axis=-1, keepdims=True)
    second = jnp.sum(offset * offset, axis=-1, keepdims=True)
    shift = first / count
    return mean1 + shift, square1 + (second - first * shift)


def packed_stats(mean, square):
    lane = lax.broadcasted_iota(jnp.int32, (TILE, HEAD), 1)
    return jnp.where(lane == 0, mean, square)


def first_kernel(*refs):
    x_refs, (w_ref, acc_q, acc_kv, stat) = refs[:4], refs[4:]

    @pl.loop(0, TILES)
    def _(t):
        rows = rows_of(t)
        block = jnp.concatenate([ref[rows, :] for ref in x_refs], axis=1)
        total = dot(block, w_ref[: 4 * GROUP, :])
        acc_q[rows, :] = total[:, :GROUP]
        acc_kv[rows, :] = total[:, GROUP:]
        stat[rows, :] = packed_stats(*row_stats(block))


def first_half(blocks, weights, *extra):
    return call(
        first_kernel,
        "first_half",
        4,
        [(VMEM, a) for a in (*blocks, weights)],
        extra,
        [
            pltpu.VMEM((VID, GROUP), F32),
            pltpu.VMEM((VID, 2 * GROUP), F32),
            pltpu.VMEM((VID, HEAD), F32),
        ],
    )


def middle_kernel(xa, xb, xc, w_ref, acc_in, stat_in, acc, stat):
    @pl.loop(0, TILES, unroll=2)
    def _(t):
        rows = rows_of(t)
        block = jnp.concatenate([xa[rows, :], xb[rows, :], xc[rows, :]], axis=1)
        acc[rows, :] = acc_in[rows, :] + dot(block, w_ref[4 * GROUP : 7 * GROUP, :GROUP])
        stat[rows, :] = packed_stats(*merged_stats(stat_in[rows, :], 4 * GROUP, block))


def middle(blocks, weights, acc, stat, *extra):
    return call(
        middle_kernel,
        "middle",
        4,
        [(VMEM, a) for a in (*blocks, weights, acc, stat)],
        extra,
        [pltpu.VMEM((VID, GROUP), F32), pltpu.VMEM((VID, HEAD), F32)],
        aliases={4: 0, 5: 1},
    )


def head_norm(part, floor):
    mean_square = jnp.mean(part * part, axis=-1, keepdims=True)
    return (part * lax.rsqrt(mean_square + floor)).astype(BF16)


def by_thirds(body, pieces):
    for k, piece in enumerate(pieces):

        @pl.loop(0, TILES // 3, unroll=True)
        def _(u, k=k, piece=piece):
            body(k * (TILES // 3) + u, piece[rows_of(u), :])


LAST = pl.ds(7 * GROUP, GROUP)


def query_kernel(
    meta_ref, xa, xb, xc, w_ref, acc, stat_in, sums_ref, qkv_ref, prev_ref, next_ref,
    pt_ref, stat,
):
    shard = meta_ref[AT_SHARD]
    before = prev_ref[...].astype(F32)
    own = qkv_ref[...].astype(F32)
    behind = next_ref[...].astype(F32)
    keys = cat(
        before[AUD : AUD + REACH], own[AUD : 2 * AUD], behind[AUD : AUD + REACH]
    ).astype(BF16)

    prev_at, next_at = jnp.maximum(shard - 1, 0), jnp.minimum(shard + 1, SHARDS - 1)
    slot = lax.broadcasted_iota(jnp.int32, (SPAN, 1), 0)
    end_prev = jnp.where(shard > 0, meta_ref[AT_AUDIO + prev_at] - (AUD - REACH), 0)
    reach = jnp.minimum(meta_ref[AT_AUDIO + next_at], meta_ref[AT_VWIN + SHARDS + shard])
    end_next = jnp.where(shard < SHARDS - 1, REACH + AUD + reach, 0)
    used = (slot >= REACH - meta_ref[AT_VWIN + shard]) & (slot < jnp.minimum(end_prev, REACH))
    used |= (slot >= REACH) & (slot < REACH + meta_ref[AT_AUDIO + shard])
    used |= (slot >= REACH + AUD) & (slot < end_next)
    sums = sums_ref[:1, :GROUP]

    def body(t, block):
        rows = rows_of(t)
        mean, square = merged_stats(stat_in[rows, :], 7 * GROUP, block)
        var = square / D
        stat[rows, :] = packed_stats(mean, var)
        total = acc[rows, :] + dot(block, w_ref[LAST, :GROUP]) - mean * sums
        floor = EPS * (var + EPS)
        place = t * TILE + lax.broadcasted_iota(jnp.int32, (1, TILE), 1)
        valid = place < meta_ref[AT_VIDEO + shard]
        for h in range(HEADS_DEV):
            cols = slice(h * HEAD, (h + 1) * HEAD)
            scores = dot_nt(keys[:, cols], head_norm(total[:, cols], floor))
            weights = jnp.where(used, jnp.exp2(scores * SCALE), 0.0)
            share = jnp.where(valid, 1.0 / jnp.sum(weights, axis=0, keepdims=True), 0.0)
            pt_ref[t, h * SPAN : (h + 1) * SPAN, :] = (weights * share).astype(BF16)

    by_thirds(body, (xa, xb, xc))


def queries_out(meta, pieces, weights, acc, stat, sums, qkv, from_prev, from_next, *extra):
    return call(
        query_kernel,
        "queries_out",
        2,
        [(SMEM, meta)]
        + [(VMEM, a) for a in (*pieces, weights, acc, stat, sums, qkv, from_prev, from_next)],
        extra,
        [pltpu.VMEM((TILES, KEYS, TILE), BF16), pltpu.VMEM((VID, HEAD), F32)],
        aliases={6: 1},
    )


def audio_part_kernel(
    meta_ref, ya, yb, yc, xa, xb, xc, w_ref, acc, stat, sums_ref, qkv_ref, prev_ref, next_ref,
    part_p, part_o, part_n,
):
    shard = meta_ref[AT_SHARD]
    queries = cat(prev_ref[:AUD], qkv_ref[:AUD], next_ref[:AUD])
    for ref in (part_p, part_o, part_n):
        ref[...] = jnp.zeros_like(ref)

    prev_at, next_at = jnp.maximum(shard - 1, 0), jnp.minimum(shard + 1, SHARDS - 1)
    count = meta_ref[AT_VIDEO + shard]
    row = lax.broadcasted_iota(jnp.int32, (3 * AUD, 1), 0)
    high_prev = jnp.where(shard > 0, jnp.minimum(count, meta_ref[AT_AWIN + SHARDS + prev_at]), 0)
    high_next = jnp.where(shard < SHARDS - 1, count, 0)
    low = jnp.where(row < 2 * AUD, 0, VID - meta_ref[AT_AWIN + next_at])
    high = jnp.where(row < AUD, high_prev, jnp.where(row < 2 * AUD, count, high_next))
    sums = sums_ref[:1, GROUP:]

    def body(t, block):
        rows = rows_of(t)
        mean, var = stat[rows, :1], stat[rows, 1:2]
        block = jnp.concatenate([ya[rows, :], yb[rows, :], yc[rows, :], block], axis=1)
        total = acc[rows, :] + dot(block, w_ref[4 * GROUP :, GROUP:]) - mean * sums
        floor = EPS * (var + EPS)
        spread = lax.rsqrt(var + EPS)
        place = t * TILE + lax.broadcasted_iota(jnp.int32, (3 * AUD, TILE), 1)
        seen = (place >= low) & (place < high)
        for h in range(HEADS_DEV):
            cols = slice(h * HEAD, (h + 1) * HEAD)
            value = (total[:, GROUP + h * HEAD : GROUP + (h + 1) * HEAD] * spread).astype(BF16)
            scores = dot_nt(queries[:, cols], head_norm(total[:, cols], floor))
            weights = jnp.where(seen, jnp.exp2(scores * SCALE), 0.0)
            lane = lax.broadcasted_iota(jnp.int32, (3 * AUD, HEAD), 1)
            bottom = jnp.where(lane == h, jnp.sum(weights, axis=1, keepdims=True), 0.0)
            top = dot(weights.astype(BF16), value)
            for g, ref in enumerate((part_p, part_o, part_n)):
                ref[:, cols] += top[g * AUD : (g + 1) * AUD]
                ref[:, GROUP:] += bottom[g * AUD : (g + 1) * AUD]

    by_thirds(body, (xa, xb, xc))


def audio_part(meta, pieces, weights, acc, stat, sums, qkv, from_prev, from_next, *extra):
    return call(
        audio_part_kernel,
        "audio_part",
        0,
        [(SMEM, meta)]
        + [(VMEM, a) for a in (*pieces, weights, acc, stat, sums, qkv, from_prev, from_next)],
        extra,
        [pltpu.VMEM((AUD, GROUP + HEAD), F32)] * 3,
    )


def audio_out_kernel(meta_ref, own_ref, prev_ref, next_ref, w_ref, keep_ref, give_ref):
    total = own_ref[...] + prev_ref[...] + next_ref[...]
    row = lax.broadcasted_iota(jnp.int32, (AUD, 1), 0)
    valid = row < meta_ref[AT_AUDIO + meta_ref[AT_SHARD]]
    heads = [
        total[:, h * HEAD : (h + 1) * HEAD] / total[:, GROUP + h : GROUP + h + 1]
        for h in range(HEADS_DEV)
    ]
    attended = jnp.where(valid, jnp.concatenate(heads, axis=1), 0.0).astype(BF16)
    for j, (dy, dx) in enumerate(OFFSETS):
        product = dot(attended, w_ref[1, :, dest_cols(meta_ref, j)]).astype(BF16)
        (give_ref if dy else keep_ref)[dx] = product


def audio_out(meta, own, from_prev, from_next, w_out, *extra):
    return call(
        audio_out_kernel,
        "audio_out",
        0,
        [(SMEM, meta), (VMEM, own), (VMEM, from_prev), (VMEM, from_next), (VMEM, w_out)],
        extra,
        [pltpu.VMEM((4, AUD, GROUP), BF16)] * 2,
    )


def audio_pair_kernel(keep_ref, got_ref, *out_refs):
    for dx in range(4):
        total = keep_ref[dx].astype(F32) + got_ref[dx].astype(F32)
        out_refs[dx][...] = total.astype(BF16)


def audio_pair(keep, got):
    return call(
        audio_pair_kernel,
        "audio_pair",
        0,
        [(VMEM, keep), (VMEM, got)],
        (),
        [pltpu.VMEM((AUD, GROUP), BF16)] * 4,
    )


def audio_sum_kernel(done_ref, *refs):
    refs[4][...] = sum(ref[...].astype(F32) for ref in refs[:4]).astype(BF16)


def audio_sum(received, done):
    (out,) = call(
        audio_sum_kernel,
        "audio_sum",
        0,
        [(HBM, done)] + [(VMEM, a) for a in received],
        (),
        [sds((AUD, GROUP), BF16)],
    )
    return out


def output_kernel(*refs):
    p_refs, (low_ref, high_ref, keep, got, out_ref, projected, out, sems) = refs[:7], refs[7:]
    half = TILES // 2

    left_ref, right_ref = p_refs[4], p_refs[5]

    def near(ref, k):
        tail = slice(k * HEAD, (k + 1) * HEAD)
        return jnp.concatenate([ref[NEAR + k], ref[NEAR + 2, :, tail]], axis=1)

    def far(ref):
        return jnp.concatenate([ref[half], ref[half + 1, :, :HEAD]], axis=1)

    blocks = (
        keep[0], near(left_ref, 0), near(right_ref, 0), got[0],
        near(left_ref, 1), far(low_ref), near(right_ref, 1), far(high_ref),
    )
    for j, block in enumerate(blocks):
        projected[j * KEYS : (j + 1) * KEYS, :] = block

    def copy(t):
        return pltpu.make_async_copy(out.at[rows_of(t), :], out_ref.at[rows_of(t), :], sems.at[t])

    for k, ref in enumerate((low_ref, high_ref)):

        @pl.loop(0, half, unroll=True)
        def _(u, k=k, ref=ref):
            t = k * half + u
            probs = jnp.concatenate([p[t] for p in p_refs] + [ref[u]], axis=0)
            result = dot_tn(probs, projected[...])
            out[rows_of(t), :] = result.astype(BF16)
            copy(t).start()

    for t in range(TILES):
        copy(t).wait()


def output(probs, low, high, keep, got, *extra):
    (out,) = call(
        output_kernel,
        "output",
        1,
        [(VMEM, a) for a in (*probs, low, high, keep, got)],
        (),
        [sds((VID, GROUP), BF16)],
        [
            pltpu.VMEM((N_TENSOR * KEYS, GROUP), BF16),
            pltpu.VMEM((VID, GROUP), BF16),
            pltpu.SemaphoreType.DMA((TILES,)),
        ],
        out_spec=ANY,
    )
    return out


def shards(
    video_tokens,
    audio_tokens,
    w_query,
    w_key,
    w_value,
    w_out,
    video_counts,
    audio_counts,
    video_windows,
    audio_windows,
):
    me = lax.axis_index("tensor")
    shard = lax.axis_index(("tower", "tm"))
    up = [(i, i + 1) for i in range(SHARDS - 1)]
    down = [(i + 1, i) for i in range(SHARDS - 1)]

    def to_next(array):
        return lax.ppermute(array, ("tower", "tm"), up)

    def to_prev(array):
        return lax.ppermute(array, ("tower", "tm"), down)

    places = np.array(
        [
            [moved(i, dy, dx) for dy, dx in OFFSETS] + [moved(i, dy, -dx) for dy, dx in OFFSETS]
            for i in range(N_TENSOR)
        ]
    )
    order = lax.dynamic_index_in_dim(jnp.asarray(places, jnp.int32), me, 0, keepdims=False)
    meta = jnp.concatenate(
        [
            order,
            shard.reshape(1).astype(jnp.int32),
            video_counts,
            audio_counts,
            video_windows.T.reshape(-1),
            audio_windows.T.reshape(-1),
        ]
    )

    xl, xr, xy = right(video_tokens), left(video_tokens), across(video_tokens)
    audio_copies, weights, w_back, sums = prefetch(
        meta, audio_tokens, w_query, w_key, w_value, w_out
    )
    audio_blocks = lax.all_to_all(audio_copies, "tensor", 0, 0)

    xl, xr, xy = gate((xl, xr, xy), audio_blocks)
    yl, xq, yr = right(xy), left(xr), across(xr)
    qkv, for_prev, for_next = audio_in(audio_blocks, w_query, w_key, w_value, xl)
    from_next, from_prev = to_prev(for_prev), to_next(for_next)
    acc_q, acc_kv, stat = first_half(
        (video_tokens, xl, xr, xy), weights, for_prev, for_next
    )

    thirds = parts(((yl, 0, THIRD), (xq, THIRD, THIRD), (yr, 2 * THIRD, THIRD)), stat)
    pieces = right(thirds[0]), across(thirds[1]), left(thirds[2])
    keep_v, give_v = value_out(meta, qkv, from_prev, from_next, w_back, thirds[0])
    got_v = across(give_v)
    blocks = (yl, xq, yr)
    acc_q, stat = middle(blocks, weights, acc_q, stat, keep_v)

    heard = (qkv, from_prev, from_next)
    probs, stat = queries_out(meta, pieces, weights, acc_q, stat, sums, *heard)
    pl_, pr_, py_ = right(probs), left(probs), across(probs)
    part_prev, part_own, part_next = audio_part(
        meta, (*blocks, *pieces), weights, acc_kv, stat, sums, *heard
    )
    for_right, for_left, for_across = mid_parts(py_, pr_, keep_v, got_v, part_prev, pl_)
    pyl, pq, pyr = right(for_right), left(for_left), across(for_across)
    audio_from_next, audio_from_prev = to_prev(part_prev), to_next(part_next)
    keep, give = audio_out(meta, part_own, audio_from_prev, audio_from_next, w_back, for_right)
    for_right, for_left = last_parts(pyl, pq, pyr, give)
    low, high = right(for_right), left(for_left)
    pairs = audio_pair(keep, across(give))
    received = [pairs[0]] + [send(pairs[dx], 0, -dx) for dx in range(1, 4)]
    video_update = output(
        (probs, pl_, pr_, py_, pyl, pq, pyr), low, high, keep_v, got_v, pairs[0]
    )
    audio_update = audio_sum(received, video_update)
    return (video_update, audio_update)


def solution(mesh):
    in_specs = (
        P(("tower", "tm"), "tensor"),
        P(("tower", "tm"), "tensor"),
        P(None, None, "tensor"),
        P(None, None, "tensor"),
        P(None, None, "tensor"),
        P(None, "tensor", None),
        P(),
        P(),
        P(),
        P(),
    )
    out_specs = (P(("tower", "tm"), "tensor"), P(("tower", "tm"), "tensor"))
    return jax.shard_map(shards, mesh=mesh, in_specs=in_specs, out_specs=out_specs, check_vma=False)
```
